32 devices in a mesh: ctx: 8 (over z, core), exp: 4 (over y, x).
Axes of the slice: x: 2, y: 2, z: 4, core: 2. Of those that a mesh axis runs over, the one named last changes fastest.
Arguments:
- queries: bfloat16 [2048, 8192], P('ctx', 'exp'), may hold values from -8 to 8
- keys: bfloat16 [2048, 512], P('ctx'), may hold values from -4 to 4
- values: bfloat16 [2048, 512], P('ctx'), may hold values from -6 to 6
- w_out: bfloat16 [8192, 4096], P('exp'), may hold values from -0.5 to 0.5
- residual: bfloat16 [2048, 4096], P(('ctx', 'exp')), may hold values from -1.5 to 1.5
- norm_gain: bfloat16 [4096], replicated, may hold values from 0.099609375 to 1.8984375
- expert_ids: int32 [2048, 2], P(('ctx', 'exp')), may hold values from 0 to 3, all different within a row; in each aligned block of 64 rows (0 to 63, 64 to 127, ...) at most 64 rows name the same one
- gate_weights: float32 [2048, 2], P(('ctx', 'exp')), may hold values from 0.2 to 1
- w_gate: bfloat16 [4, 4096, 768], P('exp', 'ctx'), may hold values from -0.09375 to 0.09375
- w_up: bfloat16 [4, 4096, 768], P('exp', 'ctx'), may hold values from -0.09375 to 0.09375
- w_down: bfloat16 [4, 768, 4096], P('exp', None, 'ctx'), may hold values from -0.21875 to 0.21875
Outputs:
- layer_out: bfloat16 [2048, 4096], P(('ctx', 'exp'))
The draws below stay inside these ranges and needn't reach their ends.
Inputs may be any that keep to these rules, and one draw needn't show every extreme that they name: `expert_ids`: each row names 2 different experts; within each aligned block of 64 rows (the rows of one device) no expert is named by more than 64 rows.
All inputs are finite; a program needn't handle non-finite values.
Results may differ from the reference program's by a relative error of at most 0.025.
Values may be sent and summed in bfloat16 or wider, within the bound.
No kernel may reach another device: no remote copies, remote signals or barrier semaphores. Data moves between devices by JAX's collectives and lax.ppermute only.
A program may use at most 128 MiB of HBM per device.

```python
import math
import jax
import jax.numpy as jnp
import numpy as np
from jax import lax

D = 4096
HQ = 64
KVH = 4
HD = 128
FF = 768
TOPK = 2
SEQ = 2048
EXPERTS = 4
ROWS = 64
CAP = 64


def draw_keys(key, part):
    shape = (SEQ, KVH * HD)
    base = jnp.clip(jax.random.normal(jax.random.fold_in(key, 1), shape, jnp.float32), -4.0, 4.0)
    return base.astype(jnp.bfloat16)


def draw_queries(key, part):
    shape = (SEQ, HQ * HD)
    base = jnp.clip(jax.random.normal(jax.random.fold_in(key, 2), shape, jnp.float32), -6.0, 6.0)
    return base.astype(jnp.bfloat16)


def levels(stream_key, shape, cuts, smallest, high):
    level, own = 1.0, jax.random.fold_in(stream_key, 6)
    for position, shards_of in cuts:
        steps = jnp.exp(jax.random.uniform(jax.random.fold_in(own, position), (shards_of,), jnp.float32, smallest / len(cuts), high / len(cuts)))
        level = level * jnp.repeat(steps, shape[position] // shards_of).reshape([-1 if axis == position else 1 for axis in range(len(shape))])
    return level


def deal_out(rng, own, number, rows, count, top, reach, slope):
    sequence = jax.random.permutation(rng, count)
    heavy_load, common = load_shares(count, rows * top, reach, slope, True), load_shares(count, rows * top, reach, slope, False)
    places = jnp.arange(count)

    def named(sizes, turn):
        used = int((sizes > 0).sum())
        fixed = max(1, used // 4)
        shifted = fixed + (places - fixed + turn * (used - fixed)) % max(1, count - fixed)
        return jnp.zeros((count,), jnp.int32).at[sequence[jnp.where(places < fixed, places, shifted)]].set(jnp.asarray(sizes, jnp.int32))

    sizes = jnp.where(number % 4 == 0, named(heavy_load, number // 4), named(common, number - number // 4 - 1))
    mixed = jax.random.permutation(jax.random.fold_in(own, 3), count)
    donor, sink = mixed[0:count // 2 * 2:2], mixed[1:count // 2 * 2:2]
    slack = jnp.minimum(sizes[donor] - 1, reach - sizes[sink]) // 2
    slack = jnp.where((donor == sequence[0]) | (sink == sequence[0]) | (sizes[sink] == 0), 0, jnp.maximum(slack, 0))
    shifted = jax.random.randint(jax.random.fold_in(own, 4), (count // 2,), 0, 1 << 20) % (slack + 1)
    sizes = sizes.at[donor].add(-shifted).at[sink].add(shifted)
    members = jnp.searchsorted(jnp.cumsum(sizes), jnp.arange(rows * top), side="right").astype(jnp.int32)
    grid = members.reshape(top, rows).T
    grid = grid[jax.random.permutation(jax.random.fold_in(own, 1), rows)]
    turn = jax.random.randint(jax.random.fold_in(own, 2), (rows, 1), 0, top)
    return jnp.take_along_axis(grid, (jnp.arange(top)[None, :] + turn) % top, axis=1)


def load_shares(count, total, most, lean, full):
    portions = [(1 << 20) // math.isqrt(grade ** lean) + 1 for grade in range(1, count + 1)]
    largest = most if full else min(most, max(-(-total // count), total * portions[0] // sum(portions)))
    least = 1 if total - largest >= count - 1 else 0
    given, rest = [largest] + [least] * (count - 1), total - largest - least * (count - 1)
    while rest > 0:
        movable = [i for i in range(1, count) if given[i] < largest] or [i for i in range(1, count) if given[i] < most]
        whole, left = sum([portions[i] for i in movable]), rest
        for i in movable:
            more = min(most - given[i], max(1, left * portions[i] // whole), rest)
            given[i] = given[i] + more
            rest = rest - more
    return np.array(given)


def normal_values(stream_key, shape, spread, reach, split=(), kind=jnp.bfloat16):
    loudness = levels(stream_key, shape, split, -0.22, 0.18) if split else 1.0
    result = jax.random.normal(stream_key, shape, jnp.float32) * spread * loudness
    return jnp.minimum(jnp.maximum(result, -reach), reach).astype(kind)


def setup_inputs(seed: int = 0) -> dict:
    seeds = jax.random.split(jax.random.key(seed), 12)
    queries = draw_queries(jax.random.fold_in(seeds[11], 71), 0)
    keys = draw_keys(jax.random.fold_in(seeds[11], 71), 0)
    values = normal_values(seeds[2], (SEQ, KVH * HD), 1.0, 6.0, ((0, 8),))
    w_out = normal_values(seeds[3], (HQ * HD, D), HD ** -0.5, 0.5, ((0, 4),))
    residual = normal_values(seeds[4], (SEQ, D), 0.25, 1.5, ((0, 32),))
    norm_gain = jnp.clip(1.0 + 0.18 * jax.random.normal(seeds[5], (D,), jnp.float32), 0.099609375, 1.8984375).astype(jnp.bfloat16)
    expert_ids_keys = jax.random.split(jax.random.fold_in(seeds[6], 1), SEQ // ROWS)
    expert_ids_turns = jax.random.permutation(jax.random.fold_in(seeds[6], 3), SEQ // ROWS)
    expert_ids = jax.vmap(lambda own, number: deal_out(jax.random.fold_in(seeds[6], 2), own, number, ROWS, EXPERTS, TOPK, CAP, 2))(expert_ids_keys, expert_ids_turns).reshape((SEQ, TOPK))
    gate_weights = jnp.clip(0.2 + 0.8 * jax.random.uniform(seeds[7], (SEQ, TOPK), jnp.float32) ** levels(seeds[7], (SEQ, TOPK), ((0, 32),), -0.2, 0.2), 0.2, 1.0)
    w_gate = normal_values(seeds[8], (EXPERTS, D, FF), D ** -0.5, 0.09375, ((0, 4), (1, 8)))
    w_up = normal_values(seeds[9], (EXPERTS, D, FF), D ** -0.5, 0.09375, ((0, 4), (1, 8)))
    w_down = normal_values(seeds[10], (EXPERTS, FF, D), FF ** -0.5, 0.21875, ((0, 4), (2, 8)))
    return {"queries": queries, "keys": keys, "values": values, "w_out": w_out, "residual": residual, "norm_gain": norm_gain, "expert_ids": expert_ids, "gate_weights": gate_weights, "w_gate": w_gate, "w_up": w_up, "w_down": w_down}


def attention_all(queries, keys, values):
    group = HQ // KVH
    qblk = 512 if SEQ % 512 == 0 else SEQ
    blocks_per_head = SEQ // qblk
    scale = 1.0 / math.sqrt(HD)
    key_pos = jnp.arange(SEQ, dtype=jnp.int32)

    def one_block(index):
        head = index // blocks_per_head
        block = index % blocks_per_head
        kv_head = head // group
        rows = lax.dynamic_slice(queries, (block * qblk, head * HD), (qblk, HD))
        key_cols = lax.dynamic_slice_in_dim(keys, kv_head * HD, HD, 1)
        value_cols = lax.dynamic_slice_in_dim(values, kv_head * HD, HD, 1)
        scores = jnp.dot(rows, key_cols.T, preferred_element_type=jnp.float32) * scale
        query_pos = block * qblk + jnp.arange(qblk, dtype=jnp.int32)
        allowed = key_pos[None, :] <= query_pos[:, None]
        scores = jnp.where(allowed, scores, -jnp.inf)
        top = lax.optimization_barrier(jnp.max(scores, axis=1, keepdims=True))
        probs = jnp.exp(scores - top)
        total = lax.optimization_barrier(jnp.sum(probs, axis=1))
        mixed = jnp.dot(probs.astype(jnp.bfloat16), value_cols, preferred_element_type=jnp.float32)
        return (mixed / total[:, None]).astype(jnp.bfloat16)
    blocks = lax.map(one_block, jnp.arange(HQ * blocks_per_head, dtype=jnp.int32))
    return blocks.reshape(HQ, SEQ, HD).transpose(1, 0, 2).reshape(SEQ, HQ * HD)

def reference(queries, keys, values, w_out, residual, norm_gain, expert_ids, gate_weights, w_gate, w_up, w_down):
    attn = attention_all(queries, keys, values)
    projected = jnp.dot(attn, w_out, preferred_element_type=jnp.float32)
    hidden_state = (residual.astype(jnp.float32) + projected).astype(jnp.bfloat16)
    state_f = hidden_state.astype(jnp.float32)
    inv_rms = 1.0 / jnp.sqrt(lax.optimization_barrier(jnp.mean(state_f * state_f, axis=1, keepdims=True)) + 1e-06)
    normed = (state_f * inv_rms * norm_gain.astype(jnp.float32)[None, :]).astype(jnp.bfloat16)
    flat_ids = expert_ids.reshape(-1)
    flat_gates = gate_weights.reshape(-1)
    most_rows = SEQ // ROWS * CAP

    def expert_step(acc, expert):
        hit = flat_ids == expert
        count = jnp.sum(hit.astype(jnp.int32))
        pairs = jnp.nonzero(hit, size=most_rows, fill_value=0)[0].astype(jnp.int32)
        valid = jnp.arange(most_rows, dtype=jnp.int32) < count
        token = pairs // TOPK
        rows = normed[token]
        gate_pre = jnp.dot(rows, w_gate[expert], preferred_element_type=jnp.float32)
        up_pre = jnp.dot(rows, w_up[expert], preferred_element_type=jnp.float32)
        expert_hidden = (jax.nn.silu(gate_pre) * up_pre).astype(jnp.bfloat16)
        expert_result = jnp.dot(expert_hidden, w_down[expert], preferred_element_type=jnp.float32).astype(jnp.bfloat16)
        weight = jnp.where(valid, flat_gates[pairs], jnp.zeros_like(flat_gates[pairs]))
        acc = acc.at[token].add(weight[:, None] * expert_result.astype(jnp.float32))
        return (acc, None)
    acc, _ = lax.scan(expert_step, jnp.zeros((SEQ, D), jnp.float32), jnp.arange(EXPERTS, dtype=jnp.int32))
    return (state_f + acc).astype(jnp.bfloat16)
```

```python
import math

import jax
import jax.numpy as jnp
from jax import lax
from jax.experimental import pallas as pl
from jax.experimental.pallas import tpu as pltpu
from jax.sharding import PartitionSpec as P

D = 4096
HQ = 64
KVH = 4
HD = 128


def general_body(
    queries,
    keys,
    values,
    w_out,
    residual,
    norm_gain,
    expert_ids,
    gate_weights,
    w_gate,
    w_up,
    w_down,
):
    tok_rows = queries.shape[0]
    half_rows = tok_rows // 2
    exp_count = lax.axis_size("exp")
    heads_here = HQ // exp_count
    group = HQ // KVH
    kv_here = max(1, heads_here // group)
    heads_per_kv = heads_here // kv_here
    exp_index = lax.axis_index("exp")
    ctx_index = lax.axis_index("ctx")
    kv_first = exp_index * heads_here // group
    key_cols = lax.dynamic_slice_in_dim(keys, kv_first * HD, kv_here * HD, 1)
    value_cols = lax.dynamic_slice_in_dim(values, kv_first * HD, kv_here * HD, 1)
    scale = 1.0 / math.sqrt(HD)
    first_rows = queries[:half_rows]
    second_rows = queries[half_rows:]
    first_start = ctx_index * tok_rows
    second_start = ctx_index * tok_rows + half_rows
    query_sets = (
        first_rows.reshape(half_rows, kv_here, heads_per_kv, HD),
        second_rows.reshape(half_rows, kv_here, heads_per_kv, HD),
    )
    query_positions = (
        first_start + jnp.arange(half_rows, dtype=jnp.int32),
        second_start + jnp.arange(half_rows, dtype=jnp.int32),
    )
    last_positions = (first_start + half_rows - 1, second_start + half_rows - 1)

    def block_update(carry, query_four, query_pos, key_block, value_block, key_start):
        run_max, run_sum, run_acc = carry
        width = key_block.shape[0]
        key_three = key_block.reshape(width, kv_here, HD)
        value_three = value_block.reshape(width, kv_here, HD)
        scores = (
            jnp.einsum("tghd,kgd->ghtk", query_four, key_three, preferred_element_type=jnp.float32)
            * scale
        )
        key_pos = key_start + jnp.arange(width, dtype=jnp.int32)
        allowed = key_pos[None, :] <= query_pos[:, None]
        scores = jnp.where(allowed, scores, -1e30)
        new_max = jnp.maximum(run_max, jnp.max(scores, axis=-1))
        probs = jnp.where(allowed, jnp.exp(scores - new_max[..., None]), 0.0)
        factor = jnp.exp(run_max - new_max)
        run_sum = run_sum * factor + jnp.sum(probs, axis=-1)
        weighted = jnp.einsum(
            "ghtk,kgd->ghtd",
            probs.astype(jnp.bfloat16),
            value_three,
            preferred_element_type=jnp.float32,
        )
        run_acc = run_acc * factor[..., None] + weighted
        return (new_max, run_sum, run_acc)

    start_max = jnp.full((kv_here, heads_per_kv, half_rows), -1e30, jnp.float32)
    start_sum = jnp.zeros((kv_here, heads_per_kv, half_rows), jnp.float32)
    start_acc = jnp.zeros((kv_here, heads_per_kv, half_rows, HD), jnp.float32)
    start_state = (start_max, start_sum, start_acc)
    key_piece = lax.all_gather(key_cols, "ctx", axis=0, tiled=True)
    value_piece = lax.all_gather(value_cols, "ctx", axis=0, tiled=True)
    count = key_piece.shape[0]
    width = 512

    def one_block(index, inner):
        key_start = index * width
        key_block = lax.dynamic_slice_in_dim(key_piece, key_start, width, 0)
        value_block = lax.dynamic_slice_in_dim(value_piece, key_start, width, 0)
        updated = []
        for which in range(2):
            query_four = query_sets[which]
            query_pos = query_positions[which]
            updated.append(
                lax.cond(
                    key_start > last_positions[which],
                    lambda state: state,
                    lambda state: block_update(
                        state, query_four, query_pos, key_block, value_block, key_start
                    ),
                    inner[which],
                )
            )
        return (updated[0], updated[1])

    states = lax.fori_loop(0, count // width, one_block, (start_state, start_state))
    halves = []
    for which in range(2):
        run_max, run_sum, run_acc = states[which]
        halves.append(
            jnp.transpose(run_acc / run_sum[..., None], (2, 0, 1, 3))
            .reshape(half_rows, heads_here * HD)
            .astype(jnp.bfloat16)
        )
    attn_second = halves[1]
    attn = jnp.concatenate([halves[0], attn_second], axis=0)
    projected = lax.psum_scatter(
        jnp.dot(attn, w_out, preferred_element_type=jnp.float32).astype(jnp.bfloat16),
        "exp",
        scatter_dimension=0,
        tiled=True,
    ).astype(jnp.float32)
    hidden_state = (residual.astype(jnp.float32) + projected).astype(jnp.bfloat16)
    state_f = hidden_state.astype(jnp.float32)
    inv_rms = 1.0 / jnp.sqrt(jnp.mean(state_f * state_f, axis=1, keepdims=True) + 1e-06)
    normed = (state_f * inv_rms * norm_gain.astype(jnp.float32)[None, :]).astype(jnp.bfloat16)
    rows_here = expert_ids.shape[0]
    top_count = expert_ids.shape[1]
    experts_all = w_gate.shape[0] * exp_count
    capacity = min(rows_here, 2 * rows_here * top_count // experts_all)
    flat_ids = expert_ids.reshape(-1)
    onehot = (flat_ids[:, None] == jnp.arange(experts_all, dtype=jnp.int32)[None, :]).astype(
        jnp.int32
    )
    earlier = jnp.cumsum(onehot, axis=0) - onehot
    slot_index = jnp.sum(earlier * onehot, axis=1)
    target = flat_ids * capacity + slot_index
    picks = target[:, None] == jnp.arange(experts_all * capacity, dtype=jnp.int32)[None, :]
    dispatch_table = jnp.any(
        picks.reshape(rows_here, top_count, experts_all * capacity), axis=1
    ).astype(jnp.bfloat16)
    outgoing = jnp.einsum(
        "rs,rd->sd", dispatch_table, normed, preferred_element_type=jnp.float32
    ).astype(jnp.bfloat16)
    arrived = lax.all_to_all(
        outgoing.reshape(experts_all, capacity, D), "exp", split_axis=0, concat_axis=0, tiled=True
    )
    slot_rows = arrived.reshape(experts_all * capacity, D)
    gate_local = w_gate[0]
    up_local = w_up[0]
    gate_pre = jnp.dot(
        slot_rows,
        lax.all_gather(gate_local, "ctx", axis=0, tiled=True),
        preferred_element_type=jnp.float32,
    )
    up_pre = jnp.dot(
        slot_rows,
        lax.all_gather(up_local, "ctx", axis=0, tiled=True),
        preferred_element_type=jnp.float32,
    )
    expert_hidden = (jax.nn.silu(gate_pre) * up_pre).astype(jnp.bfloat16)
    down_local = w_down[0]
    expert_result = jnp.dot(
        expert_hidden,
        lax.all_gather(down_local, "ctx", axis=1, tiled=True),
        preferred_element_type=jnp.float32,
    ).astype(jnp.bfloat16)
    returned = lax.all_to_all(
        expert_result.reshape(experts_all, capacity, D),
        "exp",
        split_axis=0,
        concat_axis=0,
        tiled=True,
    )
    returned_flat = returned.reshape(experts_all * capacity, D)
    picked = jnp.dot(picks.astype(jnp.bfloat16), returned_flat, preferred_element_type=jnp.float32)
    weighted = gate_weights[:, :, None] * picked.reshape(rows_here, top_count, D)
    return (state_f + jnp.sum(weighted, axis=1)).astype(jnp.bfloat16)


BF16 = jnp.bfloat16
F32 = jnp.float32
VMEM = pltpu.VMEM
QB = 256
CHUNK = 4
CHEAP = pl.CostEstimate(flops=1000, bytes_accessed=1000, transcendentals=0)


def swap(array, axis, mask):
    size = lax.axis_size(axis)
    return lax.ppermute(array, axis, [(i, i ^ mask) for i in range(size)])


def params(mib):
    return pltpu.CompilerParams(vmem_limit_bytes=mib * 1024 * 1024)


def vmem_specs(count):
    return [pl.BlockSpec(memory_space=VMEM) for _ in range(count)]


def attention_kernel(index, q, kv, w_hbm, p0, p1, p2, p3, w_all, scores, ones_values, attn, sem):
    ctx = index[0]
    exp = index[1]
    fetch = pltpu.make_async_copy(w_hbm, w_all, sem)
    fetch.start()
    factor = math.log2(math.e) / math.sqrt(HD)
    rows = CHUNK * QB
    heads = q.shape[1] // HD
    ones_values[:, :HD] = kv[:, HD:]
    ones_values[:, HD:] = jnp.ones((kv.shape[0], HD), BF16)
    row = lax.broadcasted_iota(jnp.int32, (QB, QB), 0)
    col = lax.broadcasted_iota(jnp.int32, (QB, QB), 1)
    hidden_keys = jnp.concatenate([jnp.where(col <= row, 0.0, -1e30)] * CHUNK, axis=0)
    for chunk in range(heads // CHUNK):
        first = chunk * CHUNK
        queries = jnp.concatenate(
            [q[:, (first + h) * HD : (first + h + 1) * HD] for h in range(CHUNK)], axis=0
        )

        def score_block(j):
            block = kv[pl.ds(pl.multiple_of(j * QB, QB), QB), :HD]
            return lax.dot_general(
                queries, block, (((1,), (1,)), ((), ())), preferred_element_type=F32
            )

        def first_pass(j, top):
            block = score_block(j)
            scores[j] = block
            return jnp.maximum(top, jnp.maximum(block[:, :HD], block[:, HD:]))

        last = score_block(ctx) + hidden_keys
        scores[ctx] = last
        top = jnp.maximum(last[:, :HD], last[:, HD:])
        top = lax.fori_loop(0, ctx, first_pass, top)
        top = jnp.max(top, axis=1, keepdims=True) * factor

        def second_pass(j, total):
            probs = jnp.exp2(scores[j] * factor - top).astype(BF16)
            block = ones_values[pl.ds(pl.multiple_of(j * QB, QB), QB), :]
            return total + jnp.dot(probs, block, preferred_element_type=F32)

        total = lax.fori_loop(0, ctx + 1, second_pass, jnp.zeros((rows, 2 * HD), F32))
        done = (total[:, :HD] / total[:, HD:]).astype(BF16)
        part = QB // 4
        for h in range(CHUNK):
            for i in range(4):
                start = pl.multiple_of((exp ^ i) * part, part)
                attn[pl.ds(start, part), (first + h) * HD : (first + h + 1) * HD] = done[
                    h * QB + i * part : h * QB + (i + 1) * part
                ]
    fetch.wait()
    part = QB // 4
    width = 512
    for n in range(w_all.shape[1] // width):
        cols = slice(n * width, (n + 1) * width)
        block = jnp.dot(attn[...], w_all[:, cols], preferred_element_type=F32).astype(BF16)
        for b, out in enumerate((p0, p1, p2, p3)):
            out[:, cols] = block[b * part : (b + 1) * part]


def attention(index, queries, kv, w_out):
    rows = QB // 4
    blocks = kv.shape[0] // QB
    return pl.pallas_call(
        attention_kernel,
        out_shape=[jax.ShapeDtypeStruct((rows, D), BF16)] * 4,
        in_specs=[pl.BlockSpec(memory_space=pltpu.SMEM)]
        + vmem_specs(2)
        + [pl.BlockSpec(memory_space=pl.ANY)],
        out_specs=vmem_specs(4),
        scratch_shapes=[
            VMEM(w_out.shape, BF16),
            VMEM((blocks, CHUNK * QB, QB), F32),
            VMEM((kv.shape[0], 2 * HD), BF16),
            VMEM(queries.shape, BF16),
            pltpu.SemaphoreType.DMA,
        ],
        compiler_params=params(56),
        cost_estimate=CHEAP,
        name="attention",
    )(index, queries, kv, w_out)


def norm_kernel(index, p0, r1, r2, r3, residual, gain, state, mine, theirs, work):
    ctx = index[0]
    total = p0[...].astype(F32) + r1[...].astype(F32) + r2[...].astype(F32) + r3[...].astype(F32)
    hidden = (residual[...].astype(F32) + total).astype(BF16)
    state[...] = hidden
    wide = hidden.astype(F32)
    inv = 1.0 / jnp.sqrt(jnp.mean(wide * wide, axis=1, keepdims=True) + 1e-06)
    normed = (wide * inv * gain[...].astype(F32)).astype(BF16)
    part = D // 8
    for j in range(8):
        work[j] = normed[:, j * part : (j + 1) * part]
    for j, (a, b) in enumerate(((0, 2), (1, 3), (6, 4), (7, 5))):
        mine[:, j * part : (j + 1) * part] = work[ctx ^ a]
        theirs[:, j * part : (j + 1) * part] = work[ctx ^ b]


def norm(index, p0, r1, r2, r3, residual, gain):
    rows = residual.shape[0]
    half = jax.ShapeDtypeStruct((rows, D // 2), BF16)
    return pl.pallas_call(
        norm_kernel,
        out_shape=[jax.ShapeDtypeStruct((rows, D), BF16), half, half],
        in_specs=[pl.BlockSpec(memory_space=pltpu.SMEM)] + vmem_specs(6),
        out_specs=vmem_specs(3),
        scratch_shapes=[VMEM((8, rows, D // 8), BF16)],
        compiler_params=params(16),
        cost_estimate=CHEAP,
        name="norm",
    )(index, p0, r1, r2, r3, residual, gain)


def enter_kernel(x0, x1, x2, x3, *refs):
    gates, ups, out = refs[:4], refs[4:8], refs[8]
    x = jnp.concatenate([x0[...], x1[...], x2[...], x3[...]], axis=0)
    part, width = gates[0].shape
    for which, weights in enumerate((gates, ups)):
        total = jnp.zeros((x.shape[0], width), F32)
        for j in range(4):
            total = total + jnp.dot(
                x[:, j * part : (j + 1) * part], weights[j][...], preferred_element_type=F32
            )
        out[:, which * width : (which + 1) * width] = total.astype(out.dtype)


def enter(rows, gates, ups, kind):
    count = 4 * rows[0].shape[0]
    return pl.pallas_call(
        enter_kernel,
        out_shape=jax.ShapeDtypeStruct((count, 2 * gates[0].shape[1]), kind),
        in_specs=vmem_specs(12),
        out_specs=pl.BlockSpec(memory_space=VMEM),
        compiler_params=params(32),
        cost_estimate=CHEAP,
        name="enter",
    )(*rows, *gates, *ups)


def silu_kernel(own, other, c0, c1, c2, c3, out):
    width = out.shape[1]
    part = c0.shape[0]
    total = own[...] + other[...].astype(F32)
    gate, up = total[:, :width], total[:, width:]
    hidden = gate / (1.0 + jnp.exp(-gate)) * up
    for b, share in enumerate((c0, c1, c2, c3)):
        rows = slice(b * part, (b + 1) * part)
        out[rows] = (hidden[rows] * share[...]).astype(BF16)


def silu(own, other, shares):
    return pl.pallas_call(
        silu_kernel,
        out_shape=jax.ShapeDtypeStruct((own.shape[0], own.shape[1] // 2), BF16),
        in_specs=vmem_specs(6),
        out_specs=pl.BlockSpec(memory_space=VMEM),
        compiler_params=params(16),
        cost_estimate=CHEAP,
        name="silu",
    )(own, other, *shares)


def leave_kernel(hidden, d0, d1, d2, d3, y0, y1, y2, y3):
    part = y0.shape[0]
    width = d0.shape[1]
    for j, weights in enumerate((d0, d1, d2, d3)):
        block = jnp.dot(hidden[...], weights[...], preferred_element_type=F32).astype(BF16)
        for b, out in enumerate((y0, y1, y2, y3)):
            out[:, j * width : (j + 1) * width] = block[b * part : (b + 1) * part]


def leave(hidden, downs):
    part = jax.ShapeDtypeStruct((hidden.shape[0] // 4, 4 * downs[0].shape[1]), BF16)
    return pl.pallas_call(
        leave_kernel,
        out_shape=[part] * 4,
        in_specs=vmem_specs(5),
        out_specs=vmem_specs(4),
        compiler_params=params(16),
        cost_estimate=CHEAP,
        name="leave",
    )(hidden, *downs)


def total_kernel(y0, r1, r2, r3, out):
    out[...] = (
        y0[...].astype(F32) + r1[...].astype(F32) + r2[...].astype(F32) + r3[...].astype(F32)
    ).astype(BF16)


def total_of(y0, r1, r2, r3):
    return pl.pallas_call(
        total_kernel,
        out_shape=jax.ShapeDtypeStruct(y0.shape, BF16),
        in_specs=vmem_specs(4),
        out_specs=pl.BlockSpec(memory_space=VMEM),
        cost_estimate=CHEAP,
        name="total",
    )(y0, r1, r2, r3)


def final_kernel(index, state, y0, r1, r2, r3, other, out):
    ctx = index[0]
    part = D // 8
    own = y0[...].astype(F32) + r1[...].astype(F32) + r2[...].astype(F32) + r3[...].astype(F32)
    for j, (a, b) in enumerate(((0, 2), (1, 3), (6, 4), (7, 5))):
        cols = slice(j * part, (j + 1) * part)
        here = pl.ds(pl.multiple_of((ctx ^ a) * part, part), part)
        out[:, here] = (state[:, here].astype(F32) + own[:, cols]).astype(BF16)
        there = pl.ds(pl.multiple_of((ctx ^ b) * part, part), part)
        out[:, there] = (state[:, there].astype(F32) + other[:, cols].astype(F32)).astype(BF16)


def final(index, state, y0, r1, r2, r3, other):
    return pl.pallas_call(
        final_kernel,
        out_shape=jax.ShapeDtypeStruct(state.shape, BF16),
        in_specs=[pl.BlockSpec(memory_space=pltpu.SMEM)] + vmem_specs(6),
        out_specs=pl.BlockSpec(memory_space=VMEM),
        compiler_params=params(16),
        cost_estimate=CHEAP,
        name="final",
    )(index, state, y0, r1, r2, r3, other)


def body(
    queries,
    keys,
    values,
    w_out,
    residual,
    norm_gain,
    expert_ids,
    gate_weights,
    w_gate,
    w_up,
    w_down,
):
    exp = lax.axis_index("exp")
    ctx = lax.axis_index("ctx")
    index = jnp.stack([ctx, exp]).astype(jnp.int32)
    kv_first = exp * (HQ // 4) // (HQ // KVH) * HD
    kv_here = jnp.concatenate(
        [
            lax.dynamic_slice_in_dim(keys, kv_first, HD, 1),
            lax.dynamic_slice_in_dim(values, kv_first, HD, 1),
        ],
        axis=1,
    )
    kv = lax.all_gather(kv_here, "ctx", axis=0, tiled=True)

    shares = []
    for b in range(4):
        share = jnp.sum(jnp.where(expert_ids == (exp ^ b), gate_weights, 0.0), axis=1, keepdims=True)
        shares.append(swap(share, "exp", b) if b else share)

    def slices(array):
        far = swap(array, "ctx", 6)
        return (array, swap(array, "ctx", 1), far, swap(far, "ctx", 1))

    gates = slices(w_gate[0])
    ups = slices(w_up[0])

    p = attention(index, queries, kv, w_out)
    r = [swap(p[b], "exp", b) for b in (1, 2, 3)]
    state, mine, theirs = norm(index, p[0], *r, residual, norm_gain.reshape(1, D))
    downs = slices(w_down[0])
    others = swap(theirs, "ctx", 2)
    other_rows = [others] + [swap(others, "exp", b) for b in (1, 2, 3)]
    own_rows = [mine] + [swap(mine, "exp", b) for b in (1, 2, 3)]
    other_pre = enter(other_rows, gates, ups, BF16)
    from_other = swap(other_pre, "ctx", 2)
    own_pre = enter(own_rows, gates, ups, F32)
    own_hidden = silu(own_pre, from_other, shares)
    other_hidden = swap(own_hidden, "ctx", 2)
    y = leave(own_hidden, downs)
    own_parts = [y[0]] + [swap(y[b], "exp", b) for b in (1, 2, 3)]
    z = leave(other_hidden, downs)
    other_parts = [z[0]] + [swap(z[b], "exp", b) for b in (1, 2, 3)]
    back = swap(total_of(*other_parts), "ctx", 2)
    return final(index, state, *own_parts, back)


def solution(mesh):
    placed = (
        P("ctx", "exp"),
        P("ctx", None),
        P("ctx", None),
        P("exp", None),
        P(("ctx", "exp"), None),
        P(),
        P(("ctx", "exp"), None),
        P(("ctx", "exp"), None),
        P("exp", "ctx", None),
        P("exp", "ctx", None),
        P("exp", None, "ctx"),
    )
    shape = dict(mesh.shape)
    small = shape["ctx"] == 8 and shape["exp"] == 4
    return jax.shard_map(
        body if small else general_body, mesh=mesh, in_specs=placed, out_specs=P(("ctx", "exp"), None), check_vma=False
    )
```

```python
import functools
import math

import jax
import jax.numpy as jnp
from jax import lax
from jax.experimental import pallas as pl
from jax.experimental.pallas import tpu as pltpu
from jax.sharding import PartitionSpec as P

D = 4096
HQ = 64
KVH = 4
HD = 128


def general_body(
    queries,
    keys,
    values,
    w_out,
    residual,
    norm_gain,
    expert_ids,
    gate_weights,
    w_gate,
    w_up,
    w_down,
):
    tok_rows = queries.shape[0]
    half_rows = tok_rows // 2
    exp_count = lax.axis_size("exp")
    heads_here = HQ // exp_count
    group = HQ // KVH
    kv_here = max(1, heads_here // group)
    heads_per_kv = heads_here // kv_here
    exp_index = lax.axis_index("exp")
    ctx_index = lax.axis_index("ctx")
    kv_first = exp_index * heads_here // group
    key_cols = lax.dynamic_slice_in_dim(keys, kv_first * HD, kv_here * HD, 1)
    value_cols = lax.dynamic_slice_in_dim(values, kv_first * HD, kv_here * HD, 1)
    scale = 1.0 / math.sqrt(HD)
    first_rows = queries[:half_rows]
    second_rows = queries[half_rows:]
    first_start = ctx_index * tok_rows
    second_start = ctx_index * tok_rows + half_rows
    query_sets = (
        first_rows.reshape(half_rows, kv_here, heads_per_kv, HD),
        second_rows.reshape(half_rows, kv_here, heads_per_kv, HD),
    )
    query_positions = (
        first_start + jnp.arange(half_rows, dtype=jnp.int32),
        second_start + jnp.arange(half_rows, dtype=jnp.int32),
    )
    last_positions = (first_start + half_rows - 1, second_start + half_rows - 1)

    def block_update(carry, query_four, query_pos, key_block, value_block, key_start):
        run_max, run_sum, run_acc = carry
        width = key_block.shape[0]
        key_three = key_block.reshape(width, kv_here, HD)
        value_three = value_block.reshape(width, kv_here, HD)
        scores = (
            jnp.einsum("tghd,kgd->ghtk", query_four, key_three, preferred_element_type=jnp.float32)
            * scale
        )
        key_pos = key_start + jnp.arange(width, dtype=jnp.int32)
        allowed = key_pos[None, :] <= query_pos[:, None]
        scores = jnp.where(allowed, scores, -1e30)
        new_max = jnp.maximum(run_max, jnp.max(scores, axis=-1))
        probs = jnp.where(allowed, jnp.exp(scores - new_max[..., None]), 0.0)
        factor = jnp.exp(run_max - new_max)
        run_sum = run_sum * factor + jnp.sum(probs, axis=-1)
        weighted = jnp.einsum(
            "ghtk,kgd->ghtd",
            probs.astype(jnp.bfloat16),
            value_three,
            preferred_element_type=jnp.float32,
        )
        run_acc = run_acc * factor[..., None] + weighted
        return (new_max, run_sum, run_acc)

    start_max = jnp.full((kv_here, heads_per_kv, half_rows), -1e30, jnp.float32)
    start_sum = jnp.zeros((kv_here, heads_per_kv, half_rows), jnp.float32)
    start_acc = jnp.zeros((kv_here, heads_per_kv, half_rows, HD), jnp.float32)
    start_state = (start_max, start_sum, start_acc)
    key_piece = lax.all_gather(key_cols, "ctx", axis=0, tiled=True)
    value_piece = lax.all_gather(value_cols, "ctx", axis=0, tiled=True)
    count = key_piece.shape[0]
    width = 512

    def one_block(index, inner):
        key_start = index * width
        key_block = lax.dynamic_slice_in_dim(key_piece, key_start, width, 0)
        value_block = lax.dynamic_slice_in_dim(value_piece, key_start, width, 0)
        updated = []
        for which in range(2):
            query_four = query_sets[which]
            query_pos = query_positions[which]
            updated.append(
                lax.cond(
                    key_start > last_positions[which],
                    lambda state: state,
                    lambda state: block_update(
                        state, query_four, query_pos, key_block, value_block, key_start
                    ),
                    inner[which],
                )
            )
        return (updated[0], updated[1])

    states = lax.fori_loop(0, count // width, one_block, (start_state, start_state))
    halves = []
    for which in range(2):
        run_max, run_sum, run_acc = states[which]
        halves.append(
            jnp.transpose(run_acc / run_sum[..., None], (2, 0, 1, 3))
            .reshape(half_rows, heads_here * HD)
            .astype(jnp.bfloat16)
        )
    attn_second = halves[1]
    attn = jnp.concatenate([halves[0], attn_second], axis=0)
    projected = lax.psum_scatter(
        jnp.dot(attn, w_out, preferred_element_type=jnp.float32).astype(jnp.bfloat16),
        "exp",
        scatter_dimension=0,
        tiled=True,
    ).astype(jnp.float32)
    hidden_state = (residual.astype(jnp.float32) + projected).astype(jnp.bfloat16)
    state_f = hidden_state.astype(jnp.float32)
    inv_rms = 1.0 / jnp.sqrt(jnp.mean(state_f * state_f, axis=1, keepdims=True) + 1e-06)
    normed = (state_f * inv_rms * norm_gain.astype(jnp.float32)[None, :]).astype(jnp.bfloat16)
    rows_here = expert_ids.shape[0]
    top_count = expert_ids.shape[1]
    experts_all = w_gate.shape[0] * exp_count
    capacity = min(rows_here, 2 * rows_here * top_count // experts_all)
    flat_ids = expert_ids.reshape(-1)
    onehot = (flat_ids[:, None] == jnp.arange(experts_all, dtype=jnp.int32)[None, :]).astype(
        jnp.int32
    )
    earlier = jnp.cumsum(onehot, axis=0) - onehot
    slot_index = jnp.sum(earlier * onehot, axis=1)
    target = flat_ids * capacity + slot_index
    picks = target[:, None] == jnp.arange(experts_all * capacity, dtype=jnp.int32)[None, :]
    dispatch_table = jnp.any(
        picks.reshape(rows_here, top_count, experts_all * capacity), axis=1
    ).astype(jnp.bfloat16)
    outgoing = jnp.einsum(
        "rs,rd->sd", dispatch_table, normed, preferred_element_type=jnp.float32
    ).astype(jnp.bfloat16)
    arrived = lax.all_to_all(
        outgoing.reshape(experts_all, capacity, D), "exp", split_axis=0, concat_axis=0, tiled=True
    )
    slot_rows = arrived.reshape(experts_all * capacity, D)
    gate_local = w_gate[0]
    up_local = w_up[0]
    gate_pre = jnp.dot(
        slot_rows,
        lax.all_gather(gate_local, "ctx", axis=0, tiled=True),
        preferred_element_type=jnp.float32,
    )
    up_pre = jnp.dot(
        slot_rows,
        lax.all_gather(up_local, "ctx", axis=0, tiled=True),
        preferred_element_type=jnp.float32,
    )
    expert_hidden = (jax.nn.silu(gate_pre) * up_pre).astype(jnp.bfloat16)
    down_local = w_down[0]
    expert_result = jnp.dot(
        expert_hidden,
        lax.all_gather(down_local, "ctx", axis=1, tiled=True),
        preferred_element_type=jnp.float32,
    ).astype(jnp.bfloat16)
    returned = lax.all_to_all(
        expert_result.reshape(experts_all, capacity, D),
        "exp",
        split_axis=0,
        concat_axis=0,
        tiled=True,
    )
    returned_flat = returned.reshape(experts_all * capacity, D)
    picked = jnp.dot(picks.astype(jnp.bfloat16), returned_flat, preferred_element_type=jnp.float32)
    weighted = gate_weights[:, :, None] * picked.reshape(rows_here, top_count, D)
    return (state_f + jnp.sum(weighted, axis=1)).astype(jnp.bfloat16)


BF16 = jnp.bfloat16
F32 = jnp.float32
VMEM = pltpu.VMEM
QB = 256
CHEAP = pl.CostEstimate(flops=1000, bytes_accessed=1000, transcendentals=0)


def swap(array, axis, mask):
    size = lax.axis_size(axis)
    return lax.ppermute(array, axis, [(i, i ^ mask) for i in range(size)])


def params(mib):
    return pltpu.CompilerParams(vmem_limit_bytes=mib * 1024 * 1024)


def vmem_specs(count):
    return [pl.BlockSpec(memory_space=VMEM) for _ in range(count)]


def attention_kernel(index, q, *refs):
    pieces, w_hbm, outs = refs[:8], refs[8], refs[9:13]
    w_all, keys, ones_values, bias, even, odd, attn, sems = refs[13:]
    ctx = index[0]
    exp = index[1]
    chip = ctx // 2
    steps = sems.shape[0]
    depth = w_all.shape[0] // steps
    fetches = [
        pltpu.make_async_copy(
            w_hbm.at[pl.ds(i * depth, depth)], w_all.at[pl.ds(i * depth, depth)], sems.at[i]
        )
        for i in range(steps)
    ]
    for fetch in fetches:
        fetch.start()
    factor = math.log2(math.e) / math.sqrt(HD)
    heads = q.shape[1] // HD
    ones_values[:, HD:] = jnp.ones((ones_values.shape[0], HD), BF16)
    core = ctx % 2
    for d in range(4):

        @pl.when(chip >= d)
        def _():
            for other in range(2):
                piece = pieces[2 * d + other]
                place = 2 * (chip - d) + (core ^ other)
                here = pl.ds(pl.multiple_of(place * QB, QB), QB)
                keys[:, here] = piece[:, :HD].astype(F32).T.astype(BF16)
                ones_values[here, :HD] = piece[:, HD:]

    row = lax.broadcasted_iota(jnp.int32, (QB, 2 * QB), 0) + core * QB
    col = lax.broadcasted_iota(jnp.int32, (QB, 2 * QB), 1)
    bias[...] = jnp.where(col <= row, 0.0, -1e30)
    part = QB // 4

    def run(length):
        def scores_of(h, store):
            rows = q[:, pl.ds(pl.multiple_of(h * HD, HD), HD)]
            block = jnp.dot(rows, keys[:, :length], preferred_element_type=F32)
            last = length - 2 * QB
            if last:
                store[:, :last] = block[:, :last]
            store[:, last:length] = block[:, last:] + bias[...]

        def finish(h, store):
            block = store[:, :length]
            top = jnp.max(block, axis=1, keepdims=True) * factor
            probs = jnp.exp2(block * factor - top).astype(BF16)
            total = jnp.dot(probs, ones_values[:length, :], preferred_element_type=F32)
            done = (total[:, :HD] / total[:, HD:]).astype(BF16)
            cols = pl.ds(pl.multiple_of(h * HD, HD), HD)
            for i in range(4):
                start = pl.multiple_of((exp ^ i) * part, part)
                attn[pl.ds(start, part), cols] = done[i * part : (i + 1) * part]

        scores_of(0, even)

        @pl.loop(0, heads // 2)
        def _(pair):
            scores_of(2 * pair + 1, odd)
            finish(2 * pair, even)
            scores_of(jnp.minimum(2 * pair + 2, heads - 1), even)
            finish(2 * pair + 1, odd)

    for z in range(4):
        pl.when(chip == z)(functools.partial(run, (z + 1) * 2 * QB))

    for fetch in fetches:
        fetch.wait()
    width = 512
    for n in range(w_all.shape[1] // width):
        cols = slice(n * width, (n + 1) * width)
        block = jnp.dot(attn[...], w_all[:, cols], preferred_element_type=F32).astype(BF16)
        for b, out in enumerate(outs):
            out[:, cols] = block[b * part : (b + 1) * part]


def attention(index, queries, pieces, w_out):
    rows = QB // 4
    length = 8 * QB
    return pl.pallas_call(
        attention_kernel,
        out_shape=[jax.ShapeDtypeStruct((rows, D), BF16)] * 4,
        in_specs=[pl.BlockSpec(memory_space=pltpu.SMEM)]
        + vmem_specs(9)
        + [pl.BlockSpec(memory_space=pl.ANY)],
        out_specs=vmem_specs(4),
        scratch_shapes=[
            VMEM(w_out.shape, BF16),
            VMEM((HD, length), BF16),
            VMEM((length, 2 * HD), BF16),
            VMEM((QB, 2 * QB), F32),
            VMEM((QB, length), F32),
            VMEM((QB, length), F32),
            VMEM(queries.shape, BF16),
            pltpu.SemaphoreType.DMA((16,)),
        ],
        compiler_params=params(52),
        cost_estimate=CHEAP,
        name="attention",
    )(index, queries, *pieces, w_out)


def norm_kernel(index, p0, r1, r2, r3, residual, gain, state, mine, theirs, work):
    ctx = index[0]
    total = p0[...].astype(F32) + r1[...].astype(F32) + r2[...].astype(F32) + r3[...].astype(F32)
    hidden = (residual[...].astype(F32) + total).astype(BF16)
    state[...] = hidden
    wide = hidden.astype(F32)
    inv = 1.0 / jnp.sqrt(jnp.mean(wide * wide, axis=1, keepdims=True) + 1e-06)
    normed = (wide * inv * gain[...].astype(F32)).astype(BF16)
    part = D // 8
    for j in range(8):
        work[j] = normed[:, j * part : (j + 1) * part]
    for j, (a, b) in enumerate(((0, 2), (1, 3), (6, 4), (7, 5))):
        mine[:, j * part : (j + 1) * part] = work[ctx ^ a]
        theirs[:, j * part : (j + 1) * part] = work[ctx ^ b]


def norm(index, p0, r1, r2, r3, residual, gain):
    rows = residual.shape[0]
    half = jax.ShapeDtypeStruct((rows, D // 2), BF16)
    return pl.pallas_call(
        norm_kernel,
        out_shape=[jax.ShapeDtypeStruct((rows, D), BF16), half, half],
        in_specs=[pl.BlockSpec(memory_space=pltpu.SMEM)] + vmem_specs(6),
        out_specs=vmem_specs(3),
        scratch_shapes=[VMEM((8, rows, D // 8), BF16)],
        compiler_params=params(16),
        cost_estimate=CHEAP,
        name="norm",
    )(index, p0, r1, r2, r3, residual, gain)


def enter_kernel(x0, x1, x2, x3, *refs):
    weights, out, gate_all, up_all, sems = refs[:4], refs[4], refs[5], refs[6], refs[7]
    part, width = weights[0].shape[0] // 2, weights[0].shape[1]
    fetches = []
    for which, whole in enumerate((gate_all, up_all)):
        for j, array in enumerate(weights):
            source = array.at[pl.ds(which * part, part)]
            target = whole.at[pl.ds(j * part, part)]
            fetches.append(pltpu.make_async_copy(source, target, sems.at[4 * which + j]))
            fetches[-1].start()
    x = jnp.concatenate([x0[...], x1[...], x2[...], x3[...]], axis=0)
    tile = 256
    for which, whole in enumerate((gate_all, up_all)):
        for fetch in fetches[4 * which : 4 * which + 4]:
            fetch.wait()
        for n in range(width // tile):
            cols = slice(which * width + n * tile, which * width + (n + 1) * tile)
            block = jnp.dot(x, whole[:, n * tile : (n + 1) * tile], preferred_element_type=F32)
            out[:, cols] = block.astype(out.dtype)


def enter(rows, weights, kind):
    count = 4 * rows[0].shape[0]
    part, width = weights[0].shape[0] // 2, weights[0].shape[1]
    return pl.pallas_call(
        enter_kernel,
        out_shape=jax.ShapeDtypeStruct((count, 2 * width), kind),
        in_specs=vmem_specs(4) + [pl.BlockSpec(memory_space=pl.ANY)] * 4,
        out_specs=pl.BlockSpec(memory_space=VMEM),
        scratch_shapes=[
            VMEM((4 * part, width), BF16),
            VMEM((4 * part, width), BF16),
            pltpu.SemaphoreType.DMA((8,)),
        ],
        compiler_params=params(24),
        cost_estimate=CHEAP,
        name="enter",
    )(*rows, *weights)


def silu_kernel(own, other, c0, c1, c2, c3, out):
    width = out.shape[1]
    part = c0.shape[0]
    total = own[...] + other[...].astype(F32)
    gate, up = total[:, :width], total[:, width:]
    hidden = gate / (1.0 + jnp.exp(-gate)) * up
    for b, share in enumerate((c0, c1, c2, c3)):
        rows = slice(b * part, (b + 1) * part)
        out[rows] = (hidden[rows] * share[:, :1]).astype(BF16)


def silu(own, other, shares):
    return pl.pallas_call(
        silu_kernel,
        out_shape=jax.ShapeDtypeStruct((own.shape[0], own.shape[1] // 2), BF16),
        in_specs=vmem_specs(6),
        out_specs=pl.BlockSpec(memory_space=VMEM),
        compiler_params=params(16),
        cost_estimate=CHEAP,
        name="silu",
    )(own, other, *shares)


def leave_kernel(hidden, d0, d1, d2, d3, y0, y1, y2, y3, down_all, sems):
    part = y0.shape[0]
    width = d0.shape[1]
    fetches = []
    for j, array in enumerate((d0, d1, d2, d3)):
        fetches.append(pltpu.make_async_copy(array, down_all.at[j], sems.at[j]))
        fetches[-1].start()
    for j in range(4):
        fetches[j].wait()
        block = jnp.dot(hidden[...], down_all[j], preferred_element_type=F32).astype(BF16)
        for b, out in enumerate((y0, y1, y2, y3)):
            out[:, j * width : (j + 1) * width] = block[b * part : (b + 1) * part]


def leave(hidden, downs):
    part = jax.ShapeDtypeStruct((hidden.shape[0] // 4, 4 * downs[0].shape[1]), BF16)
    return pl.pallas_call(
        leave_kernel,
        out_shape=[part] * 4,
        in_specs=vmem_specs(1) + [pl.BlockSpec(memory_space=pl.ANY)] * 4,
        out_specs=vmem_specs(4),
        scratch_shapes=[VMEM((4,) + downs[0].shape, BF16), pltpu.SemaphoreType.DMA((4,))],
        compiler_params=params(16),
        cost_estimate=CHEAP,
        name="leave",
    )(hidden, *downs)


def total_kernel(y0, r1, r2, r3, out):
    out[...] = (
        y0[...].astype(F32) + r1[...].astype(F32) + r2[...].astype(F32) + r3[...].astype(F32)
    ).astype(BF16)


def total_of(y0, r1, r2, r3):
    return pl.pallas_call(
        total_kernel,
        out_shape=jax.ShapeDtypeStruct(y0.shape, BF16),
        in_specs=vmem_specs(4),
        out_specs=pl.BlockSpec(memory_space=VMEM),
        cost_estimate=CHEAP,
        name="total",
    )(y0, r1, r2, r3)


def final_kernel(index, state, y0, r1, r2, r3, other, out):
    ctx = index[0]
    part = D // 8
    own = y0[...].astype(F32) + r1[...].astype(F32) + r2[...].astype(F32) + r3[...].astype(F32)
    for j, (a, b) in enumerate(((0, 2), (1, 3), (6, 4), (7, 5))):
        cols = slice(j * part, (j + 1) * part)
        here = pl.ds(pl.multiple_of((ctx ^ a) * part, part), part)
        out[:, here] = (state[:, here].astype(F32) + own[:, cols]).astype(BF16)
        there = pl.ds(pl.multiple_of((ctx ^ b) * part, part), part)
        out[:, there] = (state[:, there].astype(F32) + other[:, cols].astype(F32)).astype(BF16)


def final(index, state, y0, r1, r2, r3, other):
    return pl.pallas_call(
        final_kernel,
        out_shape=jax.ShapeDtypeStruct(state.shape, BF16),
        in_specs=[pl.BlockSpec(memory_space=pltpu.SMEM)] + vmem_specs(6),
        out_specs=pl.BlockSpec(memory_space=VMEM),
        compiler_params=params(16),
        cost_estimate=CHEAP,
        name="final",
    )(index, state, y0, r1, r2, r3, other)


def body(
    queries,
    keys,
    values,
    w_out,
    residual,
    norm_gain,
    expert_ids,
    gate_weights,
    w_gate,
    w_up,
    w_down,
):
    exp = lax.axis_index("exp")
    ctx = lax.axis_index("ctx")
    index = jnp.stack([ctx, exp]).astype(jnp.int32)
    kv_first = exp * (HQ // 4) // (HQ // KVH) * HD
    kv_here = jnp.concatenate(
        [
            lax.dynamic_slice_in_dim(keys, kv_first, HD, 1),
            lax.dynamic_slice_in_dim(values, kv_first, HD, 1),
        ],
        axis=1,
    )
    pair_here, down_here = jnp.concatenate([w_gate[0], w_up[0]], axis=0), w_down[0]

    def later(array, chips):
        return lax.ppermute(array, "ctx", [(i, i + 2 * chips) for i in range(8 - 2 * chips)])

    pieces = [kv_here] + [later(kv_here, d) for d in (3, 2, 1)][::-1]
    pieces = [part for piece in pieces for part in (piece, swap(piece, "ctx", 1))]

    shares = []
    for b in range(4):
        share = jnp.sum(jnp.where(expert_ids == (exp ^ b), gate_weights, 0.0), axis=1, keepdims=True)
        share = jnp.broadcast_to(share, (share.shape[0], HD))
        shares.append(swap(share, "exp", b) if b else share)
    near = [swap(array, "ctx", 1) for array in (pair_here, down_here)]

    pieces, shares, near, pair_here = lax.optimization_barrier((pieces, shares, near, pair_here))
    pair_far = swap(pair_here, "ctx", 6)

    p = attention(index, queries, pieces, w_out)
    r = [swap(p[b], "exp", b) for b in (1, 2, 3)]
    state, mine, theirs = norm(index, p[0], *r, residual, norm_gain.reshape(1, D))
    others = swap(theirs, "ctx", 2)
    own_rows = [mine] + [swap(mine, "exp", b) for b in (1, 2, 3)]
    other_rows = [others] + [swap(others, "exp", b) for b in (1, 2, 3)]
    own_rows, other_rows, pair_far, down_here = lax.optimization_barrier(
        (own_rows, other_rows, pair_far, down_here)
    )
    down_far = swap(down_here, "ctx", 6)
    pairs = (pair_here, near[0], pair_far, swap(pair_far, "ctx", 1))
    other_pre = enter(other_rows, pairs, BF16)
    from_other = swap(other_pre, "ctx", 2)
    own_pre = enter(own_rows, pairs, F32)
    own_hidden = silu(own_pre, from_other, shares)
    other_hidden = swap(own_hidden, "ctx", 2)
    own_hidden, down_far = lax.optimization_barrier((own_hidden, down_far))
    downs = (down_here, near[1], down_far, swap(down_far, "ctx", 1))
    y = leave(own_hidden, downs)
    own_parts = [y[0]] + [swap(y[b], "exp", b) for b in (1, 2, 3)]
    z = leave(other_hidden, downs)
    other_parts = [z[0]] + [swap(z[b], "exp", b) for b in (1, 2, 3)]
    back = swap(total_of(*other_parts), "ctx", 2)
    return final(index, state, *own_parts, back)


def solution(mesh):
    placed = (
        P("ctx", "exp"),
        P("ctx", None),
        P("ctx", None),
        P("exp", None),
        P(("ctx", "exp"), None),
        P(),
        P(("ctx", "exp"), None),
        P(("ctx", "exp"), None),
        P("exp", "ctx", None),
        P("exp", "ctx", None),
        P("exp", None, "ctx"),
    )
    shape = dict(mesh.shape)
    small = shape["ctx"] == 8 and shape["exp"] == 4
    return jax.shard_map(
        body if small else general_body, mesh=mesh, in_specs=placed, out_specs=P(("ctx", "exp"), None), check_vma=False
    )
```

```python
import functools
import math

import jax
import jax.numpy as jnp
from jax import lax
from jax.experimental import pallas as pl
from jax.experimental.pallas import tpu as pltpu
from jax.sharding import PartitionSpec as P

D = 4096
HQ = 64
KVH = 4
HD = 128


def general_body(
    queries,
    keys,
    values,
    w_out,
    residual,
    norm_gain,
    expert_ids,
    gate_weights,
    w_gate,
    w_up,
    w_down,
):
    tok_rows = queries.shape[0]
    half_rows = tok_rows // 2
    exp_count = lax.axis_size("exp")
    heads_here = HQ // exp_count
    group = HQ // KVH
    kv_here = max(1, heads_here // group)
    heads_per_kv = heads_here // kv_here
    exp_index = lax.axis_index("exp")
    ctx_index = lax.axis_index("ctx")
    kv_first = exp_index * heads_here // group
    key_cols = lax.dynamic_slice_in_dim(keys, kv_first * HD, kv_here * HD, 1)
    value_cols = lax.dynamic_slice_in_dim(values, kv_first * HD, kv_here * HD, 1)
    scale = 1.0 / math.sqrt(HD)
    first_rows = queries[:half_rows]
    second_rows = queries[half_rows:]
    first_start = ctx_index * tok_rows
    second_start = ctx_index * tok_rows + half_rows
    query_sets = (
        first_rows.reshape(half_rows, kv_here, heads_per_kv, HD),
        second_rows.reshape(half_rows, kv_here, heads_per_kv, HD),
    )
    query_positions = (
        first_start + jnp.arange(half_rows, dtype=jnp.int32),
        second_start + jnp.arange(half_rows, dtype=jnp.int32),
    )
    last_positions = (first_start + half_rows - 1, second_start + half_rows - 1)

    def block_update(carry, query_four, query_pos, key_block, value_block, key_start):
        run_max, run_sum, run_acc = carry
        width = key_block.shape[0]
        key_three = key_block.reshape(width, kv_here, HD)
        value_three = value_block.reshape(width, kv_here, HD)
        scores = (
            jnp.einsum("tghd,kgd->ghtk", query_four, key_three, preferred_element_type=jnp.float32)
            * scale
        )
        key_pos = key_start + jnp.arange(width, dtype=jnp.int32)
        allowed = key_pos[None, :] <= query_pos[:, None]
        scores = jnp.where(allowed, scores, -1e30)
        new_max = jnp.maximum(run_max, jnp.max(scores, axis=-1))
        probs = jnp.where(allowed, jnp.exp(scores - new_max[..., None]), 0.0)
        factor = jnp.exp(run_max - new_max)
        run_sum = run_sum * factor + jnp.sum(probs, axis=-1)
        weighted = jnp.einsum(
            "ghtk,kgd->ghtd",
            probs.astype(jnp.bfloat16),
            value_three,
            preferred_element_type=jnp.float32,
        )
        run_acc = run_acc * factor[..., None] + weighted
        return (new_max, run_sum, run_acc)

    start_max = jnp.full((kv_here, heads_per_kv, half_rows), -1e30, jnp.float32)
    start_sum = jnp.zeros((kv_here, heads_per_kv, half_rows), jnp.float32)
    start_acc = jnp.zeros((kv_here, heads_per_kv, half_rows, HD), jnp.float32)
    start_state = (start_max, start_sum, start_acc)
    key_piece = lax.all_gather(key_cols, "ctx", axis=0, tiled=True)
    value_piece = lax.all_gather(value_cols, "ctx", axis=0, tiled=True)
    count = key_piece.shape[0]
    width = 512

    def one_block(index, inner):
        key_start = index * width
        key_block = lax.dynamic_slice_in_dim(key_piece, key_start, width, 0)
        value_block = lax.dynamic_slice_in_dim(value_piece, key_start, width, 0)
        updated = []
        for which in range(2):
            query_four = query_sets[which]
            query_pos = query_positions[which]
            updated.append(
                lax.cond(
                    key_start > last_positions[which],
                    lambda state: state,
                    lambda state: block_update(
                        state, query_four, query_pos, key_block, value_block, key_start
                    ),
                    inner[which],
                )
            )
        return (updated[0], updated[1])

    states = lax.fori_loop(0, count // width, one_block, (start_state, start_state))
    halves = []
    for which in range(2):
        run_max, run_sum, run_acc = states[which]
        halves.append(
            jnp.transpose(run_acc / run_sum[..., None], (2, 0, 1, 3))
            .reshape(half_rows, heads_here * HD)
            .astype(jnp.bfloat16)
        )
    attn_second = halves[1]
    attn = jnp.concatenate([halves[0], attn_second], axis=0)
    projected = lax.psum_scatter(
        jnp.dot(attn, w_out, preferred_element_type=jnp.float32).astype(jnp.bfloat16),
        "exp",
        scatter_dimension=0,
        tiled=True,
    ).astype(jnp.float32)
    hidden_state = (residual.astype(jnp.float32) + projected).astype(jnp.bfloat16)
    state_f = hidden_state.astype(jnp.float32)
    inv_rms = 1.0 / jnp.sqrt(jnp.mean(state_f * state_f, axis=1, keepdims=True) + 1e-06)
    normed = (state_f * inv_rms * norm_gain.astype(jnp.float32)[None, :]).astype(jnp.bfloat16)
    rows_here = expert_ids.shape[0]
    top_count = expert_ids.shape[1]
    experts_all = w_gate.shape[0] * exp_count
    capacity = min(rows_here, 2 * rows_here * top_count // experts_all)
    flat_ids = expert_ids.reshape(-1)
    onehot = (flat_ids[:, None] == jnp.arange(experts_all, dtype=jnp.int32)[None, :]).astype(
        jnp.int32
    )
    earlier = jnp.cumsum(onehot, axis=0) - onehot
    slot_index = jnp.sum(earlier * onehot, axis=1)
    target = flat_ids * capacity + slot_index
    picks = target[:, None] == jnp.arange(experts_all * capacity, dtype=jnp.int32)[None, :]
    dispatch_table = jnp.any(
        picks.reshape(rows_here, top_count, experts_all * capacity), axis=1
    ).astype(jnp.bfloat16)
    outgoing = jnp.einsum(
        "rs,rd->sd", dispatch_table, normed, preferred_element_type=jnp.float32
    ).astype(jnp.bfloat16)
    arrived = lax.all_to_all(
        outgoing.reshape(experts_all, capacity, D), "exp", split_axis=0, concat_axis=0, tiled=True
    )
    slot_rows = arrived.reshape(experts_all * capacity, D)
    gate_local = w_gate[0]
    up_local = w_up[0]
    gate_pre = jnp.dot(
        slot_rows,
        lax.all_gather(gate_local, "ctx", axis=0, tiled=True),
        preferred_element_type=jnp.float32,
    )
    up_pre = jnp.dot(
        slot_rows,
        lax.all_gather(up_local, "ctx", axis=0, tiled=True),
        preferred_element_type=jnp.float32,
    )
    expert_hidden = (jax.nn.silu(gate_pre) * up_pre).astype(jnp.bfloat16)
    down_local = w_down[0]
    expert_result = jnp.dot(
        expert_hidden,
        lax.all_gather(down_local, "ctx", axis=1, tiled=True),
        preferred_element_type=jnp.float32,
    ).astype(jnp.bfloat16)
    returned = lax.all_to_all(
        expert_result.reshape(experts_all, capacity, D),
        "exp",
        split_axis=0,
        concat_axis=0,
        tiled=True,
    )
    returned_flat = returned.reshape(experts_all * capacity, D)
    picked = jnp.dot(picks.astype(jnp.bfloat16), returned_flat, preferred_element_type=jnp.float32)
    weighted = gate_weights[:, :, None] * picked.reshape(rows_here, top_count, D)
    return (state_f + jnp.sum(weighted, axis=1)).astype(jnp.bfloat16)


BF16 = jnp.bfloat16
F32 = jnp.float32
VMEM = pltpu.VMEM
QB = 256
CHEAP = pl.CostEstimate(flops=1000, bytes_accessed=1000, transcendentals=0)


def swap(array, axis, mask):
    size = lax.axis_size(axis)
    return lax.ppermute(array, axis, [(i, i ^ mask) for i in range(size)])


def params(mib):
    return pltpu.CompilerParams(vmem_limit_bytes=mib * 1024 * 1024)


def vmem_specs(count):
    return [pl.BlockSpec(memory_space=VMEM) for _ in range(count)]


def attention_kernel(index, q_hbm, *refs):
    arrived, w_hbm, outs = refs[:8], refs[8], refs[9:13]
    w_all, q, pieces, keys, ones_values, bias, even, odd, attn, q_sem, piece_sems, sems = refs[13:]
    q_fetch = pltpu.make_async_copy(q_hbm, q, q_sem)
    piece_fetches = [
        pltpu.make_async_copy(arrived[i], pieces.at[i], piece_sems.at[i]) for i in range(8)
    ]
    for fetch in piece_fetches + [q_fetch]:
        fetch.start()
    ctx = index[0]
    exp = index[1]
    chip = ctx // 2
    steps = sems.shape[0]
    depth = w_all.shape[0] // steps
    fetches = [
        pltpu.make_async_copy(
            w_hbm.at[pl.ds(i * depth, depth)], w_all.at[pl.ds(i * depth, depth)], sems.at[i]
        )
        for i in range(steps)
    ]
    for fetch in fetches:
        fetch.start()
    factor = math.log2(math.e) / math.sqrt(HD)
    heads = q.shape[1] // HD
    ones_values[:, HD:] = jnp.ones((ones_values.shape[0], HD), BF16)
    core = ctx % 2
    row = lax.broadcasted_iota(jnp.int32, (QB, 2 * QB), 0) + core * QB
    col = lax.broadcasted_iota(jnp.int32, (QB, 2 * QB), 1)
    bias[...] = jnp.where(col <= row, 0.0, -1e30)
    for fetch in piece_fetches:
        fetch.wait()
    for d in range(4):

        @pl.when(chip >= d)
        def _():
            for other in range(2):
                piece = pieces.at[2 * d + other]
                place = 2 * (chip - d) + (core ^ other)
                here = pl.ds(pl.multiple_of(place * QB, QB), QB)
                keys[:, here] = piece[:, :HD].astype(F32).T.astype(BF16)
                ones_values[here, :HD] = piece[:, HD:]

    q_fetch.wait()
    part = QB // 4

    def run(length):
        def scores_of(h, store):
            rows = q[:, pl.ds(pl.multiple_of(h * HD, HD), HD)]
            block = jnp.dot(rows, keys[:, :length], preferred_element_type=F32)
            last = length - 2 * QB
            if last:
                store[:, :last] = block[:, :last]
            store[:, last:length] = block[:, last:] + bias[...]

        def finish(h, store):
            block = store[:, :length]
            top = jnp.max(block, axis=1, keepdims=True) * factor
            probs = jnp.exp2(block * factor - top).astype(BF16)
            total = jnp.dot(probs, ones_values[:length, :], preferred_element_type=F32)
            done = (total[:, :HD] / total[:, HD:]).astype(BF16)
            cols = pl.ds(pl.multiple_of(h * HD, HD), HD)
            for i in range(4):
                start = pl.multiple_of((exp ^ i) * part, part)
                attn[pl.ds(start, part), cols] = done[i * part : (i + 1) * part]

        scores_of(0, even)

        @pl.loop(0, heads // 2)
        def _(pair):
            scores_of(2 * pair + 1, odd)
            finish(2 * pair, even)
            scores_of(jnp.minimum(2 * pair + 2, heads - 1), even)
            finish(2 * pair + 1, odd)

    for z in range(4):
        pl.when(chip == z)(functools.partial(run, (z + 1) * 2 * QB))

    for fetch in fetches:
        fetch.wait()
    width = 512
    for n in range(w_all.shape[1] // width):
        cols = slice(n * width, (n + 1) * width)
        block = jnp.dot(attn[...], w_all[:, cols], preferred_element_type=F32).astype(BF16)
        for b, out in enumerate(outs):
            out[:, cols] = block[b * part : (b + 1) * part]


def attention(index, queries, pieces, w_out):
    rows = QB // 4
    length = 8 * QB
    return pl.pallas_call(
        attention_kernel,
        out_shape=[jax.ShapeDtypeStruct((rows, D), BF16)] * 4,
        in_specs=[pl.BlockSpec(memory_space=pltpu.SMEM)]
        + [pl.BlockSpec(memory_space=pl.ANY)] * 10,
        out_specs=vmem_specs(4),
        scratch_shapes=[
            VMEM(w_out.shape, BF16),
            VMEM(queries.shape, BF16),
            VMEM((8,) + pieces[0].shape, BF16),
            VMEM((HD, length), BF16),
            VMEM((length, 2 * HD), BF16),
            VMEM((QB, 2 * QB), F32),
            VMEM((QB, length), F32),
            VMEM((QB, length), F32),
            VMEM(queries.shape, BF16),
            pltpu.SemaphoreType.DMA,
            pltpu.SemaphoreType.DMA((8,)),
            pltpu.SemaphoreType.DMA((16,)),
        ],
        compiler_params=params(52),
        cost_estimate=CHEAP,
        name="attention",
    )(index, queries, *pieces, w_out)


def norm_kernel(index, p0, r1, r2, r3, residual, gain, state, mine, theirs, work):
    ctx = index[0]
    total = p0[...].astype(F32) + r1[...].astype(F32) + r2[...].astype(F32) + r3[...].astype(F32)
    hidden = (residual[...].astype(F32) + total).astype(BF16)
    state[...] = hidden
    wide = hidden.astype(F32)
    inv = 1.0 / jnp.sqrt(jnp.mean(wide * wide, axis=1, keepdims=True) + 1e-06)
    normed = (wide * inv * gain[...].astype(F32)).astype(BF16)
    part = D // 8
    for j in range(8):
        work[j] = normed[:, j * part : (j + 1) * part]
    for j, (a, b) in enumerate(((0, 2), (1, 3), (6, 4), (7, 5))):
        mine[:, j * part : (j + 1) * part] = work[ctx ^ a]
        theirs[:, j * part : (j + 1) * part] = work[ctx ^ b]


def norm(index, p0, r1, r2, r3, residual, gain):
    rows = residual.shape[0]
    half = jax.ShapeDtypeStruct((rows, D // 2), BF16)
    return pl.pallas_call(
        norm_kernel,
        out_shape=[jax.ShapeDtypeStruct((rows, D), BF16), half, half],
        in_specs=[pl.BlockSpec(memory_space=pltpu.SMEM)] + vmem_specs(6),
        out_specs=vmem_specs(3),
        scratch_shapes=[VMEM((8, rows, D // 8), BF16)],
        compiler_params=params(16),
        cost_estimate=CHEAP,
        name="norm",
    )(index, p0, r1, r2, r3, residual, gain)


def enter_kernel(x0, x1, x2, x3, *refs):
    weights, out, gate_all, up_all, sems = refs[:4], refs[4], refs[5], refs[6], refs[7]
    part, width = weights[0].shape[0] // 2, weights[0].shape[1]
    fetches = []
    for which, whole in enumerate((gate_all, up_all)):
        for j, array in enumerate(weights):
            source = array.at[pl.ds(which * part, part)]
            target = whole.at[pl.ds(j * part, part)]
            fetches.append(pltpu.make_async_copy(source, target, sems.at[4 * which + j]))
            fetches[-1].start()
    x = jnp.concatenate([x0[...], x1[...], x2[...], x3[...]], axis=0)
    tile = 256
    for which, whole in enumerate((gate_all, up_all)):
        for fetch in fetches[4 * which : 4 * which + 4]:
            fetch.wait()
        for n in range(width // tile):
            cols = slice(which * width + n * tile, which * width + (n + 1) * tile)
            block = jnp.dot(x, whole[:, n * tile : (n + 1) * tile], preferred_element_type=F32)
            out[:, cols] = block.astype(out.dtype)


def enter(rows, weights, kind):
    count = 4 * rows[0].shape[0]
    part, width = weights[0].shape[0] // 2, weights[0].shape[1]
    return pl.pallas_call(
        enter_kernel,
        out_shape=jax.ShapeDtypeStruct((count, 2 * width), kind),
        in_specs=vmem_specs(4) + [pl.BlockSpec(memory_space=pl.ANY)] * 4,
        out_specs=pl.BlockSpec(memory_space=VMEM),
        scratch_shapes=[
            VMEM((4 * part, width), BF16),
            VMEM((4 * part, width), BF16),
            pltpu.SemaphoreType.DMA((8,)),
        ],
        compiler_params=params(24),
        cost_estimate=CHEAP,
        name="enter",
    )(*rows, *weights)


def silu_kernel(own, other, out):
    width = out.shape[1]
    total = own[...] + other[...].astype(F32)
    gate, up = total[:, :width], total[:, width:]
    out[...] = (gate / (1.0 + jnp.exp(-gate)) * up).astype(BF16)


def silu(own, other):
    return pl.pallas_call(
        silu_kernel,
        out_shape=jax.ShapeDtypeStruct((own.shape[0], own.shape[1] // 2), BF16),
        in_specs=vmem_specs(2),
        out_specs=pl.BlockSpec(memory_space=VMEM),
        compiler_params=params(16),
        cost_estimate=CHEAP,
        name="silu",
    )(own, other)


def leave_kernel(hidden, d0, d1, d2, d3, y0, y1, y2, y3, down_all, sems):
    part = y0.shape[0]
    width = d0.shape[1]
    fetches = []
    for j, array in enumerate((d0, d1, d2, d3)):
        fetches.append(pltpu.make_async_copy(array, down_all.at[j], sems.at[j]))
        fetches[-1].start()
    for j in range(4):
        fetches[j].wait()
        block = jnp.dot(hidden[...], down_all[j], preferred_element_type=F32).astype(BF16)
        for b, out in enumerate((y0, y1, y2, y3)):
            out[:, j * width : (j + 1) * width] = block[b * part : (b + 1) * part]


def leave(hidden, downs):
    part = jax.ShapeDtypeStruct((hidden.shape[0] // 4, 4 * downs[0].shape[1]), BF16)
    return pl.pallas_call(
        leave_kernel,
        out_shape=[part] * 4,
        in_specs=vmem_specs(1) + [pl.BlockSpec(memory_space=pl.ANY)] * 4,
        out_specs=vmem_specs(4),
        scratch_shapes=[VMEM((4,) + downs[0].shape, BF16), pltpu.SemaphoreType.DMA((4,))],
        compiler_params=params(16),
        cost_estimate=CHEAP,
        name="leave",
    )(hidden, *downs)


def mixed(shares, parts):
    total = shares[:, :1] * parts[0][...].astype(F32)
    for b in range(1, 4):
        total = total + shares[:, b : b + 1] * parts[b][...].astype(F32)
    return total


def total_kernel(shares, y0, r1, r2, r3, out):
    out[...] = mixed(shares, (y0, r1, r2, r3)).astype(BF16)


def total_of(shares, y0, r1, r2, r3):
    return pl.pallas_call(
        total_kernel,
        out_shape=jax.ShapeDtypeStruct(y0.shape, BF16),
        in_specs=vmem_specs(5),
        out_specs=pl.BlockSpec(memory_space=VMEM),
        cost_estimate=CHEAP,
        name="total",
    )(shares, y0, r1, r2, r3)


def final_kernel(index, state, shares, y0, r1, r2, r3, other, out):
    ctx = index[0]
    part = D // 8
    own = mixed(shares, (y0, r1, r2, r3))
    for j, (a, b) in enumerate(((0, 2), (1, 3), (6, 4), (7, 5))):
        cols = slice(j * part, (j + 1) * part)
        here = pl.ds(pl.multiple_of((ctx ^ a) * part, part), part)
        out[:, here] = (state[:, here].astype(F32) + own[:, cols]).astype(BF16)
        there = pl.ds(pl.multiple_of((ctx ^ b) * part, part), part)
        out[:, there] = (state[:, there].astype(F32) + other[:, cols].astype(F32)).astype(BF16)


def final(index, state, shares, y0, r1, r2, r3, other):
    return pl.pallas_call(
        final_kernel,
        out_shape=jax.ShapeDtypeStruct(state.shape, BF16),
        in_specs=[pl.BlockSpec(memory_space=pltpu.SMEM)] + vmem_specs(7),
        out_specs=pl.BlockSpec(memory_space=VMEM),
        compiler_params=params(16),
        cost_estimate=CHEAP,
        name="final",
    )(index, state, shares, y0, r1, r2, r3, other)


def body(
    queries,
    keys,
    values,
    w_out,
    residual,
    norm_gain,
    expert_ids,
    gate_weights,
    w_gate,
    w_up,
    w_down,
):
    exp = lax.axis_index("exp")
    ctx = lax.axis_index("ctx")
    index = jnp.stack([ctx, exp]).astype(jnp.int32)
    kv_first = exp * (HQ // 4) // (HQ // KVH) * HD
    kv_here = jnp.concatenate(
        [
            lax.dynamic_slice_in_dim(keys, kv_first, HD, 1),
            lax.dynamic_slice_in_dim(values, kv_first, HD, 1),
        ],
        axis=1,
    )
    def later(array, chips):
        return lax.ppermute(array, "ctx", [(i, i + 2 * chips) for i in range(8 - 2 * chips)])

    kv_here, gate_here, up_here = lax.optimization_barrier((kv_here, w_gate[0], w_up[0]))
    moved = [later(kv_here, d) for d in (3, 2, 1)][::-1]
    pair_here, down_here = jnp.concatenate([gate_here, up_here], axis=0), w_down[0]
    pieces = [part for piece in [kv_here] + moved for part in (piece, swap(piece, "ctx", 1))]
    pieces, pair_here = lax.optimization_barrier((pieces, pair_here))
    pair_far = swap(pair_here, "ctx", 6)

    lane = lax.broadcasted_iota(jnp.int32, (expert_ids.shape[0], HD), 1)
    shares = jnp.zeros(lane.shape, F32)
    for k in range(expert_ids.shape[1]):
        named = expert_ids[:, k : k + 1] ^ exp
        shares = shares + jnp.where(lane == named, gate_weights[:, k : k + 1], 0.0)

    p = attention(index, queries, pieces, w_out)
    p, shares, pair_here, down_here = lax.optimization_barrier((p, shares, pair_here, down_here))
    r = [swap(p[b], "exp", b) for b in (1, 2, 3)]
    pair_near, down_near = swap(pair_here, "ctx", 1), swap(down_here, "ctx", 1)
    other_shares = swap(shares, "ctx", 2)
    state, mine, theirs = norm(index, p[0], *r, residual, norm_gain.reshape(1, D))
    others = swap(theirs, "ctx", 2)
    own_rows = [mine] + [swap(mine, "exp", b) for b in (1, 2, 3)]
    other_rows = [others] + [swap(others, "exp", b) for b in (1, 2, 3)]
    own_rows, others, pair_far, down_here = lax.optimization_barrier(
        (own_rows, others, pair_far, down_here)
    )
    down_far = swap(down_here, "ctx", 6)
    pairs = (pair_here, pair_near, pair_far, swap(pair_far, "ctx", 1))
    other_pre = enter(other_rows, pairs, BF16)
    from_other = swap(other_pre, "ctx", 2)
    own_rows, down_far = lax.optimization_barrier((own_rows, down_far))
    own_pre = enter(own_rows, pairs, F32)
    own_hidden = silu(own_pre, from_other)
    other_hidden = swap(own_hidden, "ctx", 2)
    downs = (down_here, down_near, down_far, swap(down_far, "ctx", 1))
    y = leave(own_hidden, downs)
    own_parts = [y[0]] + [swap(y[b], "exp", b) for b in (1, 2, 3)]
    other_hidden, *own_parts[1:3] = lax.optimization_barrier((other_hidden, *own_parts[1:3]))
    z = leave(other_hidden, downs)
    other_parts = [z[0]] + [swap(z[b], "exp", b) for b in (1, 2, 3)]
    back = swap(total_of(other_shares, *other_parts), "ctx", 2)
    return final(index, state, shares, *own_parts, back)


def solution(mesh):
    placed = (
        P("ctx", "exp"),
        P("ctx", None),
        P("ctx", None),
        P("exp", None),
        P(("ctx", "exp"), None),
        P(),
        P(("ctx", "exp"), None),
        P(("ctx", "exp"), None),
        P("exp", "ctx", None),
        P("exp", "ctx", None),
        P("exp", None, "ctx"),
    )
    shape = dict(mesh.shape)
    small = shape["ctx"] == 8 and shape["exp"] == 4
    return jax.shard_map(
        body if small else general_body, mesh=mesh, in_specs=placed, out_specs=P(("ctx", "exp"), None), check_vma=False
    )
```

```python
import functools
import math

import jax
import jax.numpy as jnp
from jax import lax
from jax.experimental import pallas as pl
from jax.experimental.pallas import tpu as pltpu
from jax.sharding import PartitionSpec as P

D = 4096
HQ = 64
KVH = 4
HD = 128


def general_body(
    queries,
    keys,
    values,
    w_out,
    residual,
    norm_gain,
    expert_ids,
    gate_weights,
    w_gate,
    w_up,
    w_down,
):
    tok_rows = queries.shape[0]
    half_rows = tok_rows // 2
    exp_count = lax.axis_size("exp")
    heads_here = HQ // exp_count
    group = HQ // KVH
    kv_here = max(1, heads_here // group)
    heads_per_kv = heads_here // kv_here
    exp_index = lax.axis_index("exp")
    ctx_index = lax.axis_index("ctx")
    kv_first = exp_index * heads_here // group
    key_cols = lax.dynamic_slice_in_dim(keys, kv_first * HD, kv_here * HD, 1)
    value_cols = lax.dynamic_slice_in_dim(values, kv_first * HD, kv_here * HD, 1)
    scale = 1.0 / math.sqrt(HD)
    first_rows = queries[:half_rows]
    second_rows = queries[half_rows:]
    first_start = ctx_index * tok_rows
    second_start = ctx_index * tok_rows + half_rows
    query_sets = (
        first_rows.reshape(half_rows, kv_here, heads_per_kv, HD),
        second_rows.reshape(half_rows, kv_here, heads_per_kv, HD),
    )
    query_positions = (
        first_start + jnp.arange(half_rows, dtype=jnp.int32),
        second_start + jnp.arange(half_rows, dtype=jnp.int32),
    )
    last_positions = (first_start + half_rows - 1, second_start + half_rows - 1)

    def block_update(carry, query_four, query_pos, key_block, value_block, key_start):
        run_max, run_sum, run_acc = carry
        width = key_block.shape[0]
        key_three = key_block.reshape(width, kv_here, HD)
        value_three = value_block.reshape(width, kv_here, HD)
        scores = (
            jnp.einsum("tghd,kgd->ghtk", query_four, key_three, preferred_element_type=jnp.float32)
            * scale
        )
        key_pos = key_start + jnp.arange(width, dtype=jnp.int32)
        allowed = key_pos[None, :] <= query_pos[:, None]
        scores = jnp.where(allowed, scores, -1e30)
        new_max = jnp.maximum(run_max, jnp.max(scores, axis=-1))
        probs = jnp.where(allowed, jnp.exp(scores - new_max[..., None]), 0.0)
        factor = jnp.exp(run_max - new_max)
        run_sum = run_sum * factor + jnp.sum(probs, axis=-1)
        weighted = jnp.einsum(
            "ghtk,kgd->ghtd",
            probs.astype(jnp.bfloat16),
            value_three,
            preferred_element_type=jnp.float32,
        )
        run_acc = run_acc * factor[..., None] + weighted
        return (new_max, run_sum, run_acc)

    start_max = jnp.full((kv_here, heads_per_kv, half_rows), -1e30, jnp.float32)
    start_sum = jnp.zeros((kv_here, heads_per_kv, half_rows), jnp.float32)
    start_acc = jnp.zeros((kv_here, heads_per_kv, half_rows, HD), jnp.float32)
    start_state = (start_max, start_sum, start_acc)
    key_piece = lax.all_gather(key_cols, "ctx", axis=0, tiled=True)
    value_piece = lax.all_gather(value_cols, "ctx", axis=0, tiled=True)
    count = key_piece.shape[0]
    width = 512

    def one_block(index, inner):
        key_start = index * width
        key_block = lax.dynamic_slice_in_dim(key_piece, key_start, width, 0)
        value_block = lax.dynamic_slice_in_dim(value_piece, key_start, width, 0)
        updated = []
        for which in range(2):
            query_four = query_sets[which]
            query_pos = query_positions[which]
            updated.append(
                lax.cond(
                    key_start > last_positions[which],
                    lambda state: state,
                    lambda state: block_update(
                        state, query_four, query_pos, key_block, value_block, key_start
                    ),
                    inner[which],
                )
            )
        return (updated[0], updated[1])

    states = lax.fori_loop(0, count // width, one_block, (start_state, start_state))
    halves = []
    for which in range(2):
        run_max, run_sum, run_acc = states[which]
        halves.append(
            jnp.transpose(run_acc / run_sum[..., None], (2, 0, 1, 3))
            .reshape(half_rows, heads_here * HD)
            .astype(jnp.bfloat16)
        )
    attn_second = halves[1]
    attn = jnp.concatenate([halves[0], attn_second], axis=0)
    projected = lax.psum_scatter(
        jnp.dot(attn, w_out, preferred_element_type=jnp.float32).astype(jnp.bfloat16),
        "exp",
        scatter_dimension=0,
        tiled=True,
    ).astype(jnp.float32)
    hidden_state = (residual.astype(jnp.float32) + projected).astype(jnp.bfloat16)
    state_f = hidden_state.astype(jnp.float32)
    inv_rms = 1.0 / jnp.sqrt(jnp.mean(state_f * state_f, axis=1, keepdims=True) + 1e-06)
    normed = (state_f * inv_rms * norm_gain.astype(jnp.float32)[None, :]).astype(jnp.bfloat16)
    rows_here = expert_ids.shape[0]
    top_count = expert_ids.shape[1]
    experts_all = w_gate.shape[0] * exp_count
    capacity = min(rows_here, 2 * rows_here * top_count // experts_all)
    flat_ids = expert_ids.reshape(-1)
    onehot = (flat_ids[:, None] == jnp.arange(experts_all, dtype=jnp.int32)[None, :]).astype(
        jnp.int32
    )
    earlier = jnp.cumsum(onehot, axis=0) - onehot
    slot_index = jnp.sum(earlier * onehot, axis=1)
    target = flat_ids * capacity + slot_index
    picks = target[:, None] == jnp.arange(experts_all * capacity, dtype=jnp.int32)[None, :]
    dispatch_table = jnp.any(
        picks.reshape(rows_here, top_count, experts_all * capacity), axis=1
    ).astype(jnp.bfloat16)
    outgoing = jnp.einsum(
        "rs,rd->sd", dispatch_table, normed, preferred_element_type=jnp.float32
    ).astype(jnp.bfloat16)
    arrived = lax.all_to_all(
        outgoing.reshape(experts_all, capacity, D), "exp", split_axis=0, concat_axis=0, tiled=True
    )
    slot_rows = arrived.reshape(experts_all * capacity, D)
    gate_local = w_gate[0]
    up_local = w_up[0]
    gate_pre = jnp.dot(
        slot_rows,
        lax.all_gather(gate_local, "ctx", axis=0, tiled=True),
        preferred_element_type=jnp.float32,
    )
    up_pre = jnp.dot(
        slot_rows,
        lax.all_gather(up_local, "ctx", axis=0, tiled=True),
        preferred_element_type=jnp.float32,
    )
    expert_hidden = (jax.nn.silu(gate_pre) * up_pre).astype(jnp.bfloat16)
    down_local = w_down[0]
    expert_result = jnp.dot(
        expert_hidden,
        lax.all_gather(down_local, "ctx", axis=1, tiled=True),
        preferred_element_type=jnp.float32,
    ).astype(jnp.bfloat16)
    returned = lax.all_to_all(
        expert_result.reshape(experts_all, capacity, D),
        "exp",
        split_axis=0,
        concat_axis=0,
        tiled=True,
    )
    returned_flat = returned.reshape(experts_all * capacity, D)
    picked = jnp.dot(picks.astype(jnp.bfloat16), returned_flat, preferred_element_type=jnp.float32)
    weighted = gate_weights[:, :, None] * picked.reshape(rows_here, top_count, D)
    return (state_f + jnp.sum(weighted, axis=1)).astype(jnp.bfloat16)


BF16 = jnp.bfloat16
F32 = jnp.float32
VMEM = pltpu.VMEM
QB = 256
CHEAP = pl.CostEstimate(flops=1000, bytes_accessed=1000, transcendentals=0)


def swap(array, axis, mask):
    size = lax.axis_size(axis)
    return lax.ppermute(array, axis, [(i, i ^ mask) for i in range(size)])


def params(mib):
    return pltpu.CompilerParams(vmem_limit_bytes=mib * 1024 * 1024)


def vmem_specs(count):
    return [pl.BlockSpec(memory_space=VMEM) for _ in range(count)]


def attention_kernel(index, q_hbm, *refs):
    arrived, w_hbm, outs = refs[:8], refs[8], refs[9:13]
    w_all, q, pieces, keys, ones_values, bias, even, odd, attn, q_sem, piece_sems, sems = refs[13:]
    q_fetch = pltpu.make_async_copy(q_hbm, q, q_sem)
    piece_fetches = [
        pltpu.make_async_copy(arrived[i], pieces.at[i], piece_sems.at[i]) for i in range(8)
    ]
    for fetch in piece_fetches + [q_fetch]:
        fetch.start()
    ctx = index[0]
    exp = index[1]
    chip = ctx // 2
    steps = sems.shape[0]
    depth = w_all.shape[0] // steps
    fetches = [
        pltpu.make_async_copy(
            w_hbm.at[pl.ds(i * depth, depth)], w_all.at[pl.ds(i * depth, depth)], sems.at[i]
        )
        for i in range(steps)
    ]
    factor = math.log2(math.e) / math.sqrt(HD)
    heads = q.shape[1] // HD
    ones_values[:, HD:] = jnp.ones((ones_values.shape[0], HD), BF16)
    core = ctx % 2
    row = lax.broadcasted_iota(jnp.int32, (QB, 2 * QB), 0) + core * QB
    col = lax.broadcasted_iota(jnp.int32, (QB, 2 * QB), 1)
    bias[...] = jnp.where(col <= row, 0.0, -1e30)
    for fetch in piece_fetches:
        fetch.wait()
    for d in range(4):

        @pl.when(chip >= d)
        def _():
            for other in range(2):
                piece = pieces.at[2 * d + other]
                place = 2 * (chip - d) + (core ^ other)
                here = pl.ds(pl.multiple_of(place * QB, QB), QB)
                keys[:, here] = piece[:, :HD].astype(F32).T.astype(BF16)
                ones_values[here, :HD] = piece[:, HD:]

    q_fetch.wait()
    for fetch in fetches:
        fetch.start()
    part = QB // 4

    def run(length):
        def scores_of(h, store):
            rows = q[:, pl.ds(pl.multiple_of(h * HD, HD), HD)]
            block = jnp.dot(rows, keys[:, :length], preferred_element_type=F32)
            last = length - 2 * QB
            if last:
                store[:, :last] = block[:, :last]
            store[:, last:length] = block[:, last:] + bias[...]

        def finish(h, store):
            block = store[:, :length]
            top = jnp.max(block, axis=1, keepdims=True) * factor
            probs = jnp.exp2(block * factor - top).astype(BF16)
            total = jnp.dot(probs, ones_values[:length, :], preferred_element_type=F32)
            done = (total[:, :HD] / total[:, HD:]).astype(BF16)
            cols = pl.ds(pl.multiple_of(h * HD, HD), HD)
            for i in range(4):
                start = pl.multiple_of((exp ^ i) * part, part)
                attn[pl.ds(start, part), cols] = done[i * part : (i + 1) * part]

        scores_of(0, even)

        @pl.loop(0, heads // 2)
        def _(pair):
            scores_of(2 * pair + 1, odd)
            finish(2 * pair, even)
            scores_of(jnp.minimum(2 * pair + 2, heads - 1), even)
            finish(2 * pair + 1, odd)

    for z in range(4):
        pl.when(chip == z)(functools.partial(run, (z + 1) * 2 * QB))

    for fetch in fetches:
        fetch.wait()
    width = 512
    for n in range(w_all.shape[1] // width):
        cols = slice(n * width, (n + 1) * width)
        block = jnp.dot(attn[...], w_all[:, cols], preferred_element_type=F32).astype(BF16)
        for b, out in enumerate(outs):
            out[:, cols] = block[b * part : (b + 1) * part]


def attention(index, queries, pieces, w_out):
    rows = QB // 4
    length = 8 * QB
    return pl.pallas_call(
        attention_kernel,
        out_shape=[jax.ShapeDtypeStruct((rows, D), BF16)] * 4,
        in_specs=[pl.BlockSpec(memory_space=pltpu.SMEM)]
        + [pl.BlockSpec(memory_space=pl.ANY)] * 10,
        out_specs=vmem_specs(4),
        scratch_shapes=[
            VMEM(w_out.shape, BF16),
            VMEM(queries.shape, BF16),
            VMEM((8,) + pieces[0].shape, BF16),
            VMEM((HD, length), BF16),
            VMEM((length, 2 * HD), BF16),
            VMEM((QB, 2 * QB), F32),
            VMEM((QB, length), F32),
            VMEM((QB, length), F32),
            VMEM(queries.shape, BF16),
            pltpu.SemaphoreType.DMA,
            pltpu.SemaphoreType.DMA((8,)),
            pltpu.SemaphoreType.DMA((16,)),
        ],
        compiler_params=params(52),
        cost_estimate=CHEAP,
        name="attention",
    )(index, queries, *pieces, w_out)


def norm_kernel(index, p0, r1, r2, r3, residual, gain, state, mine, theirs, work):
    ctx = index[0]
    total = p0[...].astype(F32) + r1[...].astype(F32) + r2[...].astype(F32) + r3[...].astype(F32)
    hidden = (residual[...].astype(F32) + total).astype(BF16)
    state[...] = hidden
    wide = hidden.astype(F32)
    inv = 1.0 / jnp.sqrt(jnp.mean(wide * wide, axis=1, keepdims=True) + 1e-06)
    normed = (wide * inv * gain[...].astype(F32)).astype(BF16)
    part = D // 8
    for j in range(8):
        work[j] = normed[:, j * part : (j + 1) * part]
    for j, (a, b) in enumerate(((0, 2), (1, 3), (6, 4), (7, 5))):
        mine[:, j * part : (j + 1) * part] = work[ctx ^ a]
        theirs[:, j * part : (j + 1) * part] = work[ctx ^ b]


def norm(index, p0, r1, r2, r3, residual, gain):
    rows = residual.shape[0]
    half = jax.ShapeDtypeStruct((rows, D // 2), BF16)
    return pl.pallas_call(
        norm_kernel,
        out_shape=[jax.ShapeDtypeStruct((rows, D), BF16), half, half],
        in_specs=[pl.BlockSpec(memory_space=pltpu.SMEM)] + vmem_specs(6),
        out_specs=vmem_specs(3),
        scratch_shapes=[VMEM((8, rows, D // 8), BF16)],
        compiler_params=params(16),
        cost_estimate=CHEAP,
        name="norm",
    )(index, p0, r1, r2, r3, residual, gain)


def enter_kernel(*refs):
    rows, weights, (out, gate_all, up_all, sems) = refs[:-8], refs[-8:-4], refs[-4:]
    part, width = weights[0].shape[0] // 2, weights[0].shape[1]
    fetches = []
    for which, whole in enumerate((gate_all, up_all)):
        for j, array in enumerate(weights):
            source = array.at[pl.ds(which * part, part)]
            target = whole.at[pl.ds(j * part, part)]
            fetches.append(pltpu.make_async_copy(source, target, sems.at[4 * which + j]))
            fetches[-1].start()
    x = jnp.concatenate([block[...] for block in rows], axis=0)
    tile = 256
    for which, whole in enumerate((gate_all, up_all)):
        for fetch in fetches[4 * which : 4 * which + 4]:
            fetch.wait()
        for n in range(width // tile):
            cols = slice(which * width + n * tile, which * width + (n + 1) * tile)
            block = jnp.dot(x, whole[:, n * tile : (n + 1) * tile], preferred_element_type=F32)
            out[:, cols] = block.astype(out.dtype)


def enter(rows, weights, kind):
    count = len(rows) * rows[0].shape[0]
    part, width = weights[0].shape[0] // 2, weights[0].shape[1]
    return pl.pallas_call(
        enter_kernel,
        out_shape=jax.ShapeDtypeStruct((count, 2 * width), kind),
        in_specs=vmem_specs(len(rows)) + [pl.BlockSpec(memory_space=pl.ANY)] * 4,
        out_specs=pl.BlockSpec(memory_space=VMEM),
        scratch_shapes=[
            VMEM((4 * part, width), BF16),
            VMEM((4 * part, width), BF16),
            pltpu.SemaphoreType.DMA((8,)),
        ],
        compiler_params=params(24),
        cost_estimate=CHEAP,
        name="enter",
    )(*rows, *weights)


def silu_kernel(half, own, other, out):
    count, width = out.shape
    total = own[half * count : (half + 1) * count] + other[...].astype(F32)
    gate, up = total[:, :width], total[:, width:]
    out[...] = (gate / (1.0 + jnp.exp(-gate)) * up).astype(BF16)


def silu(own, other, half):
    count, width = other.shape
    return pl.pallas_call(
        functools.partial(silu_kernel, half),
        out_shape=jax.ShapeDtypeStruct((count, width // 2), BF16),
        in_specs=vmem_specs(2),
        out_specs=pl.BlockSpec(memory_space=VMEM),
        compiler_params=params(16),
        cost_estimate=CHEAP,
        name="silu",
    )(own, other)


def leave_kernel(*refs):
    count = (len(refs) - 6) // 3
    hiddens, arrays, outs, (down_all, sems) = refs[:count], refs[count : count + 4], refs[count + 4 : -2], refs[-2:]
    part = outs[0].shape[0]
    width = arrays[0].shape[1]
    fetches = []
    for j, array in enumerate(arrays):
        fetches.append(pltpu.make_async_copy(array, down_all.at[j], sems.at[j]))
        fetches[-1].start()
    hidden = jnp.concatenate([block[...] for block in hiddens], axis=0)
    for j in range(4):
        fetches[j].wait()
        block = jnp.dot(hidden, down_all[j], preferred_element_type=F32).astype(BF16)
        for b, out in enumerate(outs):
            out[:, j * width : (j + 1) * width] = block[b * part : (b + 1) * part]


def leave(hiddens, downs):
    part = jax.ShapeDtypeStruct((hiddens[0].shape[0] // 2, 4 * downs[0].shape[1]), BF16)
    return pl.pallas_call(
        leave_kernel,
        out_shape=[part] * (2 * len(hiddens)),
        in_specs=vmem_specs(len(hiddens)) + [pl.BlockSpec(memory_space=pl.ANY)] * 4,
        out_specs=vmem_specs(2 * len(hiddens)),
        scratch_shapes=[VMEM((4,) + downs[0].shape, BF16), pltpu.SemaphoreType.DMA((4,))],
        compiler_params=params(24),
        cost_estimate=CHEAP,
        name="leave",
    )(*hiddens, *downs)


def mixed(shares, parts):
    total = shares[:, :1] * parts[0][...].astype(F32)
    for b in range(1, 4):
        total = total + shares[:, b : b + 1] * parts[b][...].astype(F32)
    return total


def final_kernel(index, state, shares, y0, r1, r2, r3, other, out):
    ctx = index[0]
    part = D // 8
    own = mixed(shares, (y0, r1, r2, r3))
    for j, (a, b) in enumerate(((0, 2), (1, 3), (6, 4), (7, 5))):
        cols = slice(j * part, (j + 1) * part)
        here = pl.ds(pl.multiple_of((ctx ^ a) * part, part), part)
        out[:, here] = (state[:, here].astype(F32) + own[:, cols]).astype(BF16)
        there = pl.ds(pl.multiple_of((ctx ^ b) * part, part), part)
        out[:, there] = (state[:, there].astype(F32) + other[:, cols].astype(F32)).astype(BF16)


def final(index, state, shares, y0, r1, r2, r3, other):
    return pl.pallas_call(
        final_kernel,
        out_shape=jax.ShapeDtypeStruct(state.shape, BF16),
        in_specs=[pl.BlockSpec(memory_space=pltpu.SMEM)] + vmem_specs(7),
        out_specs=pl.BlockSpec(memory_space=VMEM),
        compiler_params=params(16),
        cost_estimate=CHEAP,
        name="final",
    )(index, state, shares, y0, r1, r2, r3, other)


def body(
    queries,
    keys,
    values,
    w_out,
    residual,
    norm_gain,
    expert_ids,
    gate_weights,
    w_gate,
    w_up,
    w_down,
):
    exp = lax.axis_index("exp")
    ctx = lax.axis_index("ctx")
    index = jnp.stack([ctx, exp]).astype(jnp.int32)
    kv_first = exp * (HQ // 4) // (HQ // KVH) * HD
    kv_here = jnp.concatenate(
        [
            lax.dynamic_slice_in_dim(keys, kv_first, HD, 1),
            lax.dynamic_slice_in_dim(values, kv_first, HD, 1),
        ],
        axis=1,
    )
    def later(array, chips):
        return lax.ppermute(array, "ctx", [(i, i + 2 * chips) for i in range(8 - 2 * chips)])

    kv_here, gate_here, up_here = lax.optimization_barrier((kv_here, w_gate[0], w_up[0]))
    moved = [later(kv_here, d) for d in (3, 2, 1)][::-1]
    pair_here, down_here = jnp.concatenate([gate_here, up_here], axis=0), w_down[0]
    moved[0], pair_here, down_here = lax.optimization_barrier((moved[0], pair_here, down_here))
    pieces = [part for piece in [kv_here] + moved for part in (piece, swap(piece, "ctx", 1))]
    pair_near, down_near = swap(pair_here, "ctx", 1), swap(down_here, "ctx", 1)
    pieces, pair_here, pair_near, down_near = lax.optimization_barrier(
        (pieces, pair_here, pair_near, down_near)
    )
    pair_far = swap(pair_here, "ctx", 6)

    lane = lax.broadcasted_iota(jnp.int32, (expert_ids.shape[0], HD), 1)
    shares = jnp.zeros(lane.shape, F32)
    for k in range(expert_ids.shape[1]):
        named = expert_ids[:, k : k + 1] ^ exp
        shares = shares + jnp.where(lane == named, gate_weights[:, k : k + 1], 0.0)

    p = attention(index, queries, pieces, w_out)
    p, shares = lax.optimization_barrier((p, shares))
    r = [swap(p[b], "exp", b) for b in (1, 2, 3)]
    other_shares = swap(shares, "ctx", 2)
    r, other_shares = lax.optimization_barrier((r, other_shares))
    state, mine, theirs = norm(index, p[0], *r, residual, norm_gain.reshape(1, D))
    others = swap(theirs, "ctx", 2)
    own_rows = [mine] + [swap(mine, "exp", b) for b in (1, 2, 3)]
    other_rows = [others] + [swap(others, "exp", b) for b in (1, 2, 3)]
    own_rows, other_rows[1:3], pair_far, down_here = lax.optimization_barrier(
        (own_rows, other_rows[1:3], pair_far, down_here)
    )
    down_far = swap(down_here, "ctx", 6)
    pairs = (pair_here, pair_near, pair_far, swap(pair_far, "ctx", 1))
    own_pre = enter(own_rows, pairs, F32)
    other_rows[:2], own_pre = lax.optimization_barrier((other_rows[:2], own_pre))
    first_pre = enter(other_rows[:2], pairs, BF16)
    first_pre, other_rows[2:] = lax.optimization_barrier((first_pre, other_rows[2:]))
    first_sum = swap(first_pre, "ctx", 2)
    last_sum = swap(enter(other_rows[2:], pairs, BF16), "ctx", 2)
    first = silu(own_pre, first_sum, 0)
    other_first = swap(first, "ctx", 2)
    last_sum, other_first, down_far = lax.optimization_barrier((last_sum, other_first, down_far))
    last = silu(own_pre, last_sum, 1)
    other_last = swap(last, "ctx", 2)
    downs = (down_here, down_near, down_far, swap(down_far, "ctx", 1))
    y = leave([first, last, other_first, other_last], downs)
    own_parts = [y[0]] + [swap(y[b], "exp", b) for b in (1, 2, 3)]
    other_parts = [y[4]] + [swap(y[4 + b], "exp", b) for b in (1, 2, 3)]
    back = swap(mixed(other_shares, other_parts).astype(BF16), "ctx", 2)
    return final(index, state, shares, *own_parts, back)


def solution(mesh):
    placed = (
        P("ctx", "exp"),
        P("ctx", None),
        P("ctx", None),
        P("exp", None),
        P(("ctx", "exp"), None),
        P(),
        P(("ctx", "exp"), None),
        P(("ctx", "exp"), None),
        P("exp", "ctx", None),
        P("exp", "ctx", None),
        P("exp", None, "ctx"),
    )
    shape = dict(mesh.shape)
    small = shape["ctx"] == 8 and shape["exp"] == 4
    return jax.shard_map(
        body if small else general_body, mesh=mesh, in_specs=placed, out_specs=P(("ctx", "exp"), None), check_vma=False
    )
```

```python
import functools
import math

import jax
import jax.numpy as jnp
from jax import lax
from jax.experimental import pallas as pl
from jax.experimental.pallas import tpu as pltpu
from jax.sharding import PartitionSpec as P

D = 4096
HQ = 64
KVH = 4
HD = 128


def general_body(
    queries,
    keys,
    values,
    w_out,
    residual,
    norm_gain,
    expert_ids,
    gate_weights,
    w_gate,
    w_up,
    w_down,
):
    tok_rows = queries.shape[0]
    half_rows = tok_rows // 2
    exp_count = lax.axis_size("exp")
    heads_here = HQ // exp_count
    group = HQ // KVH
    kv_here = max(1, heads_here // group)
    heads_per_kv = heads_here // kv_here
    exp_index = lax.axis_index("exp")
    ctx_index = lax.axis_index("ctx")
    kv_first = exp_index * heads_here // group
    key_cols = lax.dynamic_slice_in_dim(keys, kv_first * HD, kv_here * HD, 1)
    value_cols = lax.dynamic_slice_in_dim(values, kv_first * HD, kv_here * HD, 1)
    scale = 1.0 / math.sqrt(HD)
    first_rows = queries[:half_rows]
    second_rows = queries[half_rows:]
    first_start = ctx_index * tok_rows
    second_start = ctx_index * tok_rows + half_rows
    query_sets = (
        first_rows.reshape(half_rows, kv_here, heads_per_kv, HD),
        second_rows.reshape(half_rows, kv_here, heads_per_kv, HD),
    )
    query_positions = (
        first_start + jnp.arange(half_rows, dtype=jnp.int32),
        second_start + jnp.arange(half_rows, dtype=jnp.int32),
    )
    last_positions = (first_start + half_rows - 1, second_start + half_rows - 1)

    def block_update(carry, query_four, query_pos, key_block, value_block, key_start):
        run_max, run_sum, run_acc = carry
        width = key_block.shape[0]
        key_three = key_block.reshape(width, kv_here, HD)
        value_three = value_block.reshape(width, kv_here, HD)
        scores = (
            jnp.einsum("tghd,kgd->ghtk", query_four, key_three, preferred_element_type=jnp.float32)
            * scale
        )
        key_pos = key_start + jnp.arange(width, dtype=jnp.int32)
        allowed = key_pos[None, :] <= query_pos[:, None]
        scores = jnp.where(allowed, scores, -1e30)
        new_max = jnp.maximum(run_max, jnp.max(scores, axis=-1))
        probs = jnp.where(allowed, jnp.exp(scores - new_max[..., None]), 0.0)
        factor = jnp.exp(run_max - new_max)
        run_sum = run_sum * factor + jnp.sum(probs, axis=-1)
        weighted = jnp.einsum(
            "ghtk,kgd->ghtd",
            probs.astype(jnp.bfloat16),
            value_three,
            preferred_element_type=jnp.float32,
        )
        run_acc = run_acc * factor[..., None] + weighted
        return (new_max, run_sum, run_acc)

    start_max = jnp.full((kv_here, heads_per_kv, half_rows), -1e30, jnp.float32)
    start_sum = jnp.zeros((kv_here, heads_per_kv, half_rows), jnp.float32)
    start_acc = jnp.zeros((kv_here, heads_per_kv, half_rows, HD), jnp.float32)
    start_state = (start_max, start_sum, start_acc)
    key_piece = lax.all_gather(key_cols, "ctx", axis=0, tiled=True)
    value_piece = lax.all_gather(value_cols, "ctx", axis=0, tiled=True)
    count = key_piece.shape[0]
    width = 512

    def one_block(index, inner):
        key_start = index * width
        key_block = lax.dynamic_slice_in_dim(key_piece, key_start, width, 0)
        value_block = lax.dynamic_slice_in_dim(value_piece, key_start, width, 0)
        updated = []
        for which in range(2):
            query_four = query_sets[which]
            query_pos = query_positions[which]
            updated.append(
                lax.cond(
                    key_start > last_positions[which],
                    lambda state: state,
                    lambda state: block_update(
                        state, query_four, query_pos, key_block, value_block, key_start
                    ),
                    inner[which],
                )
            )
        return (updated[0], updated[1])

    states = lax.fori_loop(0, count // width, one_block, (start_state, start_state))
    halves = []
    for which in range(2):
        run_max, run_sum, run_acc = states[which]
        halves.append(
            jnp.transpose(run_acc / run_sum[..., None], (2, 0, 1, 3))
            .reshape(half_rows, heads_here * HD)
            .astype(jnp.bfloat16)
        )
    attn_second = halves[1]
    attn = jnp.concatenate([halves[0], attn_second], axis=0)
    projected = lax.psum_scatter(
        jnp.dot(attn, w_out, preferred_element_type=jnp.float32).astype(jnp.bfloat16),
        "exp",
        scatter_dimension=0,
        tiled=True,
    ).astype(jnp.float32)
    hidden_state = (residual.astype(jnp.float32) + projected).astype(jnp.bfloat16)
    state_f = hidden_state.astype(jnp.float32)
    inv_rms = 1.0 / jnp.sqrt(jnp.mean(state_f * state_f, axis=1, keepdims=True) + 1e-06)
    normed = (state_f * inv_rms * norm_gain.astype(jnp.float32)[None, :]).astype(jnp.bfloat16)
    rows_here = expert_ids.shape[0]
    top_count = expert_ids.shape[1]
    experts_all = w_gate.shape[0] * exp_count
    capacity = min(rows_here, 2 * rows_here * top_count // experts_all)
    flat_ids = expert_ids.reshape(-1)
    onehot = (flat_ids[:, None] == jnp.arange(experts_all, dtype=jnp.int32)[None, :]).astype(
        jnp.int32
    )
    earlier = jnp.cumsum(onehot, axis=0) - onehot
    slot_index = jnp.sum(earlier * onehot, axis=1)
    target = flat_ids * capacity + slot_index
    picks = target[:, None] == jnp.arange(experts_all * capacity, dtype=jnp.int32)[None, :]
    dispatch_table = jnp.any(
        picks.reshape(rows_here, top_count, experts_all * capacity), axis=1
    ).astype(jnp.bfloat16)
    outgoing = jnp.einsum(
        "rs,rd->sd", dispatch_table, normed, preferred_element_type=jnp.float32
    ).astype(jnp.bfloat16)
    arrived = lax.all_to_all(
        outgoing.reshape(experts_all, capacity, D), "exp", split_axis=0, concat_axis=0, tiled=True
    )
    slot_rows = arrived.reshape(experts_all * capacity, D)
    gate_local = w_gate[0]
    up_local = w_up[0]
    gate_pre = jnp.dot(
        slot_rows,
        lax.all_gather(gate_local, "ctx", axis=0, tiled=True),
        preferred_element_type=jnp.float32,
    )
    up_pre = jnp.dot(
        slot_rows,
        lax.all_gather(up_local, "ctx", axis=0, tiled=True),
        preferred_element_type=jnp.float32,
    )
    expert_hidden = (jax.nn.silu(gate_pre) * up_pre).astype(jnp.bfloat16)
    down_local = w_down[0]
    expert_result = jnp.dot(
        expert_hidden,
        lax.all_gather(down_local, "ctx", axis=1, tiled=True),
        preferred_element_type=jnp.float32,
    ).astype(jnp.bfloat16)
    returned = lax.all_to_all(
        expert_result.reshape(experts_all, capacity, D),
        "exp",
        split_axis=0,
        concat_axis=0,
        tiled=True,
    )
    returned_flat = returned.reshape(experts_all * capacity, D)
    picked = jnp.dot(picks.astype(jnp.bfloat16), returned_flat, preferred_element_type=jnp.float32)
    weighted = gate_weights[:, :, None] * picked.reshape(rows_here, top_count, D)
    return (state_f + jnp.sum(weighted, axis=1)).astype(jnp.bfloat16)


BF16 = jnp.bfloat16
F32 = jnp.float32
VMEM = pltpu.VMEM
QB = 256
CHEAP = pl.CostEstimate(flops=1000, bytes_accessed=1000, transcendentals=0)


def swap(array, axis, mask):
    size = lax.axis_size(axis)
    return lax.ppermute(array, axis, [(i, i ^ mask) for i in range(size)])


def params(mib):
    return pltpu.CompilerParams(vmem_limit_bytes=mib * 1024 * 1024)


def vmem_specs(count):
    return [pl.BlockSpec(memory_space=VMEM) for _ in range(count)]


def attention_kernel(index, q_hbm, *refs):
    arrived, w_hbm, outs = refs[:8], refs[8], refs[9:13]
    w_all, q, pieces, keys, ones_values, bias, even, odd, attn, q_sem, piece_sems, sems = refs[13:]
    q_fetch = pltpu.make_async_copy(q_hbm, q, q_sem)
    piece_fetches = [
        pltpu.make_async_copy(arrived[i], pieces.at[i], piece_sems.at[i]) for i in range(8)
    ]
    for fetch in piece_fetches + [q_fetch]:
        fetch.start()
    ctx = index[0]
    exp = index[1]
    chip = ctx // 2
    steps = sems.shape[0]
    depth = w_all.shape[0] // steps
    fetches = [
        pltpu.make_async_copy(
            w_hbm.at[pl.ds(i * depth, depth)], w_all.at[pl.ds(i * depth, depth)], sems.at[i]
        )
        for i in range(steps)
    ]
    factor = math.log2(math.e) / math.sqrt(HD)
    heads = q.shape[1] // HD
    ones_values[:, HD:] = jnp.ones((ones_values.shape[0], HD), BF16)
    core = ctx % 2
    row = lax.broadcasted_iota(jnp.int32, (QB, 2 * QB), 0) + core * QB
    col = lax.broadcasted_iota(jnp.int32, (QB, 2 * QB), 1)
    bias[...] = jnp.where(col <= row, 0.0, -1e30)
    for fetch in piece_fetches:
        fetch.wait()
    for d in range(4):

        @pl.when(chip >= d)
        def _():
            for other in range(2):
                piece = pieces.at[2 * d + other]
                place = 2 * (chip - d) + (core ^ other)
                here = pl.ds(pl.multiple_of(place * QB, QB), QB)
                keys[:, here] = piece[:, :HD].astype(F32).T.astype(BF16)
                ones_values[here, :HD] = piece[:, HD:]

    q_fetch.wait()
    for fetch in fetches:
        fetch.start()
    part = QB // 4

    def run(length):
        def scores_of(h, store):
            rows = q[:, pl.ds(pl.multiple_of(h * HD, HD), HD)]
            block = jnp.dot(rows, keys[:, :length], preferred_element_type=F32)
            last = length - 2 * QB
            if last:
                store[:, :last] = block[:, :last]
            store[:, last:length] = block[:, last:] + bias[...]

        def finish(h, store):
            block = store[:, :length]
            top = jnp.max(block, axis=1, keepdims=True) * factor
            probs = jnp.exp2(block * factor - top).astype(BF16)
            total = jnp.dot(probs, ones_values[:length, :], preferred_element_type=F32)
            done = (total[:, :HD] / total[:, HD:]).astype(BF16)
            cols = pl.ds(pl.multiple_of(h * HD, HD), HD)
            for i in range(4):
                start = pl.multiple_of((exp ^ i) * part, part)
                attn[pl.ds(start, part), cols] = done[i * part : (i + 1) * part]

        scores_of(0, even)

        @pl.loop(0, heads // 2)
        def _(pair):
            scores_of(2 * pair + 1, odd)
            finish(2 * pair, even)
            scores_of(jnp.minimum(2 * pair + 2, heads - 1), even)
            finish(2 * pair + 1, odd)

    for z in range(4):
        pl.when(chip == z)(functools.partial(run, (z + 1) * 2 * QB))

    for fetch in fetches:
        fetch.wait()
    width = 512
    for n in range(w_all.shape[1] // width):
        cols = slice(n * width, (n + 1) * width)
        block = jnp.dot(attn[...], w_all[:, cols], preferred_element_type=F32).astype(BF16)
        for b, out in enumerate(outs):
            out[:, cols] = block[b * part : (b + 1) * part]


def attention(index, queries, pieces, w_out):
    rows = QB // 4
    length = 8 * QB
    return pl.pallas_call(
        attention_kernel,
        out_shape=[jax.ShapeDtypeStruct((rows, D), BF16)] * 4,
        in_specs=[pl.BlockSpec(memory_space=pltpu.SMEM)]
        + [pl.BlockSpec(memory_space=pl.ANY)] * 10,
        out_specs=vmem_specs(4),
        scratch_shapes=[
            VMEM(w_out.shape, BF16),
            VMEM(queries.shape, BF16),
            VMEM((8,) + pieces[0].shape, BF16),
            VMEM((HD, length), BF16),
            VMEM((length, 2 * HD), BF16),
            VMEM((QB, 2 * QB), F32),
            VMEM((QB, length), F32),
            VMEM((QB, length), F32),
            VMEM(queries.shape, BF16),
            pltpu.SemaphoreType.DMA,
            pltpu.SemaphoreType.DMA((8,)),
            pltpu.SemaphoreType.DMA((16,)),
        ],
        compiler_params=params(52),
        cost_estimate=CHEAP,
        name="attention",
    )(index, queries, *pieces, w_out)


def norm_kernel(index, p0, r1, r2, r3, residual, gain, state, mine, theirs, work):
    ctx = index[0]
    total = p0[...].astype(F32) + r1[...].astype(F32) + r2[...].astype(F32) + r3[...].astype(F32)
    hidden = (residual[...].astype(F32) + total).astype(BF16)
    state[...] = hidden
    wide = hidden.astype(F32)
    inv = 1.0 / jnp.sqrt(jnp.mean(wide * wide, axis=1, keepdims=True) + 1e-06)
    normed = (wide * inv * gain[...].astype(F32)).astype(BF16)
    part = D // 8
    for j in range(8):
        work[j] = normed[:, j * part : (j + 1) * part]
    for j, (a, b) in enumerate(((0, 2), (1, 3), (6, 4), (7, 5))):
        mine[:, j * part : (j + 1) * part] = work[ctx ^ a]
        theirs[:, j * part : (j + 1) * part] = work[ctx ^ b]


def norm(index, p0, r1, r2, r3, residual, gain):
    rows = residual.shape[0]
    half = jax.ShapeDtypeStruct((rows, D // 2), BF16)
    return pl.pallas_call(
        norm_kernel,
        out_shape=[jax.ShapeDtypeStruct((rows, D), BF16), half, half],
        in_specs=[pl.BlockSpec(memory_space=pltpu.SMEM)] + vmem_specs(6),
        out_specs=vmem_specs(3),
        scratch_shapes=[VMEM((8, rows, D // 8), BF16)],
        compiler_params=params(16),
        cost_estimate=CHEAP,
        name="norm",
    )(index, p0, r1, r2, r3, residual, gain)


def enter_kernel(*refs):
    rows, weights, (out, gate_all, up_all, sems) = refs[:-8], refs[-8:-4], refs[-4:]
    part, width = weights[0].shape[0] // 2, weights[0].shape[1]
    fetches = []
    for which, whole in enumerate((gate_all, up_all)):
        for j, array in enumerate(weights):
            source = array.at[pl.ds(which * part, part)]
            target = whole.at[pl.ds(j * part, part)]
            fetches.append(pltpu.make_async_copy(source, target, sems.at[4 * which + j]))
            fetches[-1].start()
    x = jnp.concatenate([block[...] for block in rows], axis=0)
    tile = 256
    for which, whole in enumerate((gate_all, up_all)):
        for fetch in fetches[4 * which : 4 * which + 4]:
            fetch.wait()
        for n in range(width // tile):
            cols = slice(which * width + n * tile, which * width + (n + 1) * tile)
            block = jnp.dot(x, whole[:, n * tile : (n + 1) * tile], preferred_element_type=F32)
            out[:, cols] = block.astype(out.dtype)


def enter(rows, weights, kind):
    count = len(rows) * rows[0].shape[0]
    part, width = weights[0].shape[0] // 2, weights[0].shape[1]
    return pl.pallas_call(
        enter_kernel,
        out_shape=jax.ShapeDtypeStruct((count, 2 * width), kind),
        in_specs=vmem_specs(len(rows)) + [pl.BlockSpec(memory_space=pl.ANY)] * 4,
        out_specs=pl.BlockSpec(memory_space=VMEM),
        scratch_shapes=[
            VMEM((4 * part, width), BF16),
            VMEM((4 * part, width), BF16),
            pltpu.SemaphoreType.DMA((8,)),
        ],
        compiler_params=params(24),
        cost_estimate=CHEAP,
        name="enter",
    )(*rows, *weights)


def silu_kernel(half, own, other, out):
    count, width = out.shape
    total = own[half * count : (half + 1) * count] + other[...].astype(F32)
    gate, up = total[:, :width], total[:, width:]
    out[...] = (gate / (1.0 + jnp.exp(-gate)) * up).astype(BF16)


def silu(own, other, half):
    count, width = other.shape
    return pl.pallas_call(
        functools.partial(silu_kernel, half),
        out_shape=jax.ShapeDtypeStruct((count, width // 2), BF16),
        in_specs=vmem_specs(2),
        out_specs=pl.BlockSpec(memory_space=VMEM),
        compiler_params=params(16),
        cost_estimate=CHEAP,
        name="silu",
    )(own, other)


def leave_kernel(*refs):
    count = (len(refs) - 6) // 3
    hiddens, arrays, outs, (down_all, sems) = refs[:count], refs[count : count + 4], refs[count + 4 : -2], refs[-2:]
    part = outs[0].shape[0]
    width = arrays[0].shape[1]
    fetches = []
    for j, array in enumerate(arrays):
        fetches.append(pltpu.make_async_copy(array, down_all.at[j], sems.at[j]))
        fetches[-1].start()
    hidden = jnp.concatenate([block[...] for block in hiddens], axis=0)
    for j in range(4):
        fetches[j].wait()
        block = jnp.dot(hidden, down_all[j], preferred_element_type=F32).astype(BF16)
        for b, out in enumerate(outs):
            out[:, j * width : (j + 1) * width] = block[b * part : (b + 1) * part]


def leave(hiddens, downs):
    part = jax.ShapeDtypeStruct((hiddens[0].shape[0] // 2, 4 * downs[0].shape[1]), BF16)
    return pl.pallas_call(
        leave_kernel,
        out_shape=[part] * (2 * len(hiddens)),
        in_specs=vmem_specs(len(hiddens)) + [pl.BlockSpec(memory_space=pl.ANY)] * 4,
        out_specs=vmem_specs(2 * len(hiddens)),
        scratch_shapes=[VMEM((4,) + downs[0].shape, BF16), pltpu.SemaphoreType.DMA((4,))],
        compiler_params=params(24),
        cost_estimate=CHEAP,
        name="leave",
    )(*hiddens, *downs)


def mixed(shares, parts):
    total = shares[:, :1] * parts[0][...].astype(F32)
    for b in range(1, 4):
        total = total + shares[:, b : b + 1] * parts[b][...].astype(F32)
    return total


def final_kernel(index, state, shares, y0, r1, r2, r3, other, out):
    ctx = index[0]
    part = D // 8
    own = mixed(shares, (y0, r1, r2, r3))
    for j, (a, b) in enumerate(((0, 2), (1, 3), (6, 4), (7, 5))):
        cols = slice(j * part, (j + 1) * part)
        here = pl.ds(pl.multiple_of((ctx ^ a) * part, part), part)
        out[:, here] = (state[:, here].astype(F32) + own[:, cols]).astype(BF16)
        there = pl.ds(pl.multiple_of((ctx ^ b) * part, part), part)
        out[:, there] = (state[:, there].astype(F32) + other[:, cols].astype(F32)).astype(BF16)


def final(index, state, shares, y0, r1, r2, r3, other):
    return pl.pallas_call(
        final_kernel,
        out_shape=jax.ShapeDtypeStruct(state.shape, BF16),
        in_specs=[pl.BlockSpec(memory_space=pltpu.SMEM)] + vmem_specs(7),
        out_specs=pl.BlockSpec(memory_space=VMEM),
        compiler_params=params(16),
        cost_estimate=CHEAP,
        name="final",
    )(index, state, shares, y0, r1, r2, r3, other)


def body(
    queries,
    keys,
    values,
    w_out,
    residual,
    norm_gain,
    expert_ids,
    gate_weights,
    w_gate,
    w_up,
    w_down,
):
    exp = lax.axis_index("exp")
    ctx = lax.axis_index("ctx")
    index = jnp.stack([ctx, exp]).astype(jnp.int32)
    kv_first = exp * (HQ // 4) // (HQ // KVH) * HD
    kv_here = jnp.concatenate(
        [
            lax.dynamic_slice_in_dim(keys, kv_first, HD, 1),
            lax.dynamic_slice_in_dim(values, kv_first, HD, 1),
        ],
        axis=1,
    )
    def later(array, chips):
        return lax.ppermute(array, "ctx", [(i, i + 2 * chips) for i in range(8 - 2 * chips)])

    kv_here, gate_here, up_here = lax.optimization_barrier((kv_here, w_gate[0], w_up[0]))
    moved = [later(kv_here, d) for d in (3, 2, 1)][::-1]
    pair_here, down_here = jnp.concatenate([gate_here, up_here], axis=0), w_down[0]
    pieces = [part for piece in [kv_here] + moved for part in (piece, swap(piece, "ctx", 1))]
    pieces, pair_here = lax.optimization_barrier((pieces, pair_here))
    pair_far = swap(pair_here, "ctx", 6)

    lane = lax.broadcasted_iota(jnp.int32, (expert_ids.shape[0], HD), 1)
    shares = jnp.zeros(lane.shape, F32)
    for k in range(expert_ids.shape[1]):
        named = expert_ids[:, k : k + 1] ^ exp
        shares = shares + jnp.where(lane == named, gate_weights[:, k : k + 1], 0.0)

    p = attention(index, queries, pieces, w_out)
    p, pair_near = lax.optimization_barrier((p, swap(pair_here, "ctx", 1)))
    r = [swap(p[b], "exp", b) for b in (1, 2, 3)]
    state, mine, theirs = norm(index, p[0], *r, residual, norm_gain.reshape(1, D))
    others = swap(theirs, "ctx", 2)
    own_rows = [mine] + [swap(mine, "exp", b) for b in (1, 2, 3)]
    others, own_rows[1:3] = lax.optimization_barrier((others, own_rows[1:3]))
    other_rows = [others] + [swap(others, "exp", b) for b in (1, 2, 3)]
    own_rows, other_rows[1:3], pair_far, down_here, shares = lax.optimization_barrier(
        (own_rows, other_rows[1:3], pair_far, down_here, shares)
    )
    down_far = swap(down_here, "ctx", 6)
    pairs = (pair_here, pair_near, pair_far, swap(pair_far, "ctx", 1))
    own_pre = enter(own_rows, pairs, F32)
    other_rows[:2], own_pre = lax.optimization_barrier((other_rows[:2], own_pre))
    first_pre = enter(other_rows[:2], pairs, BF16)
    first_pre, other_rows[2:] = lax.optimization_barrier((first_pre, other_rows[2:]))
    first_sum = swap(first_pre, "ctx", 2)
    last_sum = swap(enter(other_rows[2:], pairs, BF16), "ctx", 2)
    first = silu(own_pre, first_sum, 0)
    other_first = swap(first, "ctx", 2)
    down_near, other_shares = swap(down_here, "ctx", 1), swap(shares, "ctx", 2)
    last_sum, other_first, down_far, down_near, other_shares = lax.optimization_barrier(
        (last_sum, other_first, down_far, down_near, other_shares)
    )
    last = silu(own_pre, last_sum, 1)
    other_last = swap(last, "ctx", 2)
    downs = (down_here, down_near, down_far, swap(down_far, "ctx", 1))
    y = leave([first, last, other_first, other_last], downs)
    own_parts = [y[0]] + [swap(y[b], "exp", b) for b in (1, 2, 3)]
    other_parts = [y[4]] + [swap(y[4 + b], "exp", b) for b in (1, 2, 3)]
    back = swap(mixed(other_shares, other_parts).astype(BF16), "ctx", 2)
    return final(index, state, shares, *own_parts, back)


def solution(mesh):
    placed = (
        P("ctx", "exp"),
        P("ctx", None),
        P("ctx", None),
        P("exp", None),
        P(("ctx", "exp"), None),
        P(),
        P(("ctx", "exp"), None),
        P(("ctx", "exp"), None),
        P("exp", "ctx", None),
        P("exp", "ctx", None),
        P("exp", None, "ctx"),
    )
    shape = dict(mesh.shape)
    small = shape["ctx"] == 8 and shape["exp"] == 4
    return jax.shard_map(
        body if small else general_body, mesh=mesh, in_specs=placed, out_specs=P(("ctx", "exp"), None), check_vma=False
    )
```

```python
import functools
import math

import jax
import jax.numpy as jnp
from jax import lax
from jax.experimental import pallas as pl
from jax.experimental.pallas import tpu as pltpu
from jax.sharding import PartitionSpec as P

D = 4096
HQ = 64
KVH = 4
HD = 128


def general_body(
    queries,
    keys,
    values,
    w_out,
    residual,
    norm_gain,
    expert_ids,
    gate_weights,
    w_gate,
    w_up,
    w_down,
):
    tok_rows = queries.shape[0]
    half_rows = tok_rows // 2
    exp_count = lax.axis_size("exp")
    heads_here = HQ // exp_count
    group = HQ // KVH
    kv_here = max(1, heads_here // group)
    heads_per_kv = heads_here // kv_here
    exp_index = lax.axis_index("exp")
    ctx_index = lax.axis_index("ctx")
    kv_first = exp_index * heads_here // group
    key_cols = lax.dynamic_slice_in_dim(keys, kv_first * HD, kv_here * HD, 1)
    value_cols = lax.dynamic_slice_in_dim(values, kv_first * HD, kv_here * HD, 1)
    scale = 1.0 / math.sqrt(HD)
    first_rows = queries[:half_rows]
    second_rows = queries[half_rows:]
    first_start = ctx_index * tok_rows
    second_start = ctx_index * tok_rows + half_rows
    query_sets = (
        first_rows.reshape(half_rows, kv_here, heads_per_kv, HD),
        second_rows.reshape(half_rows, kv_here, heads_per_kv, HD),
    )
    query_positions = (
        first_start + jnp.arange(half_rows, dtype=jnp.int32),
        second_start + jnp.arange(half_rows, dtype=jnp.int32),
    )
    last_positions = (first_start + half_rows - 1, second_start + half_rows - 1)

    def block_update(carry, query_four, query_pos, key_block, value_block, key_start):
        run_max, run_sum, run_acc = carry
        width = key_block.shape[0]
        key_three = key_block.reshape(width, kv_here, HD)
        value_three = value_block.reshape(width, kv_here, HD)
        scores = (
            jnp.einsum("tghd,kgd->ghtk", query_four, key_three, preferred_element_type=jnp.float32)
            * scale
        )
        key_pos = key_start + jnp.arange(width, dtype=jnp.int32)
        allowed = key_pos[None, :] <= query_pos[:, None]
        scores = jnp.where(allowed, scores, -1e30)
        new_max = jnp.maximum(run_max, jnp.max(scores, axis=-1))
        probs = jnp.where(allowed, jnp.exp(scores - new_max[..., None]), 0.0)
        factor = jnp.exp(run_max - new_max)
        run_sum = run_sum * factor + jnp.sum(probs, axis=-1)
        weighted = jnp.einsum(
            "ghtk,kgd->ghtd",
            probs.astype(jnp.bfloat16),
            value_three,
            preferred_element_type=jnp.float32,
        )
        run_acc = run_acc * factor[..., None] + weighted
        return (new_max, run_sum, run_acc)

    start_max = jnp.full((kv_here, heads_per_kv, half_rows), -1e30, jnp.float32)
    start_sum = jnp.zeros((kv_here, heads_per_kv, half_rows), jnp.float32)
    start_acc = jnp.zeros((kv_here, heads_per_kv, half_rows, HD), jnp.float32)
    start_state = (start_max, start_sum, start_acc)
    key_piece = lax.all_gather(key_cols, "ctx", axis=0, tiled=True)
    value_piece = lax.all_gather(value_cols, "ctx", axis=0, tiled=True)
    count = key_piece.shape[0]
    width = 512

    def one_block(index, inner):
        key_start = index * width
        key_block = lax.dynamic_slice_in_dim(key_piece, key_start, width, 0)
        value_block = lax.dynamic_slice_in_dim(value_piece, key_start, width, 0)
        updated = []
        for which in range(2):
            query_four = query_sets[which]
            query_pos = query_positions[which]
            updated.append(
                lax.cond(
                    key_start > last_positions[which],
                    lambda state: state,
                    lambda state: block_update(
                        state, query_four, query_pos, key_block, value_block, key_start
                    ),
                    inner[which],
                )
            )
        return (updated[0], updated[1])

    states = lax.fori_loop(0, count // width, one_block, (start_state, start_state))
    halves = []
    for which in range(2):
        run_max, run_sum, run_acc = states[which]
        halves.append(
            jnp.transpose(run_acc / run_sum[..., None], (2, 0, 1, 3))
            .reshape(half_rows, heads_here * HD)
            .astype(jnp.bfloat16)
        )
    attn_second = halves[1]
    attn = jnp.concatenate([halves[0], attn_second], axis=0)
    projected = lax.psum_scatter(
        jnp.dot(attn, w_out, preferred_element_type=jnp.float32).astype(jnp.bfloat16),
        "exp",
        scatter_dimension=0,
        tiled=True,
    ).astype(jnp.float32)
    hidden_state = (residual.astype(jnp.float32) + projected).astype(jnp.bfloat16)
    state_f = hidden_state.astype(jnp.float32)
    inv_rms = 1.0 / jnp.sqrt(jnp.mean(state_f * state_f, axis=1, keepdims=True) + 1e-06)
    normed = (state_f * inv_rms * norm_gain.astype(jnp.float32)[None, :]).astype(jnp.bfloat16)
    rows_here = expert_ids.shape[0]
    top_count = expert_ids.shape[1]
    experts_all = w_gate.shape[0] * exp_count
    capacity = min(rows_here, 2 * rows_here * top_count // experts_all)
    flat_ids = expert_ids.reshape(-1)
    onehot = (flat_ids[:, None] == jnp.arange(experts_all, dtype=jnp.int32)[None, :]).astype(
        jnp.int32
    )
    earlier = jnp.cumsum(onehot, axis=0) - onehot
    slot_index = jnp.sum(earlier * onehot, axis=1)
    target = flat_ids * capacity + slot_index
    picks = target[:, None] == jnp.arange(experts_all * capacity, dtype=jnp.int32)[None, :]
    dispatch_table = jnp.any(
        picks.reshape(rows_here, top_count, experts_all * capacity), axis=1
    ).astype(jnp.bfloat16)
    outgoing = jnp.einsum(
        "rs,rd->sd", dispatch_table, normed, preferred_element_type=jnp.float32
    ).astype(jnp.bfloat16)
    arrived = lax.all_to_all(
        outgoing.reshape(experts_all, capacity, D), "exp", split_axis=0, concat_axis=0, tiled=True
    )
    slot_rows = arrived.reshape(experts_all * capacity, D)
    gate_local = w_gate[0]
    up_local = w_up[0]
    gate_pre = jnp.dot(
        slot_rows,
        lax.all_gather(gate_local, "ctx", axis=0, tiled=True),
        preferred_element_type=jnp.float32,
    )
    up_pre = jnp.dot(
        slot_rows,
        lax.all_gather(up_local, "ctx", axis=0, tiled=True),
        preferred_element_type=jnp.float32,
    )
    expert_hidden = (jax.nn.silu(gate_pre) * up_pre).astype(jnp.bfloat16)
    down_local = w_down[0]
    expert_result = jnp.dot(
        expert_hidden,
        lax.all_gather(down_local, "ctx", axis=1, tiled=True),
        preferred_element_type=jnp.float32,
    ).astype(jnp.bfloat16)
    returned = lax.all_to_all(
        expert_result.reshape(experts_all, capacity, D),
        "exp",
        split_axis=0,
        concat_axis=0,
        tiled=True,
    )
    returned_flat = returned.reshape(experts_all * capacity, D)
    picked = jnp.dot(picks.astype(jnp.bfloat16), returned_flat, preferred_element_type=jnp.float32)
    weighted = gate_weights[:, :, None] * picked.reshape(rows_here, top_count, D)
    return (state_f + jnp.sum(weighted, axis=1)).astype(jnp.bfloat16)


BF16 = jnp.bfloat16
F32 = jnp.float32
VMEM = pltpu.VMEM
QB = 256
CHEAP = pl.CostEstimate(flops=1000, bytes_accessed=1000, transcendentals=0)


def swap(array, axis, mask):
    size = lax.axis_size(axis)
    return lax.ppermute(array, axis, [(i, i ^ mask) for i in range(size)])


def params(mib):
    return pltpu.CompilerParams(vmem_limit_bytes=mib * 1024 * 1024)


def vmem_specs(count):
    return [pl.BlockSpec(memory_space=VMEM) for _ in range(count)]


def attention_kernel(index, q_hbm, *refs):
    arrived, w_hbm, outs = refs[:8], refs[8], refs[9:13]
    w_all, q, pieces, keys, ones_values, bias, even, odd, attn, q_sem, piece_sems, sems = refs[13:]
    q_fetch = pltpu.make_async_copy(q_hbm, q, q_sem)
    piece_fetches = [
        pltpu.make_async_copy(arrived[i], pieces.at[i], piece_sems.at[i]) for i in range(8)
    ]
    for fetch in piece_fetches + [q_fetch]:
        fetch.start()
    ctx = index[0]
    exp = index[1]
    chip = ctx // 2
    steps = sems.shape[0]
    depth = w_all.shape[0] // steps
    fetches = [
        pltpu.make_async_copy(
            w_hbm.at[pl.ds(i * depth, depth)], w_all.at[pl.ds(i * depth, depth)], sems.at[i]
        )
        for i in range(steps)
    ]
    factor = math.log2(math.e) / math.sqrt(HD)
    heads = q.shape[1] // HD
    ones_values[:, HD:] = jnp.ones((ones_values.shape[0], HD), BF16)
    core = ctx % 2
    row = lax.broadcasted_iota(jnp.int32, (QB, 2 * QB), 0) + core * QB
    col = lax.broadcasted_iota(jnp.int32, (QB, 2 * QB), 1)
    bias[...] = jnp.where(col <= row, 0.0, -1e30)
    for fetch in piece_fetches:
        fetch.wait()
    for d in range(4):

        @pl.when(chip >= d)
        def _():
            for other in range(2):
                piece = pieces.at[2 * d + other]
                place = 2 * (chip - d) + (core ^ other)
                here = pl.ds(pl.multiple_of(place * QB, QB), QB)
                keys[:, here] = piece[:, :HD].astype(F32).T.astype(BF16)
                ones_values[here, :HD] = piece[:, HD:]

    q_fetch.wait()
    for fetch in fetches:
        fetch.start()
    part = QB // 4

    def run(length):
        def scores_of(h, store):
            rows = q[:, pl.ds(pl.multiple_of(h * HD, HD), HD)]
            block = jnp.dot(rows, keys[:, :length], preferred_element_type=F32)
            last = length - 2 * QB
            if last:
                store[:, :last] = block[:, :last]
            store[:, last:length] = block[:, last:] + bias[...]

        def finish(h, store):
            block = store[:, :length]
            top = jnp.max(block, axis=1, keepdims=True) * factor
            probs = jnp.exp2(block * factor - top).astype(BF16)
            total = jnp.dot(probs, ones_values[:length, :], preferred_element_type=F32)
            done = (total[:, :HD] / total[:, HD:]).astype(BF16)
            cols = pl.ds(pl.multiple_of(h * HD, HD), HD)
            for i in range(4):
                start = pl.multiple_of((exp ^ i) * part, part)
                attn[pl.ds(start, part), cols] = done[i * part : (i + 1) * part]

        scores_of(0, even)

        @pl.loop(0, heads // 2)
        def _(pair):
            scores_of(2 * pair + 1, odd)
            finish(2 * pair, even)
            scores_of(jnp.minimum(2 * pair + 2, heads - 1), even)
            finish(2 * pair + 1, odd)

    for z in range(4):
        pl.when(chip == z)(functools.partial(run, (z + 1) * 2 * QB))

    for fetch in fetches:
        fetch.wait()
    width = 512
    for n in range(w_all.shape[1] // width):
        cols = slice(n * width, (n + 1) * width)
        block = jnp.dot(attn[...], w_all[:, cols], preferred_element_type=F32).astype(BF16)
        for b, out in enumerate(outs):
            out[:, cols] = block[b * part : (b + 1) * part]


def attention(index, queries, pieces, w_out):
    rows = QB // 4
    length = 8 * QB
    return pl.pallas_call(
        attention_kernel,
        out_shape=[jax.ShapeDtypeStruct((rows, D), BF16)] * 4,
        in_specs=[pl.BlockSpec(memory_space=pltpu.SMEM)]
        + [pl.BlockSpec(memory_space=pltpu.HBM)] * 10,
        out_specs=vmem_specs(4),
        scratch_shapes=[
            VMEM(w_out.shape, BF16),
            VMEM(queries.shape, BF16),
            VMEM((8,) + pieces[0].shape, BF16),
            VMEM((HD, length), BF16),
            VMEM((length, 2 * HD), BF16),
            VMEM((QB, 2 * QB), F32),
            VMEM((QB, length), F32),
            VMEM((QB, length), F32),
            VMEM(queries.shape, BF16),
            pltpu.SemaphoreType.DMA,
            pltpu.SemaphoreType.DMA((8,)),
            pltpu.SemaphoreType.DMA((16,)),
        ],
        compiler_params=params(52),
        cost_estimate=CHEAP,
        name="attention",
    )(index, queries, *pieces, w_out)


def norm_kernel(index, p0, r1, r2, r3, residual, gain, state, mine, theirs, work):
    ctx = index[0]
    total = p0[...].astype(F32) + r1[...].astype(F32) + r2[...].astype(F32) + r3[...].astype(F32)
    hidden = (residual[...].astype(F32) + total).astype(BF16)
    state[...] = hidden
    wide = hidden.astype(F32)
    inv = 1.0 / jnp.sqrt(jnp.mean(wide * wide, axis=1, keepdims=True) + 1e-06)
    normed = (wide * inv * gain[...].astype(F32)).astype(BF16)
    part = D // 8
    for j in range(8):
        work[j] = normed[:, j * part : (j + 1) * part]
    for j, (a, b) in enumerate(((0, 2), (1, 3), (6, 4), (7, 5))):
        mine[:, j * part : (j + 1) * part] = work[ctx ^ a]
        theirs[:, j * part : (j + 1) * part] = work[ctx ^ b]


def norm(index, p0, r1, r2, r3, residual, gain):
    rows = residual.shape[0]
    half = jax.ShapeDtypeStruct((rows, D // 2), BF16)
    return pl.pallas_call(
        norm_kernel,
        out_shape=[jax.ShapeDtypeStruct((rows, D), BF16), half, half],
        in_specs=[pl.BlockSpec(memory_space=pltpu.SMEM)] + vmem_specs(6),
        out_specs=vmem_specs(3),
        scratch_shapes=[VMEM((8, rows, D // 8), BF16)],
        compiler_params=params(16),
        cost_estimate=CHEAP,
        name="norm",
    )(index, p0, r1, r2, r3, residual, gain)


def enter_kernel(x0, x1, x2, x3, *refs):
    weights, out, gate_all, up_all, sems = refs[:4], refs[4], refs[5], refs[6], refs[7]
    part, width = weights[0].shape[0] // 2, weights[0].shape[1]
    fetches = []
    for which, whole in enumerate((gate_all, up_all)):
        for j, array in enumerate(weights):
            source = array.at[pl.ds(which * part, part)]
            target = whole.at[pl.ds(j * part, part)]
            fetches.append(pltpu.make_async_copy(source, target, sems.at[4 * which + j]))
            fetches[-1].start()
    x = jnp.concatenate([x0[...], x1[...], x2[...], x3[...]], axis=0)
    tile = 256
    for which, whole in enumerate((gate_all, up_all)):
        for fetch in fetches[4 * which : 4 * which + 4]:
            fetch.wait()
        for n in range(width // tile):
            cols = slice(which * width + n * tile, which * width + (n + 1) * tile)
            block = jnp.dot(x, whole[:, n * tile : (n + 1) * tile], preferred_element_type=F32)
            out[:, cols] = block.astype(out.dtype)


def enter(rows, weights, kind):
    count = 4 * rows[0].shape[0]
    part, width = weights[0].shape[0] // 2, weights[0].shape[1]
    return pl.pallas_call(
        enter_kernel,
        out_shape=jax.ShapeDtypeStruct((count, 2 * width), kind),
        in_specs=vmem_specs(4) + [pl.BlockSpec(memory_space=pl.ANY)] * 4,
        out_specs=pl.BlockSpec(memory_space=VMEM),
        scratch_shapes=[
            VMEM((4 * part, width), BF16),
            VMEM((4 * part, width), BF16),
            pltpu.SemaphoreType.DMA((8,)),
        ],
        compiler_params=params(24),
        cost_estimate=CHEAP,
        name="enter",
    )(*rows, *weights)


def silu_kernel(own, other, out):
    width = out.shape[1]
    total = own[...] + other[...].astype(F32)
    gate, up = total[:, :width], total[:, width:]
    out[...] = (gate / (1.0 + jnp.exp(-gate)) * up).astype(BF16)


def silu(own, other):
    return pl.pallas_call(
        silu_kernel,
        out_shape=jax.ShapeDtypeStruct((own.shape[0], own.shape[1] // 2), BF16),
        in_specs=vmem_specs(2),
        out_specs=pl.BlockSpec(memory_space=VMEM),
        compiler_params=params(16),
        cost_estimate=CHEAP,
        name="silu",
    )(own, other)


def leave_kernel(hidden, d0, d1, d2, d3, y0, y1, y2, y3, down_all, sems):
    part = y0.shape[0]
    width = d0.shape[1]
    fetches = []
    for j, array in enumerate((d0, d1, d2, d3)):
        fetches.append(pltpu.make_async_copy(array, down_all.at[j], sems.at[j]))
        fetches[-1].start()
    for j in range(4):
        fetches[j].wait()
        block = jnp.dot(hidden[...], down_all[j], preferred_element_type=F32).astype(BF16)
        for b, out in enumerate((y0, y1, y2, y3)):
            out[:, j * width : (j + 1) * width] = block[b * part : (b + 1) * part]


def leave(hidden, downs):
    part = jax.ShapeDtypeStruct((hidden.shape[0] // 4, 4 * downs[0].shape[1]), BF16)
    return pl.pallas_call(
        leave_kernel,
        out_shape=[part] * 4,
        in_specs=vmem_specs(1) + [pl.BlockSpec(memory_space=pl.ANY)] * 4,
        out_specs=vmem_specs(4),
        scratch_shapes=[VMEM((4,) + downs[0].shape, BF16), pltpu.SemaphoreType.DMA((4,))],
        compiler_params=params(16),
        cost_estimate=CHEAP,
        name="leave",
    )(hidden, *downs)


def mixed(shares, parts):
    total = shares[:, :1] * parts[0][...].astype(F32)
    for b in range(1, 4):
        total = total + shares[:, b : b + 1] * parts[b][...].astype(F32)
    return total


def final_kernel(index, state, shares, y0, r1, r2, r3, other, out):
    ctx = index[0]
    part = D // 8
    own = mixed(shares, (y0, r1, r2, r3))
    for j, (a, b) in enumerate(((0, 2), (1, 3), (6, 4), (7, 5))):
        cols = slice(j * part, (j + 1) * part)
        here = pl.ds(pl.multiple_of((ctx ^ a) * part, part), part)
        out[:, here] = (state[:, here].astype(F32) + own[:, cols]).astype(BF16)
        there = pl.ds(pl.multiple_of((ctx ^ b) * part, part), part)
        out[:, there] = (state[:, there].astype(F32) + other[:, cols].astype(F32)).astype(BF16)


def final(index, state, shares, y0, r1, r2, r3, other):
    return pl.pallas_call(
        final_kernel,
        out_shape=jax.ShapeDtypeStruct(state.shape, BF16),
        in_specs=[pl.BlockSpec(memory_space=pltpu.SMEM)] + vmem_specs(7),
        out_specs=pl.BlockSpec(memory_space=VMEM),
        compiler_params=params(16),
        cost_estimate=CHEAP,
        name="final",
    )(index, state, shares, y0, r1, r2, r3, other)


def body(
    queries,
    keys,
    values,
    w_out,
    residual,
    norm_gain,
    expert_ids,
    gate_weights,
    w_gate,
    w_up,
    w_down,
):
    exp = lax.axis_index("exp")
    ctx = lax.axis_index("ctx")
    index = jnp.stack([ctx, exp]).astype(jnp.int32)
    kv_first = exp * (HQ // 4) // (HQ // KVH) * HD
    kv_here = jnp.concatenate(
        [
            lax.dynamic_slice_in_dim(keys, kv_first, HD, 1),
            lax.dynamic_slice_in_dim(values, kv_first, HD, 1),
        ],
        axis=1,
    )
    def later(array, chips):
        return lax.ppermute(array, "ctx", [(i, i + 2 * chips) for i in range(8 - 2 * chips)])

    kv_here, gate_here, up_here = lax.optimization_barrier((kv_here, w_gate[0], w_up[0]))
    moved = [later(kv_here, d) for d in (3, 2, 1)][::-1]
    pair_here, down_here = jnp.concatenate([gate_here, up_here], axis=0), w_down[0]
    pieces = [part for piece in [kv_here] + moved for part in (piece, swap(piece, "ctx", 1))]
    pieces, pair_here = lax.optimization_barrier((pieces, pair_here))
    pair_far = swap(pair_here, "ctx", 6)

    lane = lax.broadcasted_iota(jnp.int32, (expert_ids.shape[0], HD), 1)
    shares = jnp.zeros(lane.shape, F32)
    for k in range(expert_ids.shape[1]):
        named = expert_ids[:, k : k + 1] ^ exp
        shares = shares + jnp.where(lane == named, gate_weights[:, k : k + 1], 0.0)

    p = attention(index, queries, pieces, w_out)
    p, shares, pair_here, down_here = lax.optimization_barrier((p, shares, pair_here, down_here))
    r = [swap(p[b], "exp", b) for b in (1, 2, 3)]
    pair_near, down_near = swap(pair_here, "ctx", 1), swap(down_here, "ctx", 1)
    other_shares = swap(shares, "ctx", 2)
    state, mine, theirs = norm(index, p[0], *r, residual, norm_gain.reshape(1, D))
    others = swap(theirs, "ctx", 2)
    own_rows = [mine] + [swap(mine, "exp", b) for b in (1, 2, 3)]
    others, own_rows[1:3] = lax.optimization_barrier((others, own_rows[1:3]))
    other_rows = [others] + [swap(others, "exp", b) for b in (1, 2, 3)]
    own_rows, other_rows, pair_far, down_here = lax.optimization_barrier(
        (own_rows, other_rows, pair_far, down_here)
    )
    down_far = swap(down_here, "ctx", 6)
    pairs = (pair_here, pair_near, pair_far, swap(pair_far, "ctx", 1))
    other_pre = enter(other_rows, pairs, BF16)
    from_other = swap(other_pre, "ctx", 2)
    own_rows, down_far = lax.optimization_barrier((own_rows, down_far))
    own_pre = enter(own_rows, pairs, F32)
    own_hidden = silu(own_pre, from_other)
    other_hidden = swap(own_hidden, "ctx", 2)
    downs = (down_here, down_near, down_far, swap(down_far, "ctx", 1))
    y = leave(own_hidden, downs)
    own_parts = [y[0]] + [swap(y[b], "exp", b) for b in (1, 2, 3)]
    other_hidden, *own_parts[1:3] = lax.optimization_barrier((other_hidden, *own_parts[1:3]))
    z = leave(other_hidden, downs)
    other_parts = [z[0]] + [swap(z[b], "exp", b) for b in (1, 2, 3)]
    back = swap(mixed(other_shares, other_parts).astype(BF16), "ctx", 2)
    return final(index, state, shares, *own_parts, back)


def solution(mesh):
    placed = (
        P("ctx", "exp"),
        P("ctx", None),
        P("ctx", None),
        P("exp", None),
        P(("ctx", "exp"), None),
        P(),
        P(("ctx", "exp"), None),
        P(("ctx", "exp"), None),
        P("exp", "ctx", None),
        P("exp", "ctx", None),
        P("exp", None, "ctx"),
    )
    shape = dict(mesh.shape)
    small = shape["ctx"] == 8 and shape["exp"] == 4
    return jax.shard_map(
        body if small else general_body, mesh=mesh, in_specs=placed, out_specs=P(("ctx", "exp"), None), check_vma=False
    )
```

```python
import functools
import math

import jax
import jax.numpy as jnp
from jax import lax
from jax.experimental import pallas as pl
from jax.experimental.pallas import tpu as pltpu
from jax.sharding import PartitionSpec as P

D = 4096
HQ = 64
KVH = 4
HD = 128


def general_body(
    queries,
    keys,
    values,
    w_out,
    residual,
    norm_gain,
    expert_ids,
    gate_weights,
    w_gate,
    w_up,
    w_down,
):
    tok_rows = queries.shape[0]
    half_rows = tok_rows // 2
    exp_count = lax.axis_size("exp")
    heads_here = HQ // exp_count
    group = HQ // KVH
    kv_here = max(1, heads_here // group)
    heads_per_kv = heads_here // kv_here
    exp_index = lax.axis_index("exp")
    ctx_index = lax.axis_index("ctx")
    kv_first = exp_index * heads_here // group
    key_cols = lax.dynamic_slice_in_dim(keys, kv_first * HD, kv_here * HD, 1)
    value_cols = lax.dynamic_slice_in_dim(values, kv_first * HD, kv_here * HD, 1)
    scale = 1.0 / math.sqrt(HD)
    first_rows = queries[:half_rows]
    second_rows = queries[half_rows:]
    first_start = ctx_index * tok_rows
    second_start = ctx_index * tok_rows + half_rows
    query_sets = (
        first_rows.reshape(half_rows, kv_here, heads_per_kv, HD),
        second_rows.reshape(half_rows, kv_here, heads_per_kv, HD),
    )
    query_positions = (
        first_start + jnp.arange(half_rows, dtype=jnp.int32),
        second_start + jnp.arange(half_rows, dtype=jnp.int32),
    )
    last_positions = (first_start + half_rows - 1, second_start + half_rows - 1)

    def block_update(carry, query_four, query_pos, key_block, value_block, key_start):
        run_max, run_sum, run_acc = carry
        width = key_block.shape[0]
        key_three = key_block.reshape(width, kv_here, HD)
        value_three = value_block.reshape(width, kv_here, HD)
        scores = (
            jnp.einsum("tghd,kgd->ghtk", query_four, key_three, preferred_element_type=jnp.float32)
            * scale
        )
        key_pos = key_start + jnp.arange(width, dtype=jnp.int32)
        allowed = key_pos[None, :] <= query_pos[:, None]
        scores = jnp.where(allowed, scores, -1e30)
        new_max = jnp.maximum(run_max, jnp.max(scores, axis=-1))
        probs = jnp.where(allowed, jnp.exp(scores - new_max[..., None]), 0.0)
        factor = jnp.exp(run_max - new_max)
        run_sum = run_sum * factor + jnp.sum(probs, axis=-1)
        weighted = jnp.einsum(
            "ghtk,kgd->ghtd",
            probs.astype(jnp.bfloat16),
            value_three,
            preferred_element_type=jnp.float32,
        )
        run_acc = run_acc * factor[..., None] + weighted
        return (new_max, run_sum, run_acc)

    start_max = jnp.full((kv_here, heads_per_kv, half_rows), -1e30, jnp.float32)
    start_sum = jnp.zeros((kv_here, heads_per_kv, half_rows), jnp.float32)
    start_acc = jnp.zeros((kv_here, heads_per_kv, half_rows, HD), jnp.float32)
    start_state = (start_max, start_sum, start_acc)
    key_piece = lax.all_gather(key_cols, "ctx", axis=0, tiled=True)
    value_piece = lax.all_gather(value_cols, "ctx", axis=0, tiled=True)
    count = key_piece.shape[0]
    width = 512

    def one_block(index, inner):
        key_start = index * width
        key_block = lax.dynamic_slice_in_dim(key_piece, key_start, width, 0)
        value_block = lax.dynamic_slice_in_dim(value_piece, key_start, width, 0)
        updated = []
        for which in range(2):
            query_four = query_sets[which]
            query_pos = query_positions[which]
            updated.append(
                lax.cond(
                    key_start > last_positions[which],
                    lambda state: state,
                    lambda state: block_update(
                        state, query_four, query_pos, key_block, value_block, key_start
                    ),
                    inner[which],
                )
            )
        return (updated[0], updated[1])

    states = lax.fori_loop(0, count // width, one_block, (start_state, start_state))
    halves = []
    for which in range(2):
        run_max, run_sum, run_acc = states[which]
        halves.append(
            jnp.transpose(run_acc / run_sum[..., None], (2, 0, 1, 3))
            .reshape(half_rows, heads_here * HD)
            .astype(jnp.bfloat16)
        )
    attn_second = halves[1]
    attn = jnp.concatenate([halves[0], attn_second], axis=0)
    projected = lax.psum_scatter(
        jnp.dot(attn, w_out, preferred_element_type=jnp.float32).astype(jnp.bfloat16),
        "exp",
        scatter_dimension=0,
        tiled=True,
    ).astype(jnp.float32)
    hidden_state = (residual.astype(jnp.float32) + projected).astype(jnp.bfloat16)
    state_f = hidden_state.astype(jnp.float32)
    inv_rms = 1.0 / jnp.sqrt(jnp.mean(state_f * state_f, axis=1, keepdims=True) + 1e-06)
    normed = (state_f * inv_rms * norm_gain.astype(jnp.float32)[None, :]).astype(jnp.bfloat16)
    rows_here = expert_ids.shape[0]
    top_count = expert_ids.shape[1]
    experts_all = w_gate.shape[0] * exp_count
    capacity = min(rows_here, 2 * rows_here * top_count // experts_all)
    flat_ids = expert_ids.reshape(-1)
    onehot = (flat_ids[:, None] == jnp.arange(experts_all, dtype=jnp.int32)[None, :]).astype(
        jnp.int32
    )
    earlier = jnp.cumsum(onehot, axis=0) - onehot
    slot_index = jnp.sum(earlier * onehot, axis=1)
    target = flat_ids * capacity + slot_index
    picks = target[:, None] == jnp.arange(experts_all * capacity, dtype=jnp.int32)[None, :]
    dispatch_table = jnp.any(
        picks.reshape(rows_here, top_count, experts_all * capacity), axis=1
    ).astype(jnp.bfloat16)
    outgoing = jnp.einsum(
        "rs,rd->sd", dispatch_table, normed, preferred_element_type=jnp.float32
    ).astype(jnp.bfloat16)
    arrived = lax.all_to_all(
        outgoing.reshape(experts_all, capacity, D), "exp", split_axis=0, concat_axis=0, tiled=True
    )
    slot_rows = arrived.reshape(experts_all * capacity, D)
    gate_local = w_gate[0]
    up_local = w_up[0]
    gate_pre = jnp.dot(
        slot_rows,
        lax.all_gather(gate_local, "ctx", axis=0, tiled=True),
        preferred_element_type=jnp.float32,
    )
    up_pre = jnp.dot(
        slot_rows,
        lax.all_gather(up_local, "ctx", axis=0, tiled=True),
        preferred_element_type=jnp.float32,
    )
    expert_hidden = (jax.nn.silu(gate_pre) * up_pre).astype(jnp.bfloat16)
    down_local = w_down[0]
    expert_result = jnp.dot(
        expert_hidden,
        lax.all_gather(down_local, "ctx", axis=1, tiled=True),
        preferred_element_type=jnp.float32,
    ).astype(jnp.bfloat16)
    returned = lax.all_to_all(
        expert_result.reshape(experts_all, capacity, D),
        "exp",
        split_axis=0,
        concat_axis=0,
        tiled=True,
    )
    returned_flat = returned.reshape(experts_all * capacity, D)
    picked = jnp.dot(picks.astype(jnp.bfloat16), returned_flat, preferred_element_type=jnp.float32)
    weighted = gate_weights[:, :, None] * picked.reshape(rows_here, top_count, D)
    return (state_f + jnp.sum(weighted, axis=1)).astype(jnp.bfloat16)


BF16 = jnp.bfloat16
F32 = jnp.float32
VMEM = pltpu.VMEM
QB = 256
CHEAP = pl.CostEstimate(flops=1000, bytes_accessed=1000, transcendentals=0)


def swap(array, axis, mask):
    size = lax.axis_size(axis)
    return lax.ppermute(array, axis, [(i, i ^ mask) for i in range(size)])


def params(mib):
    return pltpu.CompilerParams(vmem_limit_bytes=mib * 1024 * 1024)


def vmem_specs(count):
    return [pl.BlockSpec(memory_space=VMEM) for _ in range(count)]


def attention_kernel(index, q_hbm, *refs):
    arrived, w_hbm, outs = refs[:8], refs[8], refs[9:13]
    w_all, q, pieces, keys, ones_values, bias, even, odd, attn, q_sem, piece_sems, sems = refs[13:]
    q_fetch = pltpu.make_async_copy(q_hbm, q, q_sem)
    piece_fetches = [
        pltpu.make_async_copy(arrived[i], pieces.at[i], piece_sems.at[i]) for i in range(8)
    ]
    for fetch in piece_fetches + [q_fetch]:
        fetch.start()
    ctx = index[0]
    exp = index[1]
    chip = ctx // 2
    steps = sems.shape[0]
    depth = w_all.shape[0] // steps
    fetches = [
        pltpu.make_async_copy(
            w_hbm.at[pl.ds(i * depth, depth)], w_all.at[pl.ds(i * depth, depth)], sems.at[i]
        )
        for i in range(steps)
    ]
    factor = math.log2(math.e) / math.sqrt(HD)
    heads = q.shape[1] // HD
    ones_values[:, HD:] = jnp.ones((ones_values.shape[0], HD), BF16)
    core = ctx % 2
    row = lax.broadcasted_iota(jnp.int32, (QB, 2 * QB), 0) + core * QB
    col = lax.broadcasted_iota(jnp.int32, (QB, 2 * QB), 1)
    bias[...] = jnp.where(col <= row, 0.0, -1e30)
    for fetch in piece_fetches:
        fetch.wait()
    for d in range(4):

        @pl.when(chip >= d)
        def _():
            for other in range(2):
                piece = pieces.at[2 * d + other]
                place = 2 * (chip - d) + (core ^ other)
                here = pl.ds(pl.multiple_of(place * QB, QB), QB)
                keys[:, here] = piece[:, :HD].astype(F32).T.astype(BF16)
                ones_values[here, :HD] = piece[:, HD:]

    q_fetch.wait()
    for fetch in fetches:
        fetch.start()
    part = QB // 4

    def run(length):
        def scores_of(h, store):
            rows = q[:, pl.ds(pl.multiple_of(h * HD, HD), HD)]
            block = jnp.dot(rows, keys[:, :length], preferred_element_type=F32)
            last = length - 2 * QB
            if last:
                store[:, :last] = block[:, :last]
            store[:, last:length] = block[:, last:] + bias[...]

        def finish(h, store):
            block = store[:, :length]
            top = jnp.max(block, axis=1, keepdims=True) * factor
            probs = jnp.exp2(block * factor - top).astype(BF16)
            total = jnp.dot(probs, ones_values[:length, :], preferred_element_type=F32)
            done = (total[:, :HD] / total[:, HD:]).astype(BF16)
            cols = pl.ds(pl.multiple_of(h * HD, HD), HD)
            for i in range(4):
                start = pl.multiple_of((exp ^ i) * part, part)
                attn[pl.ds(start, part), cols] = done[i * part : (i + 1) * part]

        scores_of(0, even)

        @pl.loop(0, heads // 2)
        def _(pair):
            scores_of(2 * pair + 1, odd)
            finish(2 * pair, even)
            scores_of(jnp.minimum(2 * pair + 2, heads - 1), even)
            finish(2 * pair + 1, odd)

    for z in range(4):
        pl.when(chip == z)(functools.partial(run, (z + 1) * 2 * QB))

    for fetch in fetches:
        fetch.wait()
    width = 512
    for n in range(w_all.shape[1] // width):
        cols = slice(n * width, (n + 1) * width)
        block = jnp.dot(attn[...], w_all[:, cols], preferred_element_type=F32).astype(BF16)
        for b, out in enumerate(outs):
            out[:, cols] = block[b * part : (b + 1) * part]


def attention(index, queries, pieces, w_out):
    rows = QB // 4
    length = 8 * QB
    return pl.pallas_call(
        attention_kernel,
        out_shape=[jax.ShapeDtypeStruct((rows, D), BF16)] * 4,
        in_specs=[pl.BlockSpec(memory_space=pltpu.SMEM)]
        + [pl.BlockSpec(memory_space=pltpu.HBM)] * 10,
        out_specs=vmem_specs(4),
        scratch_shapes=[
            VMEM(w_out.shape, BF16),
            VMEM(queries.shape, BF16),
            VMEM((8,) + pieces[0].shape, BF16),
            VMEM((HD, length), BF16),
            VMEM((length, 2 * HD), BF16),
            VMEM((QB, 2 * QB), F32),
            VMEM((QB, length), F32),
            VMEM((QB, length), F32),
            VMEM(queries.shape, BF16),
            pltpu.SemaphoreType.DMA,
            pltpu.SemaphoreType.DMA((8,)),
            pltpu.SemaphoreType.DMA((16,)),
        ],
        compiler_params=params(52),
        cost_estimate=CHEAP,
        name="attention",
    )(index, queries, *pieces, w_out)


def norm_kernel(index, p0, r1, r2, r3, residual, gain, state, mine, theirs, work):
    ctx = index[0]
    total = p0[...].astype(F32) + r1[...].astype(F32) + r2[...].astype(F32) + r3[...].astype(F32)
    hidden = (residual[...].astype(F32) + total).astype(BF16)
    state[...] = hidden
    wide = hidden.astype(F32)
    inv = 1.0 / jnp.sqrt(jnp.mean(wide * wide, axis=1, keepdims=True) + 1e-06)
    normed = (wide * inv * gain[...].astype(F32)).astype(BF16)
    part = D // 8
    for j in range(8):
        work[j] = normed[:, j * part : (j + 1) * part]
    for j, (a, b) in enumerate(((0, 2), (1, 3), (6, 4), (7, 5))):
        mine[:, j * part : (j + 1) * part] = work[ctx ^ a]
        theirs[:, j * part : (j + 1) * part] = work[ctx ^ b]


def norm(index, p0, r1, r2, r3, residual, gain):
    rows = residual.shape[0]
    half = jax.ShapeDtypeStruct((rows, D // 2), BF16)
    return pl.pallas_call(
        norm_kernel,
        out_shape=[jax.ShapeDtypeStruct((rows, D), BF16), half, half],
        in_specs=[pl.BlockSpec(memory_space=pltpu.SMEM)] + vmem_specs(6),
        out_specs=vmem_specs(3),
        scratch_shapes=[VMEM((8, rows, D // 8), BF16)],
        compiler_params=params(16),
        cost_estimate=CHEAP,
        name="norm",
    )(index, p0, r1, r2, r3, residual, gain)


def enter_kernel(x0, x1, x2, x3, *refs):
    weights, out, gate_all, up_all, sems = refs[:4], refs[4], refs[5], refs[6], refs[7]
    part, width = weights[0].shape[0] // 2, weights[0].shape[1]
    fetches = []
    for which, whole in enumerate((gate_all, up_all)):
        for j, array in enumerate(weights):
            source = array.at[pl.ds(which * part, part)]
            target = whole.at[pl.ds(j * part, part)]
            fetches.append(pltpu.make_async_copy(source, target, sems.at[4 * which + j]))
            fetches[-1].start()
    x = jnp.concatenate([x0[...], x1[...], x2[...], x3[...]], axis=0)
    tile = 256
    for which, whole in enumerate((gate_all, up_all)):
        for fetch in fetches[4 * which : 4 * which + 4]:
            fetch.wait()
        for n in range(width // tile):
            cols = slice(which * width + n * tile, which * width + (n + 1) * tile)
            block = jnp.dot(x, whole[:, n * tile : (n + 1) * tile], preferred_element_type=F32)
            out[:, cols] = block.astype(out.dtype)


def enter(rows, weights, kind):
    count = 4 * rows[0].shape[0]
    part, width = weights[0].shape[0] // 2, weights[0].shape[1]
    return pl.pallas_call(
        enter_kernel,
        out_shape=jax.ShapeDtypeStruct((count, 2 * width), kind),
        in_specs=vmem_specs(4) + [pl.BlockSpec(memory_space=pl.ANY)] * 4,
        out_specs=pl.BlockSpec(memory_space=VMEM),
        scratch_shapes=[
            VMEM((4 * part, width), BF16),
            VMEM((4 * part, width), BF16),
            pltpu.SemaphoreType.DMA((8,)),
        ],
        compiler_params=params(24),
        cost_estimate=CHEAP,
        name="enter",
    )(*rows, *weights)


def silu_kernel(own, other, out):
    width = out.shape[1]
    total = own[...] + other[...].astype(F32)
    gate, up = total[:, :width], total[:, width:]
    out[...] = (gate / (1.0 + jnp.exp(-gate)) * up).astype(BF16)


def silu(own, other):
    return pl.pallas_call(
        silu_kernel,
        out_shape=jax.ShapeDtypeStruct((own.shape[0], own.shape[1] // 2), BF16),
        in_specs=vmem_specs(2),
        out_specs=pl.BlockSpec(memory_space=VMEM),
        compiler_params=params(16),
        cost_estimate=CHEAP,
        name="silu",
    )(own, other)


def leave_kernel(hidden, d0, d1, d2, d3, y0, y1, y2, y3, down_all, sems):
    part = y0.shape[0]
    width = d0.shape[1]
    fetches = []
    for j, array in enumerate((d0, d1, d2, d3)):
        fetches.append(pltpu.make_async_copy(array, down_all.at[j], sems.at[j]))
        fetches[-1].start()
    for j in range(4):
        fetches[j].wait()
        block = jnp.dot(hidden[...], down_all[j], preferred_element_type=F32).astype(BF16)
        for b, out in enumerate((y0, y1, y2, y3)):
            out[:, j * width : (j + 1) * width] = block[b * part : (b + 1) * part]


def leave(hidden, downs):
    part = jax.ShapeDtypeStruct((hidden.shape[0] // 4, 4 * downs[0].shape[1]), BF16)
    return pl.pallas_call(
        leave_kernel,
        out_shape=[part] * 4,
        in_specs=vmem_specs(1) + [pl.BlockSpec(memory_space=pl.ANY)] * 4,
        out_specs=vmem_specs(4),
        scratch_shapes=[VMEM((4,) + downs[0].shape, BF16), pltpu.SemaphoreType.DMA((4,))],
        compiler_params=params(16),
        cost_estimate=CHEAP,
        name="leave",
    )(hidden, *downs)


def mixed(shares, parts):
    total = shares[:, :1] * parts[0][...].astype(F32)
    for b in range(1, 4):
        total = total + shares[:, b : b + 1] * parts[b][...].astype(F32)
    return total


def final_kernel(index, state, shares, y0, r1, r2, r3, other, out):
    ctx = index[0]
    part = D // 8
    own = mixed(shares, (y0, r1, r2, r3))
    for j, (a, b) in enumerate(((0, 2), (1, 3), (6, 4), (7, 5))):
        cols = slice(j * part, (j + 1) * part)
        here = pl.ds(pl.multiple_of((ctx ^ a) * part, part), part)
        out[:, here] = (state[:, here].astype(F32) + own[:, cols]).astype(BF16)
        there = pl.ds(pl.multiple_of((ctx ^ b) * part, part), part)
        out[:, there] = (state[:, there].astype(F32) + other[:, cols].astype(F32)).astype(BF16)


def final(index, state, shares, y0, r1, r2, r3, other):
    return pl.pallas_call(
        final_kernel,
        out_shape=jax.ShapeDtypeStruct(state.shape, BF16),
        in_specs=[pl.BlockSpec(memory_space=pltpu.SMEM)] + vmem_specs(7),
        out_specs=pl.BlockSpec(memory_space=VMEM),
        compiler_params=params(16),
        cost_estimate=CHEAP,
        name="final",
    )(index, state, shares, y0, r1, r2, r3, other)


def body(
    queries,
    keys,
    values,
    w_out,
    residual,
    norm_gain,
    expert_ids,
    gate_weights,
    w_gate,
    w_up,
    w_down,
):
    exp = lax.axis_index("exp")
    ctx = lax.axis_index("ctx")
    index = jnp.stack([ctx, exp]).astype(jnp.int32)
    kv_first = exp * (HQ // 4) // (HQ // KVH) * HD
    kv_here = jnp.concatenate(
        [
            lax.dynamic_slice_in_dim(keys, kv_first, HD, 1),
            lax.dynamic_slice_in_dim(values, kv_first, HD, 1),
        ],
        axis=1,
    )
    def later(array, chips):
        return lax.ppermute(array, "ctx", [(i, i + 2 * chips) for i in range(8 - 2 * chips)])

    kv_here, gate_here, up_here = lax.optimization_barrier((kv_here, w_gate[0], w_up[0]))
    moved = [later(kv_here, d) for d in (3, 2, 1)][::-1]
    pair_here, down_here = jnp.concatenate([gate_here, up_here], axis=0), w_down[0]
    pieces = [part for piece in [kv_here] + moved for part in (piece, swap(piece, "ctx", 1))]
    pair_far = swap(pair_here, "ctx", 6)

    lane = lax.broadcasted_iota(jnp.int32, (expert_ids.shape[0], HD), 1)
    shares = jnp.zeros(lane.shape, F32)
    for k in range(expert_ids.shape[1]):
        named = expert_ids[:, k : k + 1] ^ exp
        shares = shares + jnp.where(lane == named, gate_weights[:, k : k + 1], 0.0)

    p = attention(index, queries, pieces, w_out)
    p, shares, pair_here, down_here = lax.optimization_barrier((p, shares, pair_here, down_here))
    r = [swap(p[b], "exp", b) for b in (1, 2, 3)]
    pair_near, down_near = swap(pair_here, "ctx", 1), swap(down_here, "ctx", 1)
    other_shares = swap(shares, "ctx", 2)
    state, mine, theirs = norm(index, p[0], *r, residual, norm_gain.reshape(1, D))
    others = swap(theirs, "ctx", 2)
    own_rows = [mine] + [swap(mine, "exp", b) for b in (1, 2, 3)]
    other_rows = [others] + [swap(others, "exp", b) for b in (1, 2, 3)]
    own_rows, others, pair_far, down_here = lax.optimization_barrier(
        (own_rows, others, pair_far, down_here)
    )
    down_far = swap(down_here, "ctx", 6)
    pairs = (pair_here, pair_near, pair_far, swap(pair_far, "ctx", 1))
    other_pre = enter(other_rows, pairs, BF16)
    from_other = swap(other_pre, "ctx", 2)
    own_rows, down_far = lax.optimization_barrier((own_rows, down_far))
    own_pre = enter(own_rows, pairs, F32)
    own_hidden = silu(own_pre, from_other)
    other_hidden = swap(own_hidden, "ctx", 2)
    downs = (down_here, down_near, down_far, swap(down_far, "ctx", 1))
    y = leave(own_hidden, downs)
    own_parts = [y[0]] + [swap(y[b], "exp", b) for b in (1, 2, 3)]
    other_hidden, *own_parts[1:3] = lax.optimization_barrier((other_hidden, *own_parts[1:3]))
    z = leave(other_hidden, downs)
    other_parts = [z[0]] + [swap(z[b], "exp", b) for b in (1, 2, 3)]
    back = swap(mixed(other_shares, other_parts).astype(BF16), "ctx", 2)
    return final(index, state, shares, *own_parts, back)


def solution(mesh):
    placed = (
        P("ctx", "exp"),
        P("ctx", None),
        P("ctx", None),
        P("exp", None),
        P(("ctx", "exp"), None),
        P(),
        P(("ctx", "exp"), None),
        P(("ctx", "exp"), None),
        P("exp", "ctx", None),
        P("exp", "ctx", None),
        P("exp", None, "ctx"),
    )
    shape = dict(mesh.shape)
    small = shape["ctx"] == 8 and shape["exp"] == 4
    return jax.shard_map(
        body if small else general_body, mesh=mesh, in_specs=placed, out_specs=P(("ctx", "exp"), None), check_vma=False
    )
```

```python
import functools
import math

import jax
import jax.numpy as jnp
from jax import lax
from jax.experimental import pallas as pl
from jax.experimental.pallas import tpu as pltpu
from jax.sharding import PartitionSpec as P

D = 4096
HQ = 64
KVH = 4
HD = 128


def general_body(
    queries,
    keys,
    values,
    w_out,
    residual,
    norm_gain,
    expert_ids,
    gate_weights,
    w_gate,
    w_up,
    w_down,
):
    tok_rows = queries.shape[0]
    half_rows = tok_rows // 2
    exp_count = lax.axis_size("exp")
    heads_here = HQ // exp_count
    group = HQ // KVH
    kv_here = max(1, heads_here // group)
    heads_per_kv = heads_here // kv_here
    exp_index = lax.axis_index("exp")
    ctx_index = lax.axis_index("ctx")
    kv_first = exp_index * heads_here // group
    key_cols = lax.dynamic_slice_in_dim(keys, kv_first * HD, kv_here * HD, 1)
    value_cols = lax.dynamic_slice_in_dim(values, kv_first * HD, kv_here * HD, 1)
    scale = 1.0 / math.sqrt(HD)
    first_rows = queries[:half_rows]
    second_rows = queries[half_rows:]
    first_start = ctx_index * tok_rows
    second_start = ctx_index * tok_rows + half_rows
    query_sets = (
        first_rows.reshape(half_rows, kv_here, heads_per_kv, HD),
        second_rows.reshape(half_rows, kv_here, heads_per_kv, HD),
    )
    query_positions = (
        first_start + jnp.arange(half_rows, dtype=jnp.int32),
        second_start + jnp.arange(half_rows, dtype=jnp.int32),
    )
    last_positions = (first_start + half_rows - 1, second_start + half_rows - 1)

    def block_update(carry, query_four, query_pos, key_block, value_block, key_start):
        run_max, run_sum, run_acc = carry
        width = key_block.shape[0]
        key_three = key_block.reshape(width, kv_here, HD)
        value_three = value_block.reshape(width, kv_here, HD)
        scores = (
            jnp.einsum("tghd,kgd->ghtk", query_four, key_three, preferred_element_type=jnp.float32)
            * scale
        )
        key_pos = key_start + jnp.arange(width, dtype=jnp.int32)
        allowed = key_pos[None, :] <= query_pos[:, None]
        scores = jnp.where(allowed, scores, -1e30)
        new_max = jnp.maximum(run_max, jnp.max(scores, axis=-1))
        probs = jnp.where(allowed, jnp.exp(scores - new_max[..., None]), 0.0)
        factor = jnp.exp(run_max - new_max)
        run_sum = run_sum * factor + jnp.sum(probs, axis=-1)
        weighted = jnp.einsum(
            "ghtk,kgd->ghtd",
            probs.astype(jnp.bfloat16),
            value_three,
            preferred_element_type=jnp.float32,
        )
        run_acc = run_acc * factor[..., None] + weighted
        return (new_max, run_sum, run_acc)

    start_max = jnp.full((kv_here, heads_per_kv, half_rows), -1e30, jnp.float32)
    start_sum = jnp.zeros((kv_here, heads_per_kv, half_rows), jnp.float32)
    start_acc = jnp.zeros((kv_here, heads_per_kv, half_rows, HD), jnp.float32)
    start_state = (start_max, start_sum, start_acc)
    key_piece = lax.all_gather(key_cols, "ctx", axis=0, tiled=True)
    value_piece = lax.all_gather(value_cols, "ctx", axis=0, tiled=True)
    count = key_piece.shape[0]
    width = 512

    def one_block(index, inner):
        key_start = index * width
        key_block = lax.dynamic_slice_in_dim(key_piece, key_start, width, 0)
        value_block = lax.dynamic_slice_in_dim(value_piece, key_start, width, 0)
        updated = []
        for which in range(2):
            query_four = query_sets[which]
            query_pos = query_positions[which]
            updated.append(
                lax.cond(
                    key_start > last_positions[which],
                    lambda state: state,
                    lambda state: block_update(
                        state, query_four, query_pos, key_block, value_block, key_start
                    ),
                    inner[which],
                )
            )
        return (updated[0], updated[1])

    states = lax.fori_loop(0, count // width, one_block, (start_state, start_state))
    halves = []
    for which in range(2):
        run_max, run_sum, run_acc = states[which]
        halves.append(
            jnp.transpose(run_acc / run_sum[..., None], (2, 0, 1, 3))
            .reshape(half_rows, heads_here * HD)
            .astype(jnp.bfloat16)
        )
    attn_second = halves[1]
    attn = jnp.concatenate([halves[0], attn_second], axis=0)
    projected = lax.psum_scatter(
        jnp.dot(attn, w_out, preferred_element_type=jnp.float32).astype(jnp.bfloat16),
        "exp",
        scatter_dimension=0,
        tiled=True,
    ).astype(jnp.float32)
    hidden_state = (residual.astype(jnp.float32) + projected).astype(jnp.bfloat16)
    state_f = hidden_state.astype(jnp.float32)
    inv_rms = 1.0 / jnp.sqrt(jnp.mean(state_f * state_f, axis=1, keepdims=True) + 1e-06)
    normed = (state_f * inv_rms * norm_gain.astype(jnp.float32)[None, :]).astype(jnp.bfloat16)
    rows_here = expert_ids.shape[0]
    top_count = expert_ids.shape[1]
    experts_all = w_gate.shape[0] * exp_count
    capacity = min(rows_here, 2 * rows_here * top_count // experts_all)
    flat_ids = expert_ids.reshape(-1)
    onehot = (flat_ids[:, None] == jnp.arange(experts_all, dtype=jnp.int32)[None, :]).astype(
        jnp.int32
    )
    earlier = jnp.cumsum(onehot, axis=0) - onehot
    slot_index = jnp.sum(earlier * onehot, axis=1)
    target = flat_ids * capacity + slot_index
    picks = target[:, None] == jnp.arange(experts_all * capacity, dtype=jnp.int32)[None, :]
    dispatch_table = jnp.any(
        picks.reshape(rows_here, top_count, experts_all * capacity), axis=1
    ).astype(jnp.bfloat16)
    outgoing = jnp.einsum(
        "rs,rd->sd", dispatch_table, normed, preferred_element_type=jnp.float32
    ).astype(jnp.bfloat16)
    arrived = lax.all_to_all(
        outgoing.reshape(experts_all, capacity, D), "exp", split_axis=0, concat_axis=0, tiled=True
    )
    slot_rows = arrived.reshape(experts_all * capacity, D)
    gate_local = w_gate[0]
    up_local = w_up[0]
    gate_pre = jnp.dot(
        slot_rows,
        lax.all_gather(gate_local, "ctx", axis=0, tiled=True),
        preferred_element_type=jnp.float32,
    )
    up_pre = jnp.dot(
        slot_rows,
        lax.all_gather(up_local, "ctx", axis=0, tiled=True),
        preferred_element_type=jnp.float32,
    )
    expert_hidden = (jax.nn.silu(gate_pre) * up_pre).astype(jnp.bfloat16)
    down_local = w_down[0]
    expert_result = jnp.dot(
        expert_hidden,
        lax.all_gather(down_local, "ctx", axis=1, tiled=True),
        preferred_element_type=jnp.float32,
    ).astype(jnp.bfloat16)
    returned = lax.all_to_all(
        expert_result.reshape(experts_all, capacity, D),
        "exp",
        split_axis=0,
        concat_axis=0,
        tiled=True,
    )
    returned_flat = returned.reshape(experts_all * capacity, D)
    picked = jnp.dot(picks.astype(jnp.bfloat16), returned_flat, preferred_element_type=jnp.float32)
    weighted = gate_weights[:, :, None] * picked.reshape(rows_here, top_count, D)
    return (state_f + jnp.sum(weighted, axis=1)).astype(jnp.bfloat16)


BF16 = jnp.bfloat16
F32 = jnp.float32
VMEM = pltpu.VMEM
QB = 256
CHEAP = pl.CostEstimate(flops=1000, bytes_accessed=1000, transcendentals=0)


def swap(array, axis, mask):
    size = lax.axis_size(axis)
    return lax.ppermute(array, axis, [(i, i ^ mask) for i in range(size)])


def params(mib):
    return pltpu.CompilerParams(vmem_limit_bytes=mib * 1024 * 1024)


def vmem_specs(count):
    return [pl.BlockSpec(memory_space=VMEM) for _ in range(count)]


def attention_kernel(index, q_hbm, *refs):
    arrived, w_hbm, outs = refs[:8], refs[8], refs[9:13]
    w_all, q, pieces, keys, ones_values, bias, even, odd, attn, q_sem, piece_sems, sems = refs[13:]
    q_fetch = pltpu.make_async_copy(q_hbm, q, q_sem)
    piece_fetches = [
        pltpu.make_async_copy(arrived[i], pieces.at[i], piece_sems.at[i]) for i in range(8)
    ]
    for fetch in piece_fetches + [q_fetch]:
        fetch.start()
    ctx = index[0]
    exp = index[1]
    chip = ctx // 2
    steps = sems.shape[0]
    depth = w_all.shape[0] // steps
    fetches = [
        pltpu.make_async_copy(
            w_hbm.at[pl.ds(i * depth, depth)], w_all.at[pl.ds(i * depth, depth)], sems.at[i]
        )
        for i in range(steps)
    ]
    factor = math.log2(math.e) / math.sqrt(HD)
    heads = q.shape[1] // HD
    ones_values[:, HD:] = jnp.ones((ones_values.shape[0], HD), BF16)
    core = ctx % 2
    row = lax.broadcasted_iota(jnp.int32, (QB, 2 * QB), 0) + core * QB
    col = lax.broadcasted_iota(jnp.int32, (QB, 2 * QB), 1)
    bias[...] = jnp.where(col <= row, 0.0, -1e30)
    for fetch in piece_fetches:
        fetch.wait()
    for d in range(4):

        @pl.when(chip >= d)
        def _():
            for other in range(2):
                piece = pieces.at[2 * d + other]
                place = 2 * (chip - d) + (core ^ other)
                here = pl.ds(pl.multiple_of(place * QB, QB), QB)
                keys[:, here] = piece[:, :HD].astype(F32).T.astype(BF16)
                ones_values[here, :HD] = piece[:, HD:]

    q_fetch.wait()
    for fetch in fetches:
        fetch.start()
    part = QB // 4

    def run(length):
        def scores_of(h, store):
            rows = q[:, pl.ds(pl.multiple_of(h * HD, HD), HD)]
            block = jnp.dot(rows, keys[:, :length], preferred_element_type=F32)
            last = length - 2 * QB
            if last:
                store[:, :last] = block[:, :last]
            store[:, last:length] = block[:, last:] + bias[...]

        def finish(h, store):
            block = store[:, :length]
            top = jnp.max(block, axis=1, keepdims=True) * factor
            probs = jnp.exp2(block * factor - top).astype(BF16)
            total = jnp.dot(probs, ones_values[:length, :], preferred_element_type=F32)
            done = (total[:, :HD] / total[:, HD:]).astype(BF16)
            cols = pl.ds(pl.multiple_of(h * HD, HD), HD)
            for i in range(4):
                start = pl.multiple_of((exp ^ i) * part, part)
                attn[pl.ds(start, part), cols] = done[i * part : (i + 1) * part]

        scores_of(0, even)

        @pl.loop(0, heads // 2)
        def _(pair):
            scores_of(2 * pair + 1, odd)
            finish(2 * pair, even)
            scores_of(jnp.minimum(2 * pair + 2, heads - 1), even)
            finish(2 * pair + 1, odd)

    for z in range(4):
        pl.when(chip == z)(functools.partial(run, (z + 1) * 2 * QB))

    for fetch in fetches:
        fetch.wait()
    width = 512
    for n in range(w_all.shape[1] // width):
        cols = slice(n * width, (n + 1) * width)
        block = jnp.dot(attn[...], w_all[:, cols], preferred_element_type=F32).astype(BF16)
        for b, out in enumerate(outs):
            out[:, cols] = block[b * part : (b + 1) * part]


def attention(index, queries, pieces, w_out):
    rows = QB // 4
    length = 8 * QB
    return pl.pallas_call(
        attention_kernel,
        out_shape=[jax.ShapeDtypeStruct((rows, D), BF16)] * 4,
        in_specs=[pl.BlockSpec(memory_space=pltpu.SMEM)]
        + [pl.BlockSpec(memory_space=pltpu.HBM)] * 10,
        out_specs=vmem_specs(4),
        scratch_shapes=[
            VMEM(w_out.shape, BF16),
            VMEM(queries.shape, BF16),
            VMEM((8,) + pieces[0].shape, BF16),
            VMEM((HD, length), BF16),
            VMEM((length, 2 * HD), BF16),
            VMEM((QB, 2 * QB), F32),
            VMEM((QB, length), F32),
            VMEM((QB, length), F32),
            VMEM(queries.shape, BF16),
            pltpu.SemaphoreType.DMA,
            pltpu.SemaphoreType.DMA((8,)),
            pltpu.SemaphoreType.DMA((16,)),
        ],
        compiler_params=params(52),
        cost_estimate=CHEAP,
        name="attention",
    )(index, queries, *pieces, w_out)


def norm_kernel(index, p0, r1, r2, r3, residual, gain, state, mine, theirs, work):
    ctx = index[0]
    total = p0[...].astype(F32) + r1[...].astype(F32) + r2[...].astype(F32) + r3[...].astype(F32)
    hidden = (residual[...].astype(F32) + total).astype(BF16)
    state[...] = hidden
    wide = hidden.astype(F32)
    inv = 1.0 / jnp.sqrt(jnp.mean(wide * wide, axis=1, keepdims=True) + 1e-06)
    normed = (wide * inv * gain[...].astype(F32)).astype(BF16)
    part = D // 8
    for j in range(8):
        work[j] = normed[:, j * part : (j + 1) * part]
    for j, (a, b) in enumerate(((0, 2), (1, 3), (6, 4), (7, 5))):
        mine[:, j * part : (j + 1) * part] = work[ctx ^ a]
        theirs[:, j * part : (j + 1) * part] = work[ctx ^ b]


def norm(index, p0, r1, r2, r3, residual, gain):
    rows = residual.shape[0]
    half = jax.ShapeDtypeStruct((rows, D // 2), BF16)
    return pl.pallas_call(
        norm_kernel,
        out_shape=[jax.ShapeDtypeStruct((rows, D), BF16), half, half],
        in_specs=[pl.BlockSpec(memory_space=pltpu.SMEM)] + vmem_specs(6),
        out_specs=vmem_specs(3),
        scratch_shapes=[VMEM((8, rows, D // 8), BF16)],
        compiler_params=params(16),
        cost_estimate=CHEAP,
        name="norm",
    )(index, p0, r1, r2, r3, residual, gain)


def enter_kernel(x0, x1, x2, x3, *refs):
    weights, out, gate_all, up_all, sems = refs[:4], refs[4], refs[5], refs[6], refs[7]
    part, width = weights[0].shape[0] // 2, weights[0].shape[1]
    fetches = []
    for which, whole in enumerate((gate_all, up_all)):
        for j, array in enumerate(weights):
            source = array.at[pl.ds(which * part, part)]
            target = whole.at[pl.ds(j * part, part)]
            fetches.append(pltpu.make_async_copy(source, target, sems.at[4 * which + j]))
            fetches[-1].start()
    x = jnp.concatenate([x0[...], x1[...], x2[...], x3[...]], axis=0)
    tile = 256
    for which, whole in enumerate((gate_all, up_all)):
        for fetch in fetches[4 * which : 4 * which + 4]:
            fetch.wait()
        for n in range(width // tile):
            cols = slice(which * width + n * tile, which * width + (n + 1) * tile)
            block = jnp.dot(x, whole[:, n * tile : (n + 1) * tile], preferred_element_type=F32)
            out[:, cols] = block.astype(out.dtype)


def enter(rows, weights, kind):
    count = 4 * rows[0].shape[0]
    part, width = weights[0].shape[0] // 2, weights[0].shape[1]
    return pl.pallas_call(
        enter_kernel,
        out_shape=jax.ShapeDtypeStruct((count, 2 * width), kind),
        in_specs=vmem_specs(4) + [pl.BlockSpec(memory_space=pl.ANY)] * 4,
        out_specs=pl.BlockSpec(memory_space=VMEM),
        scratch_shapes=[
            VMEM((4 * part, width), BF16),
            VMEM((4 * part, width), BF16),
            pltpu.SemaphoreType.DMA((8,)),
        ],
        compiler_params=params(24),
        cost_estimate=CHEAP,
        name="enter",
    )(*rows, *weights)


def silu_kernel(own, other, out):
    width = out.shape[1]
    total = own[...] + other[...].astype(F32)
    gate, up = total[:, :width], total[:, width:]
    out[...] = (gate / (1.0 + jnp.exp(-gate)) * up).astype(BF16)


def silu(own, other):
    return pl.pallas_call(
        silu_kernel,
        out_shape=jax.ShapeDtypeStruct((own.shape[0], own.shape[1] // 2), BF16),
        in_specs=vmem_specs(2),
        out_specs=pl.BlockSpec(memory_space=VMEM),
        compiler_params=params(16),
        cost_estimate=CHEAP,
        name="silu",
    )(own, other)


def leave_kernel(hidden, d0, d1, d2, d3, y0, y1, y2, y3, down_all, sems):
    part = y0.shape[0]
    width = d0.shape[1]
    fetches = []
    for j, array in enumerate((d0, d1, d2, d3)):
        fetches.append(pltpu.make_async_copy(array, down_all.at[j], sems.at[j]))
        fetches[-1].start()
    for j in range(4):
        fetches[j].wait()
        block = jnp.dot(hidden[...], down_all[j], preferred_element_type=F32).astype(BF16)
        for b, out in enumerate((y0, y1, y2, y3)):
            out[:, j * width : (j + 1) * width] = block[b * part : (b + 1) * part]


def leave(hidden, downs):
    part = jax.ShapeDtypeStruct((hidden.shape[0] // 4, 4 * downs[0].shape[1]), BF16)
    return pl.pallas_call(
        leave_kernel,
        out_shape=[part] * 4,
        in_specs=vmem_specs(1) + [pl.BlockSpec(memory_space=pl.ANY)] * 4,
        out_specs=vmem_specs(4),
        scratch_shapes=[VMEM((4,) + downs[0].shape, BF16), pltpu.SemaphoreType.DMA((4,))],
        compiler_params=params(16),
        cost_estimate=CHEAP,
        name="leave",
    )(hidden, *downs)


def mixed(shares, parts):
    total = shares[:, :1] * parts[0][...].astype(F32)
    for b in range(1, 4):
        total = total + shares[:, b : b + 1] * parts[b][...].astype(F32)
    return total


def final_kernel(index, state, shares, y0, r1, r2, r3, other, out):
    ctx = index[0]
    part = D // 8
    own = mixed(shares, (y0, r1, r2, r3))
    for j, (a, b) in enumerate(((0, 2), (1, 3), (6, 4), (7, 5))):
        cols = slice(j * part, (j + 1) * part)
        here = pl.ds(pl.multiple_of((ctx ^ a) * part, part), part)
        out[:, here] = (state[:, here].astype(F32) + own[:, cols]).astype(BF16)
        there = pl.ds(pl.multiple_of((ctx ^ b) * part, part), part)
        out[:, there] = (state[:, there].astype(F32) + other[:, cols].astype(F32)).astype(BF16)


def final(index, state, shares, y0, r1, r2, r3, other):
    return pl.pallas_call(
        final_kernel,
        out_shape=jax.ShapeDtypeStruct(state.shape, BF16),
        in_specs=[pl.BlockSpec(memory_space=pltpu.SMEM)] + vmem_specs(7),
        out_specs=pl.BlockSpec(memory_space=VMEM),
        compiler_params=params(16),
        cost_estimate=CHEAP,
        name="final",
    )(index, state, shares, y0, r1, r2, r3, other)


def body(
    queries,
    keys,
    values,
    w_out,
    residual,
    norm_gain,
    expert_ids,
    gate_weights,
    w_gate,
    w_up,
    w_down,
):
    exp = lax.axis_index("exp")
    ctx = lax.axis_index("ctx")
    index = jnp.stack([ctx, exp]).astype(jnp.int32)
    kv_first = exp * (HQ // 4) // (HQ // KVH) * HD
    kv_here = jnp.concatenate(
        [
            lax.dynamic_slice_in_dim(keys, kv_first, HD, 1),
            lax.dynamic_slice_in_dim(values, kv_first, HD, 1),
        ],
        axis=1,
    )
    def later(array, chips):
        return lax.ppermute(array, "ctx", [(i, i + 2 * chips) for i in range(8 - 2 * chips)])

    kv_here, gate_here, up_here = lax.optimization_barrier((kv_here, w_gate[0], w_up[0]))
    moved = [later(kv_here, d) for d in (3, 2, 1)][::-1]
    pair_here, down_here = jnp.concatenate([gate_here, up_here], axis=0), w_down[0]
    pieces = [part for piece in [kv_here] + moved for part in (piece, swap(piece, "ctx", 1))]
    pieces, pair_here = lax.optimization_barrier((pieces, pair_here))
    pair_far = swap(pair_here, "ctx", 6)

    lane = lax.broadcasted_iota(jnp.int32, (expert_ids.shape[0], HD), 1)
    shares = jnp.zeros(lane.shape, F32)
    for k in range(expert_ids.shape[1]):
        named = expert_ids[:, k : k + 1] ^ exp
        shares = shares + jnp.where(lane == named, gate_weights[:, k : k + 1], 0.0)

    p = attention(index, queries, pieces, w_out)
    p, shares, pair_near, down_here = lax.optimization_barrier(
        (p, shares, swap(pair_here, "ctx", 1), down_here)
    )
    r = [swap(p[b], "exp", b) for b in (1, 2, 3)]
    down_near = swap(down_here, "ctx", 1)
    other_shares = swap(shares, "ctx", 2)
    state, mine, theirs = norm(index, p[0], *r, residual, norm_gain.reshape(1, D))
    others = swap(theirs, "ctx", 2)
    own_rows = [mine] + [swap(mine, "exp", b) for b in (1, 2, 3)]
    others, own_rows[1:3] = lax.optimization_barrier((others, own_rows[1:3]))
    other_rows = [others] + [swap(others, "exp", b) for b in (1, 2, 3)]
    own_rows, other_rows[1:3], pair_far, down_here = lax.optimization_barrier(
        (own_rows, other_rows[1:3], pair_far, down_here)
    )
    down_far = swap(down_here, "ctx", 6)
    pairs = (pair_here, pair_near, pair_far, swap(pair_far, "ctx", 1))
    other_pre = enter(other_rows, pairs, BF16)
    from_other = swap(other_pre, "ctx", 2)
    own_pre = enter(own_rows, pairs, F32)
    own_pre, down_far = lax.optimization_barrier((own_pre, down_far))
    own_hidden = silu(own_pre, from_other)
    other_hidden = swap(own_hidden, "ctx", 2)
    downs = (down_here, down_near, down_far, swap(down_far, "ctx", 1))
    y = leave(own_hidden, downs)
    own_parts = [y[0]] + [swap(y[b], "exp", b) for b in (1, 2, 3)]
    other_hidden, *own_parts[1:3] = lax.optimization_barrier((other_hidden, *own_parts[1:3]))
    z = leave(other_hidden, downs)
    other_parts = [z[0]] + [swap(z[b], "exp", b) for b in (1, 2, 3)]
    back = swap(mixed(other_shares, other_parts).astype(BF16), "ctx", 2)
    return final(index, state, shares, *own_parts, back)


def solution(mesh):
    placed = (
        P("ctx", "exp"),
        P("ctx", None),
        P("ctx", None),
        P("exp", None),
        P(("ctx", "exp"), None),
        P(),
        P(("ctx", "exp"), None),
        P(("ctx", "exp"), None),
        P("exp", "ctx", None),
        P("exp", "ctx", None),
        P("exp", None, "ctx"),
    )
    shape = dict(mesh.shape)
    small = shape["ctx"] == 8 and shape["exp"] == 4
    return jax.shard_map(
        body if small else general_body, mesh=mesh, in_specs=placed, out_specs=P(("ctx", "exp"), None), check_vma=False
    )
```

```python
import functools
import math

import jax
import jax.numpy as jnp
from jax import lax
from jax.experimental import pallas as pl
from jax.experimental.pallas import tpu as pltpu
from jax.sharding import PartitionSpec as P

D = 4096
HQ = 64
KVH = 4
HD = 128


def general_body(
    queries,
    keys,
    values,
    w_out,
    residual,
    norm_gain,
    expert_ids,
    gate_weights,
    w_gate,
    w_up,
    w_down,
):
    tok_rows = queries.shape[0]
    half_rows = tok_rows // 2
    exp_count = lax.axis_size("exp")
    heads_here = HQ // exp_count
    group = HQ // KVH
    kv_here = max(1, heads_here // group)
    heads_per_kv = heads_here // kv_here
    exp_index = lax.axis_index("exp")
    ctx_index = lax.axis_index("ctx")
    kv_first = exp_index * heads_here // group
    key_cols = lax.dynamic_slice_in_dim(keys, kv_first * HD, kv_here * HD, 1)
    value_cols = lax.dynamic_slice_in_dim(values, kv_first * HD, kv_here * HD, 1)
    scale = 1.0 / math.sqrt(HD)
    first_rows = queries[:half_rows]
    second_rows = queries[half_rows:]
    first_start = ctx_index * tok_rows
    second_start = ctx_index * tok_rows + half_rows
    query_sets = (
        first_rows.reshape(half_rows, kv_here, heads_per_kv, HD),
        second_rows.reshape(half_rows, kv_here, heads_per_kv, HD),
    )
    query_positions = (
        first_start + jnp.arange(half_rows, dtype=jnp.int32),
        second_start + jnp.arange(half_rows, dtype=jnp.int32),
    )
    last_positions = (first_start + half_rows - 1, second_start + half_rows - 1)

    def block_update(carry, query_four, query_pos, key_block, value_block, key_start):
        run_max, run_sum, run_acc = carry
        width = key_block.shape[0]
        key_three = key_block.reshape(width, kv_here, HD)
        value_three = value_block.reshape(width, kv_here, HD)
        scores = (
            jnp.einsum("tghd,kgd->ghtk", query_four, key_three, preferred_element_type=jnp.float32)
            * scale
        )
        key_pos = key_start + jnp.arange(width, dtype=jnp.int32)
        allowed = key_pos[None, :] <= query_pos[:, None]
        scores = jnp.where(allowed, scores, -1e30)
        new_max = jnp.maximum(run_max, jnp.max(scores, axis=-1))
        probs = jnp.where(allowed, jnp.exp(scores - new_max[..., None]), 0.0)
        factor = jnp.exp(run_max - new_max)
        run_sum = run_sum * factor + jnp.sum(probs, axis=-1)
        weighted = jnp.einsum(
            "ghtk,kgd->ghtd",
            probs.astype(jnp.bfloat16),
            value_three,
            preferred_element_type=jnp.float32,
        )
        run_acc = run_acc * factor[..., None] + weighted
        return (new_max, run_sum, run_acc)

    start_max = jnp.full((kv_here, heads_per_kv, half_rows), -1e30, jnp.float32)
    start_sum = jnp.zeros((kv_here, heads_per_kv, half_rows), jnp.float32)
    start_acc = jnp.zeros((kv_here, heads_per_kv, half_rows, HD), jnp.float32)
    start_state = (start_max, start_sum, start_acc)
    key_piece = lax.all_gather(key_cols, "ctx", axis=0, tiled=True)
    value_piece = lax.all_gather(value_cols, "ctx", axis=0, tiled=True)
    count = key_piece.shape[0]
    width = 512

    def one_block(index, inner):
        key_start = index * width
        key_block = lax.dynamic_slice_in_dim(key_piece, key_start, width, 0)
        value_block = lax.dynamic_slice_in_dim(value_piece, key_start, width, 0)
        updated = []
        for which in range(2):
            query_four = query_sets[which]
            query_pos = query_positions[which]
            updated.append(
                lax.cond(
                    key_start > last_positions[which],
                    lambda state: state,
                    lambda state: block_update(
                        state, query_four, query_pos, key_block, value_block, key_start
                    ),
                    inner[which],
                )
            )
        return (updated[0], updated[1])

    states = lax.fori_loop(0, count // width, one_block, (start_state, start_state))
    halves = []
    for which in range(2):
        run_max, run_sum, run_acc = states[which]
        halves.append(
            jnp.transpose(run_acc / run_sum[..., None], (2, 0, 1, 3))
            .reshape(half_rows, heads_here * HD)
            .astype(jnp.bfloat16)
        )
    attn_second = halves[1]
    attn = jnp.concatenate([halves[0], attn_second], axis=0)
    projected = lax.psum_scatter(
        jnp.dot(attn, w_out, preferred_element_type=jnp.float32).astype(jnp.bfloat16),
        "exp",
        scatter_dimension=0,
        tiled=True,
    ).astype(jnp.float32)
    hidden_state = (residual.astype(jnp.float32) + projected).astype(jnp.bfloat16)
    state_f = hidden_state.astype(jnp.float32)
    inv_rms = 1.0 / jnp.sqrt(jnp.mean(state_f * state_f, axis=1, keepdims=True) + 1e-06)
    normed = (state_f * inv_rms * norm_gain.astype(jnp.float32)[None, :]).astype(jnp.bfloat16)
    rows_here = expert_ids.shape[0]
    top_count = expert_ids.shape[1]
    experts_all = w_gate.shape[0] * exp_count
    capacity = min(rows_here, 2 * rows_here * top_count // experts_all)
    flat_ids = expert_ids.reshape(-1)
    onehot = (flat_ids[:, None] == jnp.arange(experts_all, dtype=jnp.int32)[None, :]).astype(
        jnp.int32
    )
    earlier = jnp.cumsum(onehot, axis=0) - onehot
    slot_index = jnp.sum(earlier * onehot, axis=1)
    target = flat_ids * capacity + slot_index
    picks = target[:, None] == jnp.arange(experts_all * capacity, dtype=jnp.int32)[None, :]
    dispatch_table = jnp.any(
        picks.reshape(rows_here, top_count, experts_all * capacity), axis=1
    ).astype(jnp.bfloat16)
    outgoing = jnp.einsum(
        "rs,rd->sd", dispatch_table, normed, preferred_element_type=jnp.float32
    ).astype(jnp.bfloat16)
    arrived = lax.all_to_all(
        outgoing.reshape(experts_all, capacity, D), "exp", split_axis=0, concat_axis=0, tiled=True
    )
    slot_rows = arrived.reshape(experts_all * capacity, D)
    gate_local = w_gate[0]
    up_local = w_up[0]
    gate_pre = jnp.dot(
        slot_rows,
        lax.all_gather(gate_local, "ctx", axis=0, tiled=True),
        preferred_element_type=jnp.float32,
    )
    up_pre = jnp.dot(
        slot_rows,
        lax.all_gather(up_local, "ctx", axis=0, tiled=True),
        preferred_element_type=jnp.float32,
    )
    expert_hidden = (jax.nn.silu(gate_pre) * up_pre).astype(jnp.bfloat16)
    down_local = w_down[0]
    expert_result = jnp.dot(
        expert_hidden,
        lax.all_gather(down_local, "ctx", axis=1, tiled=True),
        preferred_element_type=jnp.float32,
    ).astype(jnp.bfloat16)
    returned = lax.all_to_all(
        expert_result.reshape(experts_all, capacity, D),
        "exp",
        split_axis=0,
        concat_axis=0,
        tiled=True,
    )
    returned_flat = returned.reshape(experts_all * capacity, D)
    picked = jnp.dot(picks.astype(jnp.bfloat16), returned_flat, preferred_element_type=jnp.float32)
    weighted = gate_weights[:, :, None] * picked.reshape(rows_here, top_count, D)
    return (state_f + jnp.sum(weighted, axis=1)).astype(jnp.bfloat16)


BF16 = jnp.bfloat16
F32 = jnp.float32
VMEM = pltpu.VMEM
QB = 256
CHEAP = pl.CostEstimate(flops=1000, bytes_accessed=1000, transcendentals=0)


def swap(array, axis, mask):
    size = lax.axis_size(axis)
    return lax.ppermute(array, axis, [(i, i ^ mask) for i in range(size)])


def params(mib):
    return pltpu.CompilerParams(vmem_limit_bytes=mib * 1024 * 1024)


def vmem_specs(count):
    return [pl.BlockSpec(memory_space=VMEM) for _ in range(count)]


def attention_kernel(index, q_hbm, *refs):
    arrived, w_hbm, outs = refs[:8], refs[8], refs[9:13]
    w_all, q, pieces, keys, ones_values, bias, even, odd, attn, q_sem, piece_sems, sems = refs[13:]
    q_fetch = pltpu.make_async_copy(q_hbm, q, q_sem)
    piece_fetches = [
        pltpu.make_async_copy(arrived[i], pieces.at[i], piece_sems.at[i]) for i in range(8)
    ]
    for fetch in piece_fetches + [q_fetch]:
        fetch.start()
    ctx = index[0]
    exp = index[1]
    chip = ctx // 2
    steps = sems.shape[0]
    depth = w_all.shape[0] // steps
    fetches = [
        pltpu.make_async_copy(
            w_hbm.at[pl.ds(i * depth, depth)], w_all.at[pl.ds(i * depth, depth)], sems.at[i]
        )
        for i in range(steps)
    ]
    factor = math.log2(math.e) / math.sqrt(HD)
    heads = q.shape[1] // HD
    ones_values[:, HD:] = jnp.ones((ones_values.shape[0], HD), BF16)
    core = ctx % 2
    row = lax.broadcasted_iota(jnp.int32, (QB, 2 * QB), 0) + core * QB
    col = lax.broadcasted_iota(jnp.int32, (QB, 2 * QB), 1)
    bias[...] = jnp.where(col <= row, 0.0, -1e30)
    for fetch in piece_fetches:
        fetch.wait()
    for d in range(4):

        @pl.when(chip >= d)
        def _():
            for other in range(2):
                piece = pieces.at[2 * d + other]
                place = 2 * (chip - d) + (core ^ other)
                here = pl.ds(pl.multiple_of(place * QB, QB), QB)
                keys[:, here] = piece[:, :HD].astype(F32).T.astype(BF16)
                ones_values[here, :HD] = piece[:, HD:]

    q_fetch.wait()
    for fetch in fetches:
        fetch.start()
    part = QB // 4

    def run(length):
        def scores_of(h, store):
            rows = q[:, pl.ds(pl.multiple_of(h * HD, HD), HD)]
            block = jnp.dot(rows, keys[:, :length], preferred_element_type=F32)
            last = length - 2 * QB
            if last:
                store[:, :last] = block[:, :last]
            store[:, last:length] = block[:, last:] + bias[...]

        def finish(h, store):
            block = store[:, :length]
            top = jnp.max(block, axis=1, keepdims=True) * factor
            probs = jnp.exp2(block * factor - top).astype(BF16)
            total = jnp.dot(probs, ones_values[:length, :], preferred_element_type=F32)
            done = (total[:, :HD] / total[:, HD:]).astype(BF16)
            cols = pl.ds(pl.multiple_of(h * HD, HD), HD)
            for i in range(4):
                start = pl.multiple_of((exp ^ i) * part, part)
                attn[pl.ds(start, part), cols] = done[i * part : (i + 1) * part]

        scores_of(0, even)

        @pl.loop(0, heads // 2)
        def _(pair):
            scores_of(2 * pair + 1, odd)
            finish(2 * pair, even)
            scores_of(jnp.minimum(2 * pair + 2, heads - 1), even)
            finish(2 * pair + 1, odd)

    for z in range(4):
        pl.when(chip == z)(functools.partial(run, (z + 1) * 2 * QB))

    for fetch in fetches:
        fetch.wait()
    width = 512
    for n in range(w_all.shape[1] // width):
        cols = slice(n * width, (n + 1) * width)
        block = jnp.dot(attn[...], w_all[:, cols], preferred_element_type=F32).astype(BF16)
        for b, out in enumerate(outs):
            out[:, cols] = block[b * part : (b + 1) * part]


def attention(index, queries, pieces, w_out):
    rows = QB // 4
    length = 8 * QB
    return pl.pallas_call(
        attention_kernel,
        out_shape=[jax.ShapeDtypeStruct((rows, D), BF16)] * 4,
        in_specs=[pl.BlockSpec(memory_space=pltpu.SMEM)]
        + [pl.BlockSpec(memory_space=pltpu.HBM)] * 10,
        out_specs=vmem_specs(4),
        scratch_shapes=[
            VMEM(w_out.shape, BF16),
            VMEM(queries.shape, BF16),
            VMEM((8,) + pieces[0].shape, BF16),
            VMEM((HD, length), BF16),
            VMEM((length, 2 * HD), BF16),
            VMEM((QB, 2 * QB), F32),
            VMEM((QB, length), F32),
            VMEM((QB, length), F32),
            VMEM(queries.shape, BF16),
            pltpu.SemaphoreType.DMA,
            pltpu.SemaphoreType.DMA((8,)),
            pltpu.SemaphoreType.DMA((16,)),
        ],
        compiler_params=params(52),
        cost_estimate=CHEAP,
        name="attention",
    )(index, queries, *pieces, w_out)


def norm_kernel(index, p0, r1, r2, r3, residual, gain, state, mine, theirs, work):
    ctx = index[0]
    total = p0[...].astype(F32) + r1[...].astype(F32) + r2[...].astype(F32) + r3[...].astype(F32)
    hidden = (residual[...].astype(F32) + total).astype(BF16)
    state[...] = hidden
    wide = hidden.astype(F32)
    inv = 1.0 / jnp.sqrt(jnp.mean(wide * wide, axis=1, keepdims=True) + 1e-06)
    normed = (wide * inv * gain[...].astype(F32)).astype(BF16)
    part = D // 8
    for j in range(8):
        work[j] = normed[:, j * part : (j + 1) * part]
    for j, (a, b) in enumerate(((0, 2), (1, 3), (6, 4), (7, 5))):
        mine[:, j * part : (j + 1) * part] = work[ctx ^ a]
        theirs[:, j * part : (j + 1) * part] = work[ctx ^ b]


def norm(index, p0, r1, r2, r3, residual, gain):
    rows = residual.shape[0]
    half = jax.ShapeDtypeStruct((rows, D // 2), BF16)
    return pl.pallas_call(
        norm_kernel,
        out_shape=[jax.ShapeDtypeStruct((rows, D), BF16), half, half],
        in_specs=[pl.BlockSpec(memory_space=pltpu.SMEM)] + vmem_specs(6),
        out_specs=vmem_specs(3),
        scratch_shapes=[VMEM((8, rows, D // 8), BF16)],
        compiler_params=params(16),
        cost_estimate=CHEAP,
        name="norm",
    )(index, p0, r1, r2, r3, residual, gain)


def enter_kernel(x0, x1, x2, x3, *refs):
    weights, out, gate_all, up_all, sems = refs[:4], refs[4], refs[5], refs[6], refs[7]
    part, width = weights[0].shape[0] // 2, weights[0].shape[1]
    fetches = []
    for which, whole in enumerate((gate_all, up_all)):
        for j, array in enumerate(weights):
            source = array.at[pl.ds(which * part, part)]
            target = whole.at[pl.ds(j * part, part)]
            fetches.append(pltpu.make_async_copy(source, target, sems.at[4 * which + j]))
            fetches[-1].start()
    x = jnp.concatenate([x0[...], x1[...], x2[...], x3[...]], axis=0)
    tile = 256
    for which, whole in enumerate((gate_all, up_all)):
        for fetch in fetches[4 * which : 4 * which + 4]:
            fetch.wait()
        for n in range(width // tile):
            cols = slice(which * width + n * tile, which * width + (n + 1) * tile)
            block = jnp.dot(x, whole[:, n * tile : (n + 1) * tile], preferred_element_type=F32)
            out[:, cols] = block.astype(out.dtype)


def enter(rows, weights, kind):
    count = 4 * rows[0].shape[0]
    part, width = weights[0].shape[0] // 2, weights[0].shape[1]
    return pl.pallas_call(
        enter_kernel,
        out_shape=jax.ShapeDtypeStruct((count, 2 * width), kind),
        in_specs=vmem_specs(4) + [pl.BlockSpec(memory_space=pl.ANY)] * 4,
        out_specs=pl.BlockSpec(memory_space=VMEM),
        scratch_shapes=[
            VMEM((4 * part, width), BF16),
            VMEM((4 * part, width), BF16),
            pltpu.SemaphoreType.DMA((8,)),
        ],
        compiler_params=params(24),
        cost_estimate=CHEAP,
        name="enter",
    )(*rows, *weights)


def silu_kernel(own, other, out):
    width = out.shape[1]
    total = own[...] + other[...].astype(F32)
    gate, up = total[:, :width], total[:, width:]
    out[...] = (gate / (1.0 + jnp.exp(-gate)) * up).astype(BF16)


def silu(own, other):
    return pl.pallas_call(
        silu_kernel,
        out_shape=jax.ShapeDtypeStruct((own.shape[0], own.shape[1] // 2), BF16),
        in_specs=vmem_specs(2),
        out_specs=pl.BlockSpec(memory_space=VMEM),
        compiler_params=params(16),
        cost_estimate=CHEAP,
        name="silu",
    )(own, other)


def leave_kernel(hidden, d0, d1, d2, d3, y0, y1, y2, y3, down_all, sems):
    part = y0.shape[0]
    width = d0.shape[1]
    fetches = []
    for j, array in enumerate((d0, d1, d2, d3)):
        fetches.append(pltpu.make_async_copy(array, down_all.at[j], sems.at[j]))
        fetches[-1].start()
    for j in range(4):
        fetches[j].wait()
        block = jnp.dot(hidden[...], down_all[j], preferred_element_type=F32).astype(BF16)
        for b, out in enumerate((y0, y1, y2, y3)):
            out[:, j * width : (j + 1) * width] = block[b * part : (b + 1) * part]


def leave(hidden, downs):
    part = jax.ShapeDtypeStruct((hidden.shape[0] // 4, 4 * downs[0].shape[1]), BF16)
    return pl.pallas_call(
        leave_kernel,
        out_shape=[part] * 4,
        in_specs=vmem_specs(1) + [pl.BlockSpec(memory_space=pl.ANY)] * 4,
        out_specs=vmem_specs(4),
        scratch_shapes=[VMEM((4,) + downs[0].shape, BF16), pltpu.SemaphoreType.DMA((4,))],
        compiler_params=params(16),
        cost_estimate=CHEAP,
        name="leave",
    )(hidden, *downs)


def mixed(shares, parts):
    total = shares[:, :1] * parts[0][...].astype(F32)
    for b in range(1, 4):
        total = total + shares[:, b : b + 1] * parts[b][...].astype(F32)
    return total


def final_kernel(index, state, shares, y0, r1, r2, r3, other, out):
    ctx = index[0]
    part = D // 8
    own = mixed(shares, (y0, r1, r2, r3))
    for j, (a, b) in enumerate(((0, 2), (1, 3), (6, 4), (7, 5))):
        cols = slice(j * part, (j + 1) * part)
        here = pl.ds(pl.multiple_of((ctx ^ a) * part, part), part)
        out[:, here] = (state[:, here].astype(F32) + own[:, cols]).astype(BF16)
        there = pl.ds(pl.multiple_of((ctx ^ b) * part, part), part)
        out[:, there] = (state[:, there].astype(F32) + other[:, cols].astype(F32)).astype(BF16)


def final(index, state, shares, y0, r1, r2, r3, other):
    return pl.pallas_call(
        final_kernel,
        out_shape=jax.ShapeDtypeStruct(state.shape, BF16),
        in_specs=[pl.BlockSpec(memory_space=pltpu.SMEM)] + vmem_specs(7),
        out_specs=pl.BlockSpec(memory_space=VMEM),
        compiler_params=params(16),
        cost_estimate=CHEAP,
        name="final",
    )(index, state, shares, y0, r1, r2, r3, other)


def body(
    queries,
    keys,
    values,
    w_out,
    residual,
    norm_gain,
    expert_ids,
    gate_weights,
    w_gate,
    w_up,
    w_down,
):
    exp = lax.axis_index("exp")
    ctx = lax.axis_index("ctx")
    index = jnp.stack([ctx, exp]).astype(jnp.int32)
    kv_first = exp * (HQ // 4) // (HQ // KVH) * HD
    kv_here = jnp.concatenate(
        [
            lax.dynamic_slice_in_dim(keys, kv_first, HD, 1),
            lax.dynamic_slice_in_dim(values, kv_first, HD, 1),
        ],
        axis=1,
    )
    def later(array, chips):
        return lax.ppermute(array, "ctx", [(i, i + 2 * chips) for i in range(8 - 2 * chips)])

    kv_here, gate_here, up_here = lax.optimization_barrier((kv_here, w_gate[0], w_up[0]))
    moved = [later(kv_here, d) for d in (3, 2, 1)][::-1]
    pair_here, down_here = jnp.concatenate([gate_here, up_here], axis=0), w_down[0]
    pieces = [part for piece in [kv_here] + moved for part in (piece, swap(piece, "ctx", 1))]
    pieces, pair_here = lax.optimization_barrier((pieces, pair_here))
    pair_far = swap(pair_here, "ctx", 6)

    lane = lax.broadcasted_iota(jnp.int32, (expert_ids.shape[0], HD), 1)
    shares = jnp.zeros(lane.shape, F32)
    for k in range(expert_ids.shape[1]):
        named = expert_ids[:, k : k + 1] ^ exp
        shares = shares + jnp.where(lane == named, gate_weights[:, k : k + 1], 0.0)

    p = attention(index, queries, pieces, w_out)
    p, shares, pair_here, down_here = lax.optimization_barrier((p, shares, pair_here, down_here))
    r = [swap(p[b], "exp", b) for b in (1, 2, 3)]
    pair_near, down_near = swap(pair_here, "ctx", 1), swap(down_here, "ctx", 1)
    other_shares = swap(shares, "ctx", 2)
    state, mine, theirs = norm(index, p[0], *r, residual, norm_gain.reshape(1, D))
    others = swap(theirs, "ctx", 2)
    own_rows = [mine] + [swap(mine, "exp", b) for b in (1, 2, 3)]
    other_rows = [others] + [swap(others, "exp", b) for b in (1, 2, 3)]
    own_rows, others, pair_far, down_here = lax.optimization_barrier(
        (own_rows, others, pair_far, down_here)
    )
    down_far = swap(down_here, "ctx", 6)
    pairs = (pair_here, pair_near, pair_far, swap(pair_far, "ctx", 1))
    other_pre = enter(other_rows, pairs, BF16)
    from_other = swap(other_pre, "ctx", 2)
    own_pre = enter(own_rows, pairs, F32)
    own_pre, down_far = lax.optimization_barrier((own_pre, down_far))
    own_hidden = silu(own_pre, from_other)
    other_hidden = swap(own_hidden, "ctx", 2)
    downs = (down_here, down_near, down_far, swap(down_far, "ctx", 1))
    y = leave(own_hidden, downs)
    own_parts = [y[0]] + [swap(y[b], "exp", b) for b in (1, 2, 3)]
    other_hidden, *own_parts[1:3] = lax.optimization_barrier((other_hidden, *own_parts[1:3]))
    z = leave(other_hidden, downs)
    other_parts = [z[0]] + [swap(z[b], "exp", b) for b in (1, 2, 3)]
    back = swap(mixed(other_shares, other_parts).astype(BF16), "ctx", 2)
    return final(index, state, shares, *own_parts, back)


def solution(mesh):
    placed = (
        P("ctx", "exp"),
        P("ctx", None),
        P("ctx", None),
        P("exp", None),
        P(("ctx", "exp"), None),
        P(),
        P(("ctx", "exp"), None),
        P(("ctx", "exp"), None),
        P("exp", "ctx", None),
        P("exp", "ctx", None),
        P("exp", None, "ctx"),
    )
    shape = dict(mesh.shape)
    small = shape["ctx"] == 8 and shape["exp"] == 4
    return jax.shard_map(
        body if small else general_body, mesh=mesh, in_specs=placed, out_specs=P(("ctx", "exp"), None), check_vma=False
    )
```

```python
import functools
import math

import jax
import jax.numpy as jnp
from jax import lax
from jax.experimental import pallas as pl
from jax.experimental.pallas import tpu as pltpu
from jax.sharding import PartitionSpec as P

D = 4096
HQ = 64
KVH = 4
HD = 128


def general_body(
    queries,
    keys,
    values,
    w_out,
    residual,
    norm_gain,
    expert_ids,
    gate_weights,
    w_gate,
    w_up,
    w_down,
):
    tok_rows = queries.shape[0]
    half_rows = tok_rows // 2
    exp_count = lax.axis_size("exp")
    heads_here = HQ // exp_count
    group = HQ // KVH
    kv_here = max(1, heads_here // group)
    heads_per_kv = heads_here // kv_here
    exp_index = lax.axis_index("exp")
    ctx_index = lax.axis_index("ctx")
    kv_first = exp_index * heads_here // group
    key_cols = lax.dynamic_slice_in_dim(keys, kv_first * HD, kv_here * HD, 1)
    value_cols = lax.dynamic_slice_in_dim(values, kv_first * HD, kv_here * HD, 1)
    scale = 1.0 / math.sqrt(HD)
    first_rows = queries[:half_rows]
    second_rows = queries[half_rows:]
    first_start = ctx_index * tok_rows
    second_start = ctx_index * tok_rows + half_rows
    query_sets = (
        first_rows.reshape(half_rows, kv_here, heads_per_kv, HD),
        second_rows.reshape(half_rows, kv_here, heads_per_kv, HD),
    )
    query_positions = (
        first_start + jnp.arange(half_rows, dtype=jnp.int32),
        second_start + jnp.arange(half_rows, dtype=jnp.int32),
    )
    last_positions = (first_start + half_rows - 1, second_start + half_rows - 1)

    def block_update(carry, query_four, query_pos, key_block, value_block, key_start):
        run_max, run_sum, run_acc = carry
        width = key_block.shape[0]
        key_three = key_block.reshape(width, kv_here, HD)
        value_three = value_block.reshape(width, kv_here, HD)
        scores = (
            jnp.einsum("tghd,kgd->ghtk", query_four, key_three, preferred_element_type=jnp.float32)
            * scale
        )
        key_pos = key_start + jnp.arange(width, dtype=jnp.int32)
        allowed = key_pos[None, :] <= query_pos[:, None]
        scores = jnp.where(allowed, scores, -1e30)
        new_max = jnp.maximum(run_max, jnp.max(scores, axis=-1))
        probs = jnp.where(allowed, jnp.exp(scores - new_max[..., None]), 0.0)
        factor = jnp.exp(run_max - new_max)
        run_sum = run_sum * factor + jnp.sum(probs, axis=-1)
        weighted = jnp.einsum(
            "ghtk,kgd->ghtd",
            probs.astype(jnp.bfloat16),
            value_three,
            preferred_element_type=jnp.float32,
        )
        run_acc = run_acc * factor[..., None] + weighted
        return (new_max, run_sum, run_acc)

    start_max = jnp.full((kv_here, heads_per_kv, half_rows), -1e30, jnp.float32)
    start_sum = jnp.zeros((kv_here, heads_per_kv, half_rows), jnp.float32)
    start_acc = jnp.zeros((kv_here, heads_per_kv, half_rows, HD), jnp.float32)
    start_state = (start_max, start_sum, start_acc)
    key_piece = lax.all_gather(key_cols, "ctx", axis=0, tiled=True)
    value_piece = lax.all_gather(value_cols, "ctx", axis=0, tiled=True)
    count = key_piece.shape[0]
    width = 512

    def one_block(index, inner):
        key_start = index * width
        key_block = lax.dynamic_slice_in_dim(key_piece, key_start, width, 0)
        value_block = lax.dynamic_slice_in_dim(value_piece, key_start, width, 0)
        updated = []
        for which in range(2):
            query_four = query_sets[which]
            query_pos = query_positions[which]
            updated.append(
                lax.cond(
                    key_start > last_positions[which],
                    lambda state: state,
                    lambda state: block_update(
                        state, query_four, query_pos, key_block, value_block, key_start
                    ),
                    inner[which],
                )
            )
        return (updated[0], updated[1])

    states = lax.fori_loop(0, count // width, one_block, (start_state, start_state))
    halves = []
    for which in range(2):
        run_max, run_sum, run_acc = states[which]
        halves.append(
            jnp.transpose(run_acc / run_sum[..., None], (2, 0, 1, 3))
            .reshape(half_rows, heads_here * HD)
            .astype(jnp.bfloat16)
        )
    attn_second = halves[1]
    attn = jnp.concatenate([halves[0], attn_second], axis=0)
    projected = lax.psum_scatter(
        jnp.dot(attn, w_out, preferred_element_type=jnp.float32).astype(jnp.bfloat16),
        "exp",
        scatter_dimension=0,
        tiled=True,
    ).astype(jnp.float32)
    hidden_state = (residual.astype(jnp.float32) + projected).astype(jnp.bfloat16)
    state_f = hidden_state.astype(jnp.float32)
    inv_rms = 1.0 / jnp.sqrt(jnp.mean(state_f * state_f, axis=1, keepdims=True) + 1e-06)
    normed = (state_f * inv_rms * norm_gain.astype(jnp.float32)[None, :]).astype(jnp.bfloat16)
    rows_here = expert_ids.shape[0]
    top_count = expert_ids.shape[1]
    experts_all = w_gate.shape[0] * exp_count
    capacity = min(rows_here, 2 * rows_here * top_count // experts_all)
    flat_ids = expert_ids.reshape(-1)
    onehot = (flat_ids[:, None] == jnp.arange(experts_all, dtype=jnp.int32)[None, :]).astype(
        jnp.int32
    )
    earlier = jnp.cumsum(onehot, axis=0) - onehot
    slot_index = jnp.sum(earlier * onehot, axis=1)
    target = flat_ids * capacity + slot_index
    picks = target[:, None] == jnp.arange(experts_all * capacity, dtype=jnp.int32)[None, :]
    dispatch_table = jnp.any(
        picks.reshape(rows_here, top_count, experts_all * capacity), axis=1
    ).astype(jnp.bfloat16)
    outgoing = jnp.einsum(
        "rs,rd->sd", dispatch_table, normed, preferred_element_type=jnp.float32
    ).astype(jnp.bfloat16)
    arrived = lax.all_to_all(
        outgoing.reshape(experts_all, capacity, D), "exp", split_axis=0, concat_axis=0, tiled=True
    )
    slot_rows = arrived.reshape(experts_all * capacity, D)
    gate_local = w_gate[0]
    up_local = w_up[0]
    gate_pre = jnp.dot(
        slot_rows,
        lax.all_gather(gate_local, "ctx", axis=0, tiled=True),
        preferred_element_type=jnp.float32,
    )
    up_pre = jnp.dot(
        slot_rows,
        lax.all_gather(up_local, "ctx", axis=0, tiled=True),
        preferred_element_type=jnp.float32,
    )
    expert_hidden = (jax.nn.silu(gate_pre) * up_pre).astype(jnp.bfloat16)
    down_local = w_down[0]
    expert_result = jnp.dot(
        expert_hidden,
        lax.all_gather(down_local, "ctx", axis=1, tiled=True),
        preferred_element_type=jnp.float32,
    ).astype(jnp.bfloat16)
    returned = lax.all_to_all(
        expert_result.reshape(experts_all, capacity, D),
        "exp",
        split_axis=0,
        concat_axis=0,
        tiled=True,
    )
    returned_flat = returned.reshape(experts_all * capacity, D)
    picked = jnp.dot(picks.astype(jnp.bfloat16), returned_flat, preferred_element_type=jnp.float32)
    weighted = gate_weights[:, :, None] * picked.reshape(rows_here, top_count, D)
    return (state_f + jnp.sum(weighted, axis=1)).astype(jnp.bfloat16)


BF16 = jnp.bfloat16
F32 = jnp.float32
VMEM = pltpu.VMEM
QB = 256
CHEAP = pl.CostEstimate(flops=1000, bytes_accessed=1000, transcendentals=0)


def swap(array, axis, mask):
    size = lax.axis_size(axis)
    return lax.ppermute(array, axis, [(i, i ^ mask) for i in range(size)])


def params(mib):
    return pltpu.CompilerParams(vmem_limit_bytes=mib * 1024 * 1024)


def vmem_specs(count):
    return [pl.BlockSpec(memory_space=VMEM) for _ in range(count)]


def attention_kernel(index, q_hbm, *refs):
    arrived, w_hbm, outs = refs[:8], refs[8], refs[9:13]
    w_all, q, pieces, keys, ones_values, bias, even, odd, attn, q_sem, piece_sems, sems = refs[13:]
    q_fetch = pltpu.make_async_copy(q_hbm, q, q_sem)
    piece_fetches = [
        pltpu.make_async_copy(arrived[i], pieces.at[i], piece_sems.at[i]) for i in range(8)
    ]
    for fetch in piece_fetches + [q_fetch]:
        fetch.start()
    ctx = index[0]
    exp = index[1]
    chip = ctx // 2
    steps = sems.shape[0]
    depth = w_all.shape[0] // steps
    fetches = [
        pltpu.make_async_copy(
            w_hbm.at[pl.ds(i * depth, depth)], w_all.at[pl.ds(i * depth, depth)], sems.at[i]
        )
        for i in range(steps)
    ]
    for fetch in fetches:
        fetch.start()
    factor = math.log2(math.e) / math.sqrt(HD)
    heads = q.shape[1] // HD
    ones_values[:, HD:] = jnp.ones((ones_values.shape[0], HD), BF16)
    core = ctx % 2
    row = lax.broadcasted_iota(jnp.int32, (QB, 2 * QB), 0) + core * QB
    col = lax.broadcasted_iota(jnp.int32, (QB, 2 * QB), 1)
    bias[...] = jnp.where(col <= row, 0.0, -1e30)
    for fetch in piece_fetches:
        fetch.wait()
    for d in range(4):

        @pl.when(chip >= d)
        def _():
            for other in range(2):
                piece = pieces.at[2 * d + other]
                place = 2 * (chip - d) + (core ^ other)
                here = pl.ds(pl.multiple_of(place * QB, QB), QB)
                keys[:, here] = piece[:, :HD].astype(F32).T.astype(BF16)
                ones_values[here, :HD] = piece[:, HD:]

    q_fetch.wait()
    part = QB // 4

    def run(length):
        def scores_of(h, store):
            rows = q[:, pl.ds(pl.multiple_of(h * HD, HD), HD)]
            block = jnp.dot(rows, keys[:, :length], preferred_element_type=F32)
            last = length - 2 * QB
            if last:
                store[:, :last] = block[:, :last]
            store[:, last:length] = block[:, last:] + bias[...]

        def finish(h, store):
            block = store[:, :length]
            top = jnp.max(block, axis=1, keepdims=True) * factor
            probs = jnp.exp2(block * factor - top).astype(BF16)
            total = jnp.dot(probs, ones_values[:length, :], preferred_element_type=F32)
            done = (total[:, :HD] / total[:, HD:]).astype(BF16)
            cols = pl.ds(pl.multiple_of(h * HD, HD), HD)
            for i in range(4):
                start = pl.multiple_of((exp ^ i) * part, part)
                attn[pl.ds(start, part), cols] = done[i * part : (i + 1) * part]

        scores_of(0, even)

        @pl.loop(0, heads // 2)
        def _(pair):
            scores_of(2 * pair + 1, odd)
            finish(2 * pair, even)
            scores_of(jnp.minimum(2 * pair + 2, heads - 1), even)
            finish(2 * pair + 1, odd)

    for z in range(4):
        pl.when(chip == z)(functools.partial(run, (z + 1) * 2 * QB))

    for fetch in fetches:
        fetch.wait()
    width = 512
    for n in range(w_all.shape[1] // width):
        cols = slice(n * width, (n + 1) * width)
        block = jnp.dot(attn[...], w_all[:, cols], preferred_element_type=F32).astype(BF16)
        for b, out in enumerate(outs):
            out[:, cols] = block[b * part : (b + 1) * part]


def attention(index, queries, pieces, w_out):
    rows = QB // 4
    length = 8 * QB
    return pl.pallas_call(
        attention_kernel,
        out_shape=[jax.ShapeDtypeStruct((rows, D), BF16)] * 4,
        in_specs=[pl.BlockSpec(memory_space=pltpu.SMEM)]
        + [pl.BlockSpec(memory_space=pl.ANY)] * 10,
        out_specs=vmem_specs(4),
        scratch_shapes=[
            VMEM(w_out.shape, BF16),
            VMEM(queries.shape, BF16),
            VMEM((8,) + pieces[0].shape, BF16),
            VMEM((HD, length), BF16),
            VMEM((length, 2 * HD), BF16),
            VMEM((QB, 2 * QB), F32),
            VMEM((QB, length), F32),
            VMEM((QB, length), F32),
            VMEM(queries.shape, BF16),
            pltpu.SemaphoreType.DMA,
            pltpu.SemaphoreType.DMA((8,)),
            pltpu.SemaphoreType.DMA((16,)),
        ],
        compiler_params=params(52),
        cost_estimate=CHEAP,
        name="attention",
    )(index, queries, *pieces, w_out)


def norm_kernel(index, p0, r1, r2, r3, residual, gain, state, mine, theirs, work):
    ctx = index[0]
    total = p0[...].astype(F32) + r1[...].astype(F32) + r2[...].astype(F32) + r3[...].astype(F32)
    hidden = (residual[...].astype(F32) + total).astype(BF16)
    state[...] = hidden
    wide = hidden.astype(F32)
    inv = 1.0 / jnp.sqrt(jnp.mean(wide * wide, axis=1, keepdims=True) + 1e-06)
    normed = (wide * inv * gain[...].astype(F32)).astype(BF16)
    part = D // 8
    for j in range(8):
        work[j] = normed[:, j * part : (j + 1) * part]
    for j, (a, b) in enumerate(((0, 2), (1, 3), (6, 4), (7, 5))):
        mine[:, j * part : (j + 1) * part] = work[ctx ^ a]
        theirs[:, j * part : (j + 1) * part] = work[ctx ^ b]


def norm(index, p0, r1, r2, r3, residual, gain):
    rows = residual.shape[0]
    half = jax.ShapeDtypeStruct((rows, D // 2), BF16)
    return pl.pallas_call(
        norm_kernel,
        out_shape=[jax.ShapeDtypeStruct((rows, D), BF16), half, half],
        in_specs=[pl.BlockSpec(memory_space=pltpu.SMEM)] + vmem_specs(6),
        out_specs=vmem_specs(3),
        scratch_shapes=[VMEM((8, rows, D // 8), BF16)],
        compiler_params=params(16),
        cost_estimate=CHEAP,
        name="norm",
    )(index, p0, r1, r2, r3, residual, gain)


def enter_kernel(x0, x1, x2, x3, *refs):
    weights, out, gate_all, up_all, sems = refs[:4], refs[4], refs[5], refs[6], refs[7]
    part, width = weights[0].shape[0] // 2, weights[0].shape[1]
    fetches = []
    for which, whole in enumerate((gate_all, up_all)):
        for j, array in enumerate(weights):
            source = array.at[pl.ds(which * part, part)]
            target = whole.at[pl.ds(j * part, part)]
            fetches.append(pltpu.make_async_copy(source, target, sems.at[4 * which + j]))
            fetches[-1].start()
    x = jnp.concatenate([x0[...], x1[...], x2[...], x3[...]], axis=0)
    tile = 256
    for which, whole in enumerate((gate_all, up_all)):
        for fetch in fetches[4 * which : 4 * which + 4]:
            fetch.wait()
        for n in range(width // tile):
            cols = slice(which * width + n * tile, which * width + (n + 1) * tile)
            block = jnp.dot(x, whole[:, n * tile : (n + 1) * tile], preferred_element_type=F32)
            out[:, cols] = block.astype(out.dtype)


def enter(rows, weights, kind):
    count = 4 * rows[0].shape[0]
    part, width = weights[0].shape[0] // 2, weights[0].shape[1]
    return pl.pallas_call(
        enter_kernel,
        out_shape=jax.ShapeDtypeStruct((count, 2 * width), kind),
        in_specs=vmem_specs(4) + [pl.BlockSpec(memory_space=pl.ANY)] * 4,
        out_specs=pl.BlockSpec(memory_space=VMEM),
        scratch_shapes=[
            VMEM((4 * part, width), BF16),
            VMEM((4 * part, width), BF16),
            pltpu.SemaphoreType.DMA((8,)),
        ],
        compiler_params=params(24),
        cost_estimate=CHEAP,
        name="enter",
    )(*rows, *weights)


def silu_kernel(own, other, out):
    width = out.shape[1]
    total = own[...] + other[...].astype(F32)
    gate, up = total[:, :width], total[:, width:]
    out[...] = (gate / (1.0 + jnp.exp(-gate)) * up).astype(BF16)


def silu(own, other):
    return pl.pallas_call(
        silu_kernel,
        out_shape=jax.ShapeDtypeStruct((own.shape[0], own.shape[1] // 2), BF16),
        in_specs=vmem_specs(2),
        out_specs=pl.BlockSpec(memory_space=VMEM),
        compiler_params=params(16),
        cost_estimate=CHEAP,
        name="silu",
    )(own, other)


def leave_kernel(hidden, d0, d1, d2, d3, y0, y1, y2, y3, down_all, sems):
    part = y0.shape[0]
    width = d0.shape[1]
    fetches = []
    for j, array in enumerate((d0, d1, d2, d3)):
        fetches.append(pltpu.make_async_copy(array, down_all.at[j], sems.at[j]))
        fetches[-1].start()
    for j in range(4):
        fetches[j].wait()
        block = jnp.dot(hidden[...], down_all[j], preferred_element_type=F32).astype(BF16)
        for b, out in enumerate((y0, y1, y2, y3)):
            out[:, j * width : (j + 1) * width] = block[b * part : (b + 1) * part]


def leave(hidden, downs):
    part = jax.ShapeDtypeStruct((hidden.shape[0] // 4, 4 * downs[0].shape[1]), BF16)
    return pl.pallas_call(
        leave_kernel,
        out_shape=[part] * 4,
        in_specs=vmem_specs(1) + [pl.BlockSpec(memory_space=pl.ANY)] * 4,
        out_specs=vmem_specs(4),
        scratch_shapes=[VMEM((4,) + downs[0].shape, BF16), pltpu.SemaphoreType.DMA((4,))],
        compiler_params=params(16),
        cost_estimate=CHEAP,
        name="leave",
    )(hidden, *downs)


def mixed(shares, parts):
    total = shares[:, :1] * parts[0][...].astype(F32)
    for b in range(1, 4):
        total = total + shares[:, b : b + 1] * parts[b][...].astype(F32)
    return total


def final_kernel(index, state, shares, y0, r1, r2, r3, other, out):
    ctx = index[0]
    part = D // 8
    own = mixed(shares, (y0, r1, r2, r3))
    for j, (a, b) in enumerate(((0, 2), (1, 3), (6, 4), (7, 5))):
        cols = slice(j * part, (j + 1) * part)
        here = pl.ds(pl.multiple_of((ctx ^ a) * part, part), part)
        out[:, here] = (state[:, here].astype(F32) + own[:, cols]).astype(BF16)
        there = pl.ds(pl.multiple_of((ctx ^ b) * part, part), part)
        out[:, there] = (state[:, there].astype(F32) + other[:, cols].astype(F32)).astype(BF16)


def final(index, state, shares, y0, r1, r2, r3, other):
    return pl.pallas_call(
        final_kernel,
        out_shape=jax.ShapeDtypeStruct(state.shape, BF16),
        in_specs=[pl.BlockSpec(memory_space=pltpu.SMEM)] + vmem_specs(7),
        out_specs=pl.BlockSpec(memory_space=VMEM),
        compiler_params=params(16),
        cost_estimate=CHEAP,
        name="final",
    )(index, state, shares, y0, r1, r2, r3, other)


def body(
    queries,
    keys,
    values,
    w_out,
    residual,
    norm_gain,
    expert_ids,
    gate_weights,
    w_gate,
    w_up,
    w_down,
):
    exp = lax.axis_index("exp")
    ctx = lax.axis_index("ctx")
    index = jnp.stack([ctx, exp]).astype(jnp.int32)
    kv_first = exp * (HQ // 4) // (HQ // KVH) * HD
    kv_here = jnp.concatenate(
        [
            lax.dynamic_slice_in_dim(keys, kv_first, HD, 1),
            lax.dynamic_slice_in_dim(values, kv_first, HD, 1),
        ],
        axis=1,
    )
    def later(array, chips):
        return lax.ppermute(array, "ctx", [(i, i + 2 * chips) for i in range(8 - 2 * chips)])

    kv_here, gate_here, up_here = lax.optimization_barrier((kv_here, w_gate[0], w_up[0]))
    moved = [later(kv_here, d) for d in (3, 2, 1)][::-1]
    pair_here, down_here = jnp.concatenate([gate_here, up_here], axis=0), w_down[0]
    pieces = [part for piece in [kv_here] + moved for part in (piece, swap(piece, "ctx", 1))]
    pieces, pair_here = lax.optimization_barrier((pieces, pair_here))
    pair_far = swap(pair_here, "ctx", 6)

    lane = lax.broadcasted_iota(jnp.int32, (expert_ids.shape[0], HD), 1)
    shares = jnp.zeros(lane.shape, F32)
    for k in range(expert_ids.shape[1]):
        named = expert_ids[:, k : k + 1] ^ exp
        shares = shares + jnp.where(lane == named, gate_weights[:, k : k + 1], 0.0)

    p = attention(index, queries, pieces, w_out)
    p, shares, pair_here, down_here = lax.optimization_barrier((p, shares, pair_here, down_here))
    r = [swap(p[b], "exp", b) for b in (1, 2, 3)]
    pair_near, down_near = swap(pair_here, "ctx", 1), swap(down_here, "ctx", 1)
    other_shares = swap(shares, "ctx", 2)
    state, mine, theirs = norm(index, p[0], *r, residual, norm_gain.reshape(1, D))
    others = swap(theirs, "ctx", 2)
    own_rows = [mine] + [swap(mine, "exp", b) for b in (1, 2, 3)]
    other_rows = [others] + [swap(others, "exp", b) for b in (1, 2, 3)]
    own_rows, others, pair_far, down_here = lax.optimization_barrier(
        (own_rows, others, pair_far, down_here)
    )
    down_far = swap(down_here, "ctx", 6)
    pairs = (pair_here, pair_near, pair_far, swap(pair_far, "ctx", 1))
    other_pre = enter(other_rows, pairs, BF16)
    from_other = swap(other_pre, "ctx", 2)
    own_pre = enter(own_rows, pairs, F32)
    own_pre, down_far = lax.optimization_barrier((own_pre, down_far))
    own_hidden = silu(own_pre, from_other)
    other_hidden = swap(own_hidden, "ctx", 2)
    downs = (down_here, down_near, down_far, swap(down_far, "ctx", 1))
    y = leave(own_hidden, downs)
    own_parts = [y[0]] + [swap(y[b], "exp", b) for b in (1, 2, 3)]
    other_hidden, *own_parts[1:3] = lax.optimization_barrier((other_hidden, *own_parts[1:3]))
    z = leave(other_hidden, downs)
    other_parts = [z[0]] + [swap(z[b], "exp", b) for b in (1, 2, 3)]
    back = swap(mixed(other_shares, other_parts).astype(BF16), "ctx", 2)
    return final(index, state, shares, *own_parts, back)


def solution(mesh):
    placed = (
        P("ctx", "exp"),
        P("ctx", None),
        P("ctx", None),
        P("exp", None),
        P(("ctx", "exp"), None),
        P(),
        P(("ctx", "exp"), None),
        P(("ctx", "exp"), None),
        P("exp", "ctx", None),
        P("exp", "ctx", None),
        P("exp", None, "ctx"),
    )
    shape = dict(mesh.shape)
    small = shape["ctx"] == 8 and shape["exp"] == 4
    return jax.shard_map(
        body if small else general_body, mesh=mesh, in_specs=placed, out_specs=P(("ctx", "exp"), None), check_vma=False
    )
```

```python
import functools
import math

import jax
import jax.numpy as jnp
from jax import lax
from jax.experimental import pallas as pl
from jax.experimental.pallas import tpu as pltpu
from jax.sharding import PartitionSpec as P

D = 4096
HQ = 64
KVH = 4
HD = 128


def general_body(
    queries,
    keys,
    values,
    w_out,
    residual,
    norm_gain,
    expert_ids,
    gate_weights,
    w_gate,
    w_up,
    w_down,
):
    tok_rows = queries.shape[0]
    half_rows = tok_rows // 2
    exp_count = lax.axis_size("exp")
    heads_here = HQ // exp_count
    group = HQ // KVH
    kv_here = max(1, heads_here // group)
    heads_per_kv = heads_here // kv_here
    exp_index = lax.axis_index("exp")
    ctx_index = lax.axis_index("ctx")
    kv_first = exp_index * heads_here // group
    key_cols = lax.dynamic_slice_in_dim(keys, kv_first * HD, kv_here * HD, 1)
    value_cols = lax.dynamic_slice_in_dim(values, kv_first * HD, kv_here * HD, 1)
    scale = 1.0 / math.sqrt(HD)
    first_rows = queries[:half_rows]
    second_rows = queries[half_rows:]
    first_start = ctx_index * tok_rows
    second_start = ctx_index * tok_rows + half_rows
    query_sets = (
        first_rows.reshape(half_rows, kv_here, heads_per_kv, HD),
        second_rows.reshape(half_rows, kv_here, heads_per_kv, HD),
    )
    query_positions = (
        first_start + jnp.arange(half_rows, dtype=jnp.int32),
        second_start + jnp.arange(half_rows, dtype=jnp.int32),
    )
    last_positions = (first_start + half_rows - 1, second_start + half_rows - 1)

    def block_update(carry, query_four, query_pos, key_block, value_block, key_start):
        run_max, run_sum, run_acc = carry
        width = key_block.shape[0]
        key_three = key_block.reshape(width, kv_here, HD)
        value_three = value_block.reshape(width, kv_here, HD)
        scores = (
            jnp.einsum("tghd,kgd->ghtk", query_four, key_three, preferred_element_type=jnp.float32)
            * scale
        )
        key_pos = key_start + jnp.arange(width, dtype=jnp.int32)
        allowed = key_pos[None, :] <= query_pos[:, None]
        scores = jnp.where(allowed, scores, -1e30)
        new_max = jnp.maximum(run_max, jnp.max(scores, axis=-1))
        probs = jnp.where(allowed, jnp.exp(scores - new_max[..., None]), 0.0)
        factor = jnp.exp(run_max - new_max)
        run_sum = run_sum * factor + jnp.sum(probs, axis=-1)
        weighted = jnp.einsum(
            "ghtk,kgd->ghtd",
            probs.astype(jnp.bfloat16),
            value_three,
            preferred_element_type=jnp.float32,
        )
        run_acc = run_acc * factor[..., None] + weighted
        return (new_max, run_sum, run_acc)

    start_max = jnp.full((kv_here, heads_per_kv, half_rows), -1e30, jnp.float32)
    start_sum = jnp.zeros((kv_here, heads_per_kv, half_rows), jnp.float32)
    start_acc = jnp.zeros((kv_here, heads_per_kv, half_rows, HD), jnp.float32)
    start_state = (start_max, start_sum, start_acc)
    key_piece = lax.all_gather(key_cols, "ctx", axis=0, tiled=True)
    value_piece = lax.all_gather(value_cols, "ctx", axis=0, tiled=True)
    count = key_piece.shape[0]
    width = 512

    def one_block(index, inner):
        key_start = index * width
        key_block = lax.dynamic_slice_in_dim(key_piece, key_start, width, 0)
        value_block = lax.dynamic_slice_in_dim(value_piece, key_start, width, 0)
        updated = []
        for which in range(2):
            query_four = query_sets[which]
            query_pos = query_positions[which]
            updated.append(
                lax.cond(
                    key_start > last_positions[which],
                    lambda state: state,
                    lambda state: block_update(
                        state, query_four, query_pos, key_block, value_block, key_start
                    ),
                    inner[which],
                )
            )
        return (updated[0], updated[1])

    states = lax.fori_loop(0, count // width, one_block, (start_state, start_state))
    halves = []
    for which in range(2):
        run_max, run_sum, run_acc = states[which]
        halves.append(
            jnp.transpose(run_acc / run_sum[..., None], (2, 0, 1, 3))
            .reshape(half_rows, heads_here * HD)
            .astype(jnp.bfloat16)
        )
    attn_second = halves[1]
    attn = jnp.concatenate([halves[0], attn_second], axis=0)
    projected = lax.psum_scatter(
        jnp.dot(attn, w_out, preferred_element_type=jnp.float32).astype(jnp.bfloat16),
        "exp",
        scatter_dimension=0,
        tiled=True,
    ).astype(jnp.float32)
    hidden_state = (residual.astype(jnp.float32) + projected).astype(jnp.bfloat16)
    state_f = hidden_state.astype(jnp.float32)
    inv_rms = 1.0 / jnp.sqrt(jnp.mean(state_f * state_f, axis=1, keepdims=True) + 1e-06)
    normed = (state_f * inv_rms * norm_gain.astype(jnp.float32)[None, :]).astype(jnp.bfloat16)
    rows_here = expert_ids.shape[0]
    top_count = expert_ids.shape[1]
    experts_all = w_gate.shape[0] * exp_count
    capacity = min(rows_here, 2 * rows_here * top_count // experts_all)
    flat_ids = expert_ids.reshape(-1)
    onehot = (flat_ids[:, None] == jnp.arange(experts_all, dtype=jnp.int32)[None, :]).astype(
        jnp.int32
    )
    earlier = jnp.cumsum(onehot, axis=0) - onehot
    slot_index = jnp.sum(earlier * onehot, axis=1)
    target = flat_ids * capacity + slot_index
    picks = target[:, None] == jnp.arange(experts_all * capacity, dtype=jnp.int32)[None, :]
    dispatch_table = jnp.any(
        picks.reshape(rows_here, top_count, experts_all * capacity), axis=1
    ).astype(jnp.bfloat16)
    outgoing = jnp.einsum(
        "rs,rd->sd", dispatch_table, normed, preferred_element_type=jnp.float32
    ).astype(jnp.bfloat16)
    arrived = lax.all_to_all(
        outgoing.reshape(experts_all, capacity, D), "exp", split_axis=0, concat_axis=0, tiled=True
    )
    slot_rows = arrived.reshape(experts_all * capacity, D)
    gate_local = w_gate[0]
    up_local = w_up[0]
    gate_pre = jnp.dot(
        slot_rows,
        lax.all_gather(gate_local, "ctx", axis=0, tiled=True),
        preferred_element_type=jnp.float32,
    )
    up_pre = jnp.dot(
        slot_rows,
        lax.all_gather(up_local, "ctx", axis=0, tiled=True),
        preferred_element_type=jnp.float32,
    )
    expert_hidden = (jax.nn.silu(gate_pre) * up_pre).astype(jnp.bfloat16)
    down_local = w_down[0]
    expert_result = jnp.dot(
        expert_hidden,
        lax.all_gather(down_local, "ctx", axis=1, tiled=True),
        preferred_element_type=jnp.float32,
    ).astype(jnp.bfloat16)
    returned = lax.all_to_all(
        expert_result.reshape(experts_all, capacity, D),
        "exp",
        split_axis=0,
        concat_axis=0,
        tiled=True,
    )
    returned_flat = returned.reshape(experts_all * capacity, D)
    picked = jnp.dot(picks.astype(jnp.bfloat16), returned_flat, preferred_element_type=jnp.float32)
    weighted = gate_weights[:, :, None] * picked.reshape(rows_here, top_count, D)
    return (state_f + jnp.sum(weighted, axis=1)).astype(jnp.bfloat16)


BF16 = jnp.bfloat16
F32 = jnp.float32
VMEM = pltpu.VMEM
QB = 256
CHEAP = pl.CostEstimate(flops=1000, bytes_accessed=1000, transcendentals=0)


def swap(array, axis, mask):
    size = lax.axis_size(axis)
    return lax.ppermute(array, axis, [(i, i ^ mask) for i in range(size)])


def params(mib):
    return pltpu.CompilerParams(vmem_limit_bytes=mib * 1024 * 1024)


def vmem_specs(count):
    return [pl.BlockSpec(memory_space=VMEM) for _ in range(count)]


def attention_kernel(index, q_hbm, *refs):
    arrived, w_hbm, outs = refs[:8], refs[8], refs[9:13]
    w_all, q, pieces, keys, ones_values, bias, even, odd, attn, q_sem, piece_sems, sems = refs[13:]
    q_fetch = pltpu.make_async_copy(q_hbm, q, q_sem)
    piece_fetches = [
        pltpu.make_async_copy(arrived[i], pieces.at[i], piece_sems.at[i]) for i in range(8)
    ]
    for fetch in piece_fetches + [q_fetch]:
        fetch.start()
    ctx = index[0]
    exp = index[1]
    chip = ctx // 2
    steps = sems.shape[0]
    depth = w_all.shape[0] // steps
    fetches = [
        pltpu.make_async_copy(
            w_hbm.at[pl.ds(i * depth, depth)], w_all.at[pl.ds(i * depth, depth)], sems.at[i]
        )
        for i in range(steps)
    ]
    for fetch in fetches:
        fetch.start()
    factor = math.log2(math.e) / math.sqrt(HD)
    heads = q.shape[1] // HD
    ones_values[:, HD:] = jnp.ones((ones_values.shape[0], HD), BF16)
    core = ctx % 2
    row = lax.broadcasted_iota(jnp.int32, (QB, 2 * QB), 0) + core * QB
    col = lax.broadcasted_iota(jnp.int32, (QB, 2 * QB), 1)
    bias[...] = jnp.where(col <= row, 0.0, -1e30)
    for fetch in piece_fetches:
        fetch.wait()
    for d in range(4):

        @pl.when(chip >= d)
        def _():
            for other in range(2):
                piece = pieces.at[2 * d + other]
                place = 2 * (chip - d) + (core ^ other)
                here = pl.ds(pl.multiple_of(place * QB, QB), QB)
                keys[:, here] = piece[:, :HD].astype(F32).T.astype(BF16)
                ones_values[here, :HD] = piece[:, HD:]

    q_fetch.wait()
    part = QB // 4

    def run(length):
        def scores_of(h, store):
            rows = q[:, pl.ds(pl.multiple_of(h * HD, HD), HD)]
            block = jnp.dot(rows, keys[:, :length], preferred_element_type=F32)
            last = length - 2 * QB
            if last:
                store[:, :last] = block[:, :last]
            store[:, last:length] = block[:, last:] + bias[...]

        def finish(h, store):
            block = store[:, :length]
            top = jnp.max(block, axis=1, keepdims=True) * factor
            probs = jnp.exp2(block * factor - top).astype(BF16)
            total = jnp.dot(probs, ones_values[:length, :], preferred_element_type=F32)
            done = (total[:, :HD] / total[:, HD:]).astype(BF16)
            cols = pl.ds(pl.multiple_of(h * HD, HD), HD)
            for i in range(4):
                start = pl.multiple_of((exp ^ i) * part, part)
                attn[pl.ds(start, part), cols] = done[i * part : (i + 1) * part]

        scores_of(0, even)

        @pl.loop(0, heads // 2)
        def _(pair):
            scores_of(2 * pair + 1, odd)
            finish(2 * pair, even)
            scores_of(jnp.minimum(2 * pair + 2, heads - 1), even)
            finish(2 * pair + 1, odd)

    for z in range(4):
        pl.when(chip == z)(functools.partial(run, (z + 1) * 2 * QB))

    for fetch in fetches:
        fetch.wait()
    width = 512
    for n in range(w_all.shape[1] // width):
        cols = slice(n * width, (n + 1) * width)
        block = jnp.dot(attn[...], w_all[:, cols], preferred_element_type=F32).astype(BF16)
        for b, out in enumerate(outs):
            out[:, cols] = block[b * part : (b + 1) * part]


def attention(index, queries, pieces, w_out):
    rows = QB // 4
    length = 8 * QB
    return pl.pallas_call(
        attention_kernel,
        out_shape=[jax.ShapeDtypeStruct((rows, D), BF16)] * 4,
        in_specs=[pl.BlockSpec(memory_space=pltpu.SMEM)]
        + [pl.BlockSpec(memory_space=pl.ANY)] * 10,
        out_specs=vmem_specs(4),
        scratch_shapes=[
            VMEM(w_out.shape, BF16),
            VMEM(queries.shape, BF16),
            VMEM((8,) + pieces[0].shape, BF16),
            VMEM((HD, length), BF16),
            VMEM((length, 2 * HD), BF16),
            VMEM((QB, 2 * QB), F32),
            VMEM((QB, length), F32),
            VMEM((QB, length), F32),
            VMEM(queries.shape, BF16),
            pltpu.SemaphoreType.DMA,
            pltpu.SemaphoreType.DMA((8,)),
            pltpu.SemaphoreType.DMA((16,)),
        ],
        compiler_params=params(52),
        cost_estimate=CHEAP,
        name="attention",
    )(index, queries, *pieces, w_out)


def norm_kernel(index, p0, r1, r2, r3, residual, gain, state, mine, theirs, work):
    ctx = index[0]
    total = p0[...].astype(F32) + r1[...].astype(F32) + r2[...].astype(F32) + r3[...].astype(F32)
    hidden = (residual[...].astype(F32) + total).astype(BF16)
    state[...] = hidden
    wide = hidden.astype(F32)
    inv = 1.0 / jnp.sqrt(jnp.mean(wide * wide, axis=1, keepdims=True) + 1e-06)
    normed = (wide * inv * gain[...].astype(F32)).astype(BF16)
    part = D // 8
    for j in range(8):
        work[j] = normed[:, j * part : (j + 1) * part]
    for j, (a, b) in enumerate(((0, 2), (1, 3), (6, 4), (7, 5))):
        mine[:, j * part : (j + 1) * part] = work[ctx ^ a]
        theirs[:, j * part : (j + 1) * part] = work[ctx ^ b]


def norm(index, p0, r1, r2, r3, residual, gain):
    rows = residual.shape[0]
    half = jax.ShapeDtypeStruct((rows, D // 2), BF16)
    return pl.pallas_call(
        norm_kernel,
        out_shape=[jax.ShapeDtypeStruct((rows, D), BF16), half, half],
        in_specs=[pl.BlockSpec(memory_space=pltpu.SMEM)] + vmem_specs(6),
        out_specs=vmem_specs(3),
        scratch_shapes=[VMEM((8, rows, D // 8), BF16)],
        compiler_params=params(16),
        cost_estimate=CHEAP,
        name="norm",
    )(index, p0, r1, r2, r3, residual, gain)


def enter_kernel(x0, x1, x2, x3, *refs):
    weights, out, gate_all, up_all, sems = refs[:4], refs[4], refs[5], refs[6], refs[7]
    part, width = weights[0].shape[0] // 2, weights[0].shape[1]
    fetches = []
    for which, whole in enumerate((gate_all, up_all)):
        for j, array in enumerate(weights):
            source = array.at[pl.ds(which * part, part)]
            target = whole.at[pl.ds(j * part, part)]
            fetches.append(pltpu.make_async_copy(source, target, sems.at[4 * which + j]))
            fetches[-1].start()
    x = jnp.concatenate([x0[...], x1[...], x2[...], x3[...]], axis=0)
    tile = 256
    for which, whole in enumerate((gate_all, up_all)):
        for fetch in fetches[4 * which : 4 * which + 4]:
            fetch.wait()
        for n in range(width // tile):
            cols = slice(which * width + n * tile, which * width + (n + 1) * tile)
            block = jnp.dot(x, whole[:, n * tile : (n + 1) * tile], preferred_element_type=F32)
            out[:, cols] = block.astype(out.dtype)


def enter(rows, weights, kind):
    count = 4 * rows[0].shape[0]
    part, width = weights[0].shape[0] // 2, weights[0].shape[1]
    return pl.pallas_call(
        enter_kernel,
        out_shape=jax.ShapeDtypeStruct((count, 2 * width), kind),
        in_specs=vmem_specs(4) + [pl.BlockSpec(memory_space=pl.ANY)] * 4,
        out_specs=pl.BlockSpec(memory_space=VMEM),
        scratch_shapes=[
            VMEM((4 * part, width), BF16),
            VMEM((4 * part, width), BF16),
            pltpu.SemaphoreType.DMA((8,)),
        ],
        compiler_params=params(24),
        cost_estimate=CHEAP,
        name="enter",
    )(*rows, *weights)


def silu_kernel(own, other, out):
    width = out.shape[1]
    total = own[...] + other[...].astype(F32)
    gate, up = total[:, :width], total[:, width:]
    out[...] = (gate / (1.0 + jnp.exp(-gate)) * up).astype(BF16)


def silu(own, other):
    return pl.pallas_call(
        silu_kernel,
        out_shape=jax.ShapeDtypeStruct((own.shape[0], own.shape[1] // 2), BF16),
        in_specs=vmem_specs(2),
        out_specs=pl.BlockSpec(memory_space=VMEM),
        compiler_params=params(16),
        cost_estimate=CHEAP,
        name="silu",
    )(own, other)


def leave_kernel(hidden, d0, d1, d2, d3, y0, y1, y2, y3, down_all, sems):
    part = y0.shape[0]
    width = d0.shape[1]
    fetches = []
    for j, array in enumerate((d0, d1, d2, d3)):
        fetches.append(pltpu.make_async_copy(array, down_all.at[j], sems.at[j]))
        fetches[-1].start()
    for j in range(4):
        fetches[j].wait()
        block = jnp.dot(hidden[...], down_all[j], preferred_element_type=F32).astype(BF16)
        for b, out in enumerate((y0, y1, y2, y3)):
            out[:, j * width : (j + 1) * width] = block[b * part : (b + 1) * part]


def leave(hidden, downs):
    part = jax.ShapeDtypeStruct((hidden.shape[0] // 4, 4 * downs[0].shape[1]), BF16)
    return pl.pallas_call(
        leave_kernel,
        out_shape=[part] * 4,
        in_specs=vmem_specs(1) + [pl.BlockSpec(memory_space=pl.ANY)] * 4,
        out_specs=vmem_specs(4),
        scratch_shapes=[VMEM((4,) + downs[0].shape, BF16), pltpu.SemaphoreType.DMA((4,))],
        compiler_params=params(16),
        cost_estimate=CHEAP,
        name="leave",
    )(hidden, *downs)


def mixed(shares, parts):
    total = shares[:, :1] * parts[0][...].astype(F32)
    for b in range(1, 4):
        total = total + shares[:, b : b + 1] * parts[b][...].astype(F32)
    return total


def final_kernel(index, state, shares, y0, r1, r2, r3, other, out):
    ctx = index[0]
    part = D // 8
    own = mixed(shares, (y0, r1, r2, r3))
    for j, (a, b) in enumerate(((0, 2), (1, 3), (6, 4), (7, 5))):
        cols = slice(j * part, (j + 1) * part)
        here = pl.ds(pl.multiple_of((ctx ^ a) * part, part), part)
        out[:, here] = (state[:, here].astype(F32) + own[:, cols]).astype(BF16)
        there = pl.ds(pl.multiple_of((ctx ^ b) * part, part), part)
        out[:, there] = (state[:, there].astype(F32) + other[:, cols].astype(F32)).astype(BF16)


def final(index, state, shares, y0, r1, r2, r3, other):
    return pl.pallas_call(
        final_kernel,
        out_shape=jax.ShapeDtypeStruct(state.shape, BF16),
        in_specs=[pl.BlockSpec(memory_space=pltpu.SMEM)] + vmem_specs(7),
        out_specs=pl.BlockSpec(memory_space=VMEM),
        compiler_params=params(16),
        cost_estimate=CHEAP,
        name="final",
    )(index, state, shares, y0, r1, r2, r3, other)


def body(
    queries,
    keys,
    values,
    w_out,
    residual,
    norm_gain,
    expert_ids,
    gate_weights,
    w_gate,
    w_up,
    w_down,
):
    exp = lax.axis_index("exp")
    ctx = lax.axis_index("ctx")
    index = jnp.stack([ctx, exp]).astype(jnp.int32)
    kv_first = exp * (HQ // 4) // (HQ // KVH) * HD
    kv_here = jnp.concatenate(
        [
            lax.dynamic_slice_in_dim(keys, kv_first, HD, 1),
            lax.dynamic_slice_in_dim(values, kv_first, HD, 1),
        ],
        axis=1,
    )
    def later(array, chips):
        return lax.ppermute(array, "ctx", [(i, i + 2 * chips) for i in range(8 - 2 * chips)])

    kv_here, gate_here, up_here = lax.optimization_barrier((kv_here, w_gate[0], w_up[0]))
    moved = [later(kv_here, d) for d in (3, 2, 1)][::-1]
    pair_here, down_here = jnp.concatenate([gate_here, up_here], axis=0), w_down[0]
    pieces = [part for piece in [kv_here] + moved for part in (piece, swap(piece, "ctx", 1))]
    pieces, pair_here = lax.optimization_barrier((pieces, pair_here))
    pair_far = swap(pair_here, "ctx", 6)

    lane = lax.broadcasted_iota(jnp.int32, (expert_ids.shape[0], HD), 1)
    shares = jnp.zeros(lane.shape, F32)
    for k in range(expert_ids.shape[1]):
        named = expert_ids[:, k : k + 1] ^ exp
        shares = shares + jnp.where(lane == named, gate_weights[:, k : k + 1], 0.0)

    p = attention(index, queries, pieces, w_out)
    p, shares, pair_here, down_here = lax.optimization_barrier((p, shares, pair_here, down_here))
    r = [swap(p[b], "exp", b) for b in (1, 2, 3)]
    pair_near, down_near = swap(pair_here, "ctx", 1), swap(down_here, "ctx", 1)
    other_shares = swap(shares, "ctx", 2)
    state, mine, theirs = norm(index, p[0], *r, residual, norm_gain.reshape(1, D))
    others = swap(theirs, "ctx", 2)
    own_rows = [mine] + [swap(mine, "exp", b) for b in (1, 2, 3)]
    other_rows = [others] + [swap(others, "exp", b) for b in (1, 2, 3)]
    own_rows, others, pair_far, down_here = lax.optimization_barrier(
        (own_rows, others, pair_far, down_here)
    )
    down_far = swap(down_here, "ctx", 6)
    pairs = (pair_here, pair_near, pair_far, swap(pair_far, "ctx", 1))
    other_pre = enter(other_rows, pairs, BF16)
    from_other = swap(other_pre, "ctx", 2)
    own_pre = enter(own_rows, pairs, F32)
    own_pre, down_far, other_shares = lax.optimization_barrier((own_pre, down_far, other_shares))
    own_hidden = silu(own_pre, from_other)
    other_hidden = swap(own_hidden, "ctx", 2)
    downs = (down_here, down_near, down_far, swap(down_far, "ctx", 1))
    y = leave(own_hidden, downs)
    own_parts = [y[0]] + [swap(y[b], "exp", b) for b in (1, 2, 3)]
    other_hidden, *own_parts[1:3] = lax.optimization_barrier((other_hidden, *own_parts[1:3]))
    z = leave(other_hidden, downs)
    other_parts = [z[0]] + [swap(z[b], "exp", b) for b in (1, 2, 3)]
    back = swap(mixed(other_shares, other_parts).astype(BF16), "ctx", 2)
    return final(index, state, shares, *own_parts, back)


def solution(mesh):
    placed = (
        P("ctx", "exp"),
        P("ctx", None),
        P("ctx", None),
        P("exp", None),
        P(("ctx", "exp"), None),
        P(),
        P(("ctx", "exp"), None),
        P(("ctx", "exp"), None),
        P("exp", "ctx", None),
        P("exp", "ctx", None),
        P("exp", None, "ctx"),
    )
    shape = dict(mesh.shape)
    small = shape["ctx"] == 8 and shape["exp"] == 4
    return jax.shard_map(
        body if small else general_body, mesh=mesh, in_specs=placed, out_specs=P(("ctx", "exp"), None), check_vma=False
    )
```
